32 devices in a mesh: seq: 8 (over z, y), wt: 4 (over x, core).
Axes of the slice: x: 2, y: 2, z: 4, core: 2. Of those that a mesh axis runs over, the one named last changes fastest.
Arguments:
- tokens: bfloat16 [4, 4096, 1536], P('wt', 'seq'), may hold values from -6 to 6
- norm_gain: float32 [1536], replicated, may hold values from 0.5 to 1.5
- in_weight: bfloat16 [1536, 6448], P('wt'), may hold values from -0.15625 to 0.15625
- conv_kernel: float32 [4, 3328], replicated, may hold values from -2 to 2
- conv_bias: float32 [3328], replicated, may hold values from -1.5 to 1.5
- step_bias: float32 [48], replicated, may hold values from -10 to -3
- decay_log: float32 [48], replicated, may hold values from 0 to 2.77
- skip_gain: float32 [48], replicated, may hold values from 0.5 to 1.5
- out_gain: float32 [3072], replicated, may hold values from 0.5 to 1.5
- out_weight: bfloat16 [3072, 1536], P('wt'), may hold values from -0.109375 to 0.109375
- cotangent: bfloat16 [4, 4096, 1536], P('wt', 'seq'), may hold values from -6 to 6
Outputs:
- mixed_out: bfloat16 [4, 4096, 1536], P('wt', 'seq')
- grad_tokens: float32 [4, 4096, 1536], P('wt', 'seq')
- grad_norm_gain: float32 [1536], replicated
- grad_in_weight: float32 [1536, 6448], P('wt')
- grad_conv_kernel: float32 [4, 3328], replicated
- grad_conv_bias: float32 [3328], replicated
- grad_step_bias: float32 [48], replicated
- grad_decay_log: float32 [48], replicated
- grad_skip_gain: float32 [48], replicated
- grad_out_gain: float32 [3072], replicated
- grad_out_weight: float32 [3072, 1536], P('wt')
The draws below stay inside these ranges and needn't reach their ends.
All inputs are finite; a program needn't handle non-finite values.
Results may differ from the reference program's by a relative error of at most 0.013.
Values may be sent and summed in bfloat16 or wider, within the bound.
A program may use at most 320 MiB of HBM per device.

```python
import jax
import jax.numpy as jnp
from jax import lax

D = 1536
DI = 3072
HEADS = 48
HDIM = 64
NSTATE = 128
CONV = 4
GROUP = 256
NSEQ = 4
LENGTH = 4096
CDIM = 3328
E = 6448


def levels(rng, dims, cuts, least, high):
    level, own = 1.0, jax.random.fold_in(rng, 6)
    for axis_at, parts in cuts:
        heights = jnp.exp(jax.random.uniform(jax.random.fold_in(own, axis_at), (parts,), jnp.float32, least / len(cuts), high / len(cuts)))
        level = level * jnp.repeat(heights, dims[axis_at] // parts).reshape([-1 if axis == axis_at else 1 for axis in range(len(dims))])
    return level


def gaussian(key, dims, scale, bound, shards=(), kind=jnp.bfloat16):
    array = jax.random.normal(key, dims, jnp.float32) * scale
    if len(shards) > 0:
        array = levels(key, dims, shards, -0.22, 0.18) * array
    return jnp.clip(array, min=-bound, max=bound).astype(kind)


def setup_inputs(seed: int = 0) -> dict:
    key_of = jax.random.split(jax.random.key(seed), 12)
    tokens = gaussian(key_of[0], (NSEQ, LENGTH, D), 1.0, 6.0, ((0, 4), (1, 8)))
    norm_gain = jnp.clip(1.0 + 0.1 * jax.random.normal(key_of[1], (D,), jnp.float32), 0.5, 1.5)
    in_weight = gaussian(key_of[2], (D, E), D ** -0.5, 0.15625, ((0, 4),))
    conv_kernel = gaussian(key_of[3], (CONV, CDIM), 0.5, 2.0, (), jnp.float32)
    conv_bias = gaussian(key_of[4], (CDIM,), 0.3, 1.5, (), jnp.float32)
    step_bias = jnp.clip(jax.random.uniform(key_of[5], (HEADS,), jnp.float32, -10.0, -3.0), -10.0, -3.0)
    decay_log = jnp.clip(jax.random.uniform(key_of[6], (HEADS,), jnp.float32, 0.0, 2.77), 0.0, 2.77)
    skip_gain = jnp.clip(jax.random.uniform(key_of[7], (HEADS,), jnp.float32, 0.5, 1.5), 0.5, 1.5)
    out_gain = jnp.clip(1.0 + 0.1 * jax.random.normal(key_of[8], (DI,), jnp.float32), 0.5, 1.5)
    out_weight = gaussian(key_of[9], (DI, D), DI ** -0.5, 0.109375, ((0, 4),))
    cotangent = gaussian(key_of[10], (NSEQ, LENGTH, D), 1.0, 6.0, ((0, 4), (1, 8)))
    return {"tokens": tokens, "norm_gain": norm_gain, "in_weight": in_weight, "conv_kernel": conv_kernel, "conv_bias": conv_bias, "step_bias": step_bias, "decay_log": decay_log, "skip_gain": skip_gain, "out_gain": out_gain, "out_weight": out_weight, "cotangent": cotangent}


EPS = 1e-05
HIGH = lax.Precision.HIGHEST

@jax.custom_vjp
def low(v):
    return lax.optimization_barrier(v.astype(jnp.bfloat16)).astype(jnp.float32)

@jax.custom_vjp
def low_back(v):
    return v

def low_keep(v):
    return (low(v), None)

def low_pass(kept, grad):
    return (grad,)

def back_keep(v):
    return (v, None)

def back_low(kept, grad):
    return (low(grad),)
low.defvjp(low_keep, low_pass)
low_back.defvjp(back_keep, back_low)

def block_step(state, piece):
    heads_in, input_mat, output_mat, step_size, log_decay = piece
    running = jnp.cumsum(log_decay, axis=0)
    spread = running[:, None, :] - running[None, :, :]
    row_ids = lax.broadcasted_iota(jnp.int32, spread.shape, 0)
    col_ids = lax.broadcasted_iota(jnp.int32, spread.shape, 1)
    decay = jnp.exp(jnp.where(row_ids >= col_ids, spread, -jnp.inf))
    scores = jnp.dot(output_mat, input_mat.T, precision=HIGH)
    mixing = scores[:, :, None] * decay * step_size[None, :, :]
    inside = jnp.einsum('tsh,shp->thp', mixing, heads_in, precision=HIGH)
    carried = jnp.exp(running)[:, :, None] * jnp.einsum('tn,hpn->thp', output_mat, state, precision=HIGH)
    weight_end = jnp.exp(running[-1][None, :] - running) * step_size
    new_state = jnp.exp(running[-1])[:, None, None] * state + jnp.einsum('shp,sn->hpn', weight_end[:, :, None] * heads_in, input_mat, precision=HIGH)
    return (new_state, inside + carried)

def scan_blocks(heads_in, input_mat, output_mat, step_size, log_decay):
    count = heads_in.shape[0] // GROUP
    pieces = tuple((v.reshape((count, GROUP) + v.shape[1:]) for v in (heads_in, input_mat, output_mat, step_size, log_decay)))
    start = jnp.zeros((HEADS, HDIM, NSTATE), jnp.float32)
    final, outputs = lax.scan(jax.checkpoint(block_step), start, pieces)
    return outputs.reshape(heads_in.shape)

def layer(inputs, norm_gain, in_weight, conv_kernel, conv_bias, step_bias, decay_log, skip_gain, out_gain, out_weight):
    length = inputs.shape[0]
    normed = inputs * lax.rsqrt(lax.optimization_barrier(jnp.mean(inputs * inputs, axis=-1, keepdims=True)) + EPS) * norm_gain
    proj = low_back(low(jnp.dot(low(normed), in_weight, precision=HIGH)))
    gate_in = proj[:, :DI]
    conv_in = proj[:, DI:DI + CDIM]
    step_raw = proj[:, DI + CDIM:]
    padded = jnp.pad(conv_in, ((CONV - 1, 0), (0, 0)))
    summed = conv_bias + sum((conv_kernel[k] * padded[k:k + length] for k in range(CONV)))
    conv_act = jax.nn.silu(summed)
    heads_in = conv_act[:, :DI].reshape(length, HEADS, HDIM)
    input_mat = conv_act[:, DI:DI + NSTATE]
    output_mat = conv_act[:, DI + NSTATE:]
    step_size = jax.nn.softplus(step_raw + step_bias)
    log_decay = -step_size * jnp.exp(decay_log)
    scanned = scan_blocks(heads_in, input_mat, output_mat, step_size, log_decay)
    scan_out = (scanned + skip_gain[:, None] * heads_in).reshape(length, DI)
    gated = scan_out * jax.nn.silu(gate_in)
    normed_out = gated * lax.rsqrt(lax.optimization_barrier(jnp.mean(gated * gated, axis=-1, keepdims=True)) + EPS) * out_gain
    return inputs + jnp.dot(low(normed_out), out_weight, precision=HIGH)

def reference(tokens, norm_gain, in_weight, conv_kernel, conv_bias, step_bias, decay_log, skip_gain, out_gain, out_weight, cotangent):
    params = (norm_gain.astype(jnp.float32), in_weight.astype(jnp.float32), conv_kernel.astype(jnp.float32), conv_bias.astype(jnp.float32), step_bias.astype(jnp.float32), decay_log.astype(jnp.float32), skip_gain.astype(jnp.float32), out_gain.astype(jnp.float32), out_weight.astype(jnp.float32))
    outputs = []
    input_grads = []
    totals = None
    for index in range(NSEQ):
        result, pull = jax.vjp(layer, tokens[index].astype(jnp.float32), *params)
        grads = pull(cotangent[index].astype(jnp.float32))
        outputs.append(result.astype(jnp.bfloat16))
        input_grads.append(grads[0])
        if totals is None:
            totals = grads[1:]
        else:
            totals = tuple((a + b for a, b in zip(totals, grads[1:])))
    return (jnp.stack(outputs), jnp.stack(input_grads), totals[0], totals[1], totals[2], totals[3], totals[4], totals[5], totals[6], totals[7], totals[8])
```

```python
import jax
import jax.numpy as jnp
import numpy as np
from jax import lax
from jax.experimental import pallas as pl
from jax.experimental.pallas import tpu as pltpu
from jax.sharding import PartitionSpec as P

DI = 3072
HEADS = 48
HDIM = 64
NSTATE = 128
CONV = 4
CDIM = 3328
EDGE = 16
BLOCK = 128
GROUP = 8
WIDE = GROUP * HDIM
STEPS = HEADS // GROUP
LONG = (STEPS + 1) * WIDE
LANES = 128
TILE = 512
FINE = 256
SHORT = 64
AHEAD = 4
LAG = 2
LAST = 320
PARTS = 4
DM = 1536
PART = DM // PARTS
OUT_PART = DI // PARTS
SLOTS = 16
FEW = 4
SLACK = 2
MESH = pl.DeviceIdType.MESH

EPS = 1e-05
F32 = jnp.float32
LOW = jnp.bfloat16


def dot(a, b, ca, cb):
    return lax.dot_general(a, b, (((ca,), (cb,)), ((), ())), preferred_element_type=F32)


def nn(a, b):
    return dot(a, b, 1, 0)


def nt(a, b):
    return dot(a, b, 1, 1)


def tn(a, b):
    return dot(a, b, 0, 0)


def exact(a, b):
    return jnp.dot(a, b, precision=lax.Precision.HIGHEST, preferred_element_type=F32)


def halves(v):
    high = v.astype(LOW)
    return jnp.concatenate([high, (v - high.astype(F32)).astype(LOW)], axis=1)


def softplus(v):
    z = jnp.exp(-jnp.abs(v))
    small = z * (1.0 - z * (0.5 - z * (1.0 / 3.0 - z * 0.25)))
    return jnp.maximum(v, 0.0) + jnp.where(z < 0.01, small, jnp.log(1.0 + z))


def rows_cols(shape):
    return (lax.broadcasted_iota(jnp.int32, shape, 0), lax.broadcasted_iota(jnp.int32, shape, 1))


class Begin:
    def __init__(self, proj_ref, taps_ref, heads_ref, e2_ref, x_ref, bc_ref, dt_ref, rb_ref, rt_ref, er_ref, ew_ref, d2_ref, ed_ref, state_ref, pad_ref, wd_ref):
        self.proj, self.taps, self.heads, self.e2 = proj_ref, taps_ref, heads_ref, e2_ref
        self.x, self.bc, self.dt, self.rb, self.rt = x_ref, bc_ref, dt_ref, rb_ref, rt_ref
        self.er, self.ew, self.d2, self.ed, self.state = er_ref, ew_ref, d2_ref, ed_ref, state_ref
        self.pad, self.wd = pad_ref, wd_ref
        self.length = x_ref.shape[0]

    def convolved(self, first, width):
        self.pad[:, :width] = self.proj[:, first : first + width].astype(F32)
        total = self.taps[CONV : CONV + 1, first : first + WIDE]
        for k in range(CONV):
            at = EDGE - CONV + 1 + k
            total = total + self.taps[k : k + 1, first : first + WIDE] * self.pad[at : at + self.length, :]
        return total * jax.nn.sigmoid(total)

    def sizes(self):
        length = self.length
        self.pad[...] = jnp.zeros_like(self.pad)
        act = self.convolved(DI, CDIM + HEADS - DI)
        self.bc[...] = act[:, : 2 * NSTATE].astype(LOW)
        raw = self.pad[EDGE:, 2 * NSTATE : 2 * NSTATE + LANES]
        used = lax.broadcasted_iota(jnp.int32, raw.shape, 1) < HEADS
        dt = jnp.where(used, softplus(jnp.where(used, raw + self.heads[0:1, :], 0.0)), 0.0)
        self.dt[...] = dt
        self.d2[...] = halves(dt)
        decay = -dt * jnp.exp(self.heads[1:2, :])
        ids, jds = rows_cols((BLOCK, BLOCK))
        lower = (ids >= jds).astype(F32)
        before = jnp.zeros((1, LANES), F32)
        whole = []
        for c in range(length // BLOCK):
            at = slice(c * BLOCK, (c + 1) * BLOCK)
            run = exact(lower, decay[at])
            last = run[BLOCK - 1 : BLOCK]
            for j in range(STEPS):
                turned = jnp.concatenate([run[:, GROUP * j :], run[:, : GROUP * j]], axis=1) if j else run
                self.rb[at, j * LANES : (j + 1) * LANES] = turned
            self.rt[:, at] = run.T
            self.er[at, :] = halves(jnp.exp(run))
            self.ew[at, :] = halves(jnp.exp(last - run))
            whole.append(run + before)
            self.ed[at, :] = halves(jnp.exp(run + before))
            before = before + last
        for c in range(length // BLOCK):
            at = slice(c * BLOCK, (c + 1) * BLOCK)
            self.wd[at, :] = halves(jnp.exp(before - whole[c]) * dt[at])

    def block(self, j):
        at = slice(j * WIDE, (j + 1) * WIDE)
        x = self.convolved(j * WIDE, WIDE).astype(LOW)
        self.x[:, at] = x
        e2 = self.e2[:, at]
        weighed = (x.astype(F32) * nn(self.wd[...], e2)).astype(LOW)
        self.state[0:NSTATE, at] = tn(self.bc[:, :NSTATE], weighed).astype(LOW)
        decay = nn(self.ed[self.length - 16 : self.length, :], e2)[15:16, :]
        high = decay.astype(LOW).astype(F32)
        ids = lax.broadcasted_iota(jnp.int32, (16, WIDE), 0)
        self.state[NSTATE : NSTATE + 16, at] = jnp.where(ids == 0, high, jnp.where(ids == 1, decay - high, 0.0)).astype(LOW)


class Stages:
    def __init__(self, ref, sem):
        self.ref, self.sem, self.count = ref, sem, ref.shape[0]
        self.flying = [None] * self.count
        self.turn = 0

    def put(self, value, target):
        at = self.turn % self.count
        if self.flying[at] is not None:
            self.flying[at].wait()
        self.ref[at] = value
        self.flying[at] = pltpu.make_async_copy(self.ref.at[at], target, self.sem.at[at])
        self.flying[at].start()
        self.turn += 1

    def rest(self):
        for one in self.flying:
            if one is not None:
                one.wait()


class Inside:
    def __init__(self, x_ref, bc_ref, rb_ref, rt_ref, er_ref, ew_ref, d2_ref, e2_ref, held_ref, y_out, states_out, ys, states):
        self.x, self.bc, self.rb, self.rt = x_ref, bc_ref, rb_ref, rt_ref
        self.er, self.ew, self.d2, self.e2, self.held = er_ref, ew_ref, d2_ref, e2_ref, held_ref
        self.y_out, self.states_out, self.ys, self.states = y_out, states_out, ys, states
        self.blocks = x_ref.shape[0] // BLOCK

    def turn(self, at):
        if at < STEPS * self.blocks:
            self.block(at // self.blocks, at % self.blocks)

    def block(self, j, c):
        at, own = slice(c * BLOCK, (c + 1) * BLOCK), slice(j * WIDE, (j + 1) * WIDE)
        ids, jds = rows_cols((BLOCK, BLOCK))
        left = lax.broadcasted_iota(jnp.int32, (BLOCK, LANES), 1) < HDIM
        input_mat, output_mat = self.bc[at, :NSTATE], self.bc[at, NSTATE:]
        e2 = self.e2[:, own]
        grow, leave = nn(self.er[at, :], e2), nn(self.ew[at, :], e2)
        x = self.x[at, own].astype(F32) * nn(self.d2[at, :], e2)
        scores = jnp.where(ids >= jds, nt(output_mat, input_mat), 0.0)
        held = self.held[...] if c else jnp.zeros_like(self.held)
        self.states.put(held.astype(LOW), self.states_out.at[c, :, own])
        carried = grow * nn(output_mat, held.astype(LOW))
        parts = []
        for pair in range(GROUP // 2):
            lanes = slice(pair * LANES, (pair + 1) * LANES)
            piece = x[:, lanes]
            mixed = []
            for head in (2 * pair, 2 * pair + 1):
                column = self.rb[at, j * LANES + head : j * LANES + head + 1]
                spread = column - self.rt[j * GROUP + head : j * GROUP + head + 1, at]
                mixed.append((scores * jnp.exp(jnp.minimum(spread, 0.0))).astype(LOW))
            both = jnp.concatenate([jnp.where(left, piece, 0.0), jnp.where(left, 0.0, piece)], axis=0)
            parts.append(nn(jnp.concatenate(mixed, axis=1), both.astype(LOW)) + carried[:, lanes])
        self.ys.put(jnp.concatenate(parts, axis=1), self.y_out.at[at, own])
        self.held[...] = held * grow[BLOCK - 1 : BLOCK, :] + tn(input_mat, (x * leave).astype(LOW))


def middle_kernel(y_ref, bc_ref, in_ref, ed_ref, e2_ref, x_ref, gate_ref, dno_ref, gains_ref, low_ref, dy_ref, dgate_ref, sums_ref, din_ref, out_ref, gated_ref):
    @pl.when(pl.program_id(0) == 0)
    def _():
        sums_ref[...] = jnp.zeros_like(sums_ref)
        din_ref[...] = jnp.zeros_like(din_ref)

    output_mat = bc_ref[:, NSTATE:]
    part = DI // PARTS
    tiles = []
    for j in range(PARTS):
        there = relative(j)
        tiles.append((slice(j * part, (j + 1) * part), pl.ds(pl.multiple_of(there * part, LANES), part)))
    square = jnp.zeros((BLOCK, 1), F32)
    cross = jnp.zeros((BLOCK, 1), F32)
    for at, there in tiles:
        far = nn(ed_ref[...], e2_ref[:, at]) * nn(output_mat, in_ref[:, at])
        out = y_ref[:, at] + far + gains_ref[1:2, at] * x_ref[:, at].astype(F32)
        gate = gate_ref[:, at].astype(F32)
        gated = out * gate * jax.nn.sigmoid(gate)
        out_ref[:, at] = out
        gated_ref[:, at] = gated
        square = square + jnp.sum(gated * gated, axis=1, keepdims=True)
        cross = cross + jnp.sum(gated * (dno_ref[:, there] * gains_ref[0:1, at]), axis=1, keepdims=True)
    scale = lax.rsqrt(square * (1.0 / DI) + EPS)
    pull = scale * scale * scale * (cross * (1.0 / DI))
    for at, there in tiles:
        gate = gate_ref[:, at].astype(F32)
        gated, out, gain = gated_ref[:, at], out_ref[:, at], gains_ref[0:1, at]
        shape = jax.nn.sigmoid(gate)
        unit = gated * scale
        low_ref[:, there] = (unit * gain).astype(LOW)
        dno = dno_ref[:, there]
        dgated = scale * (dno * gain) - gated * pull
        dy = dgated * (gate * shape)
        dy_ref[:, at] = dy.astype(LOW)
        dgate_ref[:, at] = (dgated * out * (shape * (1.0 + gate * (1.0 - shape)))).astype(LOW)
        sums_ref[0:1, at] += jnp.sum(dno * unit, axis=0, keepdims=True)
        sums_ref[1:2, at] += jnp.sum(dy * x_ref[:, at].astype(F32), axis=0, keepdims=True)
        din_ref[:, at] += tn(output_mat, (dy * nn(ed_ref[...], e2_ref[:, at])).astype(LOW))


def middle(y, bc, incoming, ed, e2, x, gate, dno, gains, length):
    rows = lambda c: (c, 0)
    fixed = lambda c: (0, 0)
    return pl.pallas_call(
        middle_kernel,
        grid=(length // BLOCK,),
        in_specs=[
            pl.BlockSpec((BLOCK, DI), rows),
            pl.BlockSpec((BLOCK, 2 * NSTATE), rows),
            pl.BlockSpec((NSTATE, DI), fixed),
            pl.BlockSpec((BLOCK, 2 * LANES), rows),
            pl.BlockSpec((2 * LANES, DI), fixed),
            pl.BlockSpec((BLOCK, DI), rows),
            pl.BlockSpec((BLOCK, DI), rows),
            pl.BlockSpec((BLOCK, DI), rows),
            pl.BlockSpec((8, DI), fixed),
        ],
        out_specs=[
            pl.BlockSpec((BLOCK, DI), rows),
            pl.BlockSpec((BLOCK, DI), rows),
            pl.BlockSpec((BLOCK, DI), rows),
            pl.BlockSpec((8, DI), fixed),
            pl.BlockSpec((NSTATE, DI), fixed),
        ],
        out_shape=[
            jax.ShapeDtypeStruct((length, DI), LOW),
            jax.ShapeDtypeStruct((length, DI), LOW),
            jax.ShapeDtypeStruct((length, DI), LOW),
            jax.ShapeDtypeStruct((8, DI), F32),
            jax.ShapeDtypeStruct((NSTATE, DI), F32),
        ],
        scratch_shapes=[pltpu.VMEM((BLOCK, DI), F32), pltpu.VMEM((BLOCK, DI), F32)],
        compiler_params=pltpu.CompilerParams(vmem_limit_bytes=48 << 20),
        cost_estimate=pl.CostEstimate(flops=12 << 30, bytes_accessed=32 << 20, transcendentals=4 << 20),
        name="middle",
    )(y, bc, incoming, ed, e2, x, gate, dno, gains)


def spot():
    wt, seq = lax.axis_index("wt"), lax.axis_index("seq")
    return wt // 2, wt % 2, seq % 2


def relative(block):
    x, core, _ = spot()
    high, low = block // 2, block % 2
    return 2 * (core + low - 2 * core * low) + (x + high - 2 * x * high)


def across_bit(axis, bit):
    index = lax.axis_index(axis)
    return {axis: index + bit - 2 * bit * ((index // bit) % 2)}


def greet(devices):
    barrier = pltpu.get_barrier_semaphore()
    for device in devices:
        pl.semaphore_signal(barrier, inc=1, device_id=device, device_id_type=MESH)
    pl.semaphore_wait(barrier, len(devices))


class Piece:
    def __init__(self, source, near, mine, pair, twin, half, sems, at):
        bit = 1 + at % 2
        part = pl.multiple_of((lax.axis_index("seq") // bit) % 2 * half, 16)
        own, xs, xr, ys, yr, ts, tr, keep = sems
        rows = lambda ref: ref.at[pl.ds(part, half), :]
        self.own = pltpu.make_async_copy(source, mine, own.at[at])
        self.x = self.remote(rows(source), rows(near), xs.at[at], xr.at[at], across_bit("wt", 2))
        self.y = self.remote(rows(near), rows(near), ys.at[at], yr.at[at], across_bit("seq", bit))
        self.twin = self.remote(pair, twin, ts.at[at], tr.at[at], across_bit("wt", 1))

    def remote(self, source, target, send, recv, device):
        return pltpu.make_async_remote_copy(src_ref=source, dst_ref=target, send_sem=send, recv_sem=recv, device_id=device, device_id_type=MESH)


def gather_sems(count):
    return [pltpu.SemaphoreType.DMA((count,)) for _ in range(8)]


def enter_kernel(tok_ref, gain_ref, kernel_ref, bias_ref, step_ref, log_ref, e2_ref, w_ref, taps_ref, heads_ref, proj_ref, normed_ref, x_ref, bc_ref, dt_ref, rb_ref, rt_ref, er_ref, ew_ref, d2_ref, ed_ref, state_ref, all_ref, wide_ref, last_ref, edge_ref, pad_ref, wd_ref, edge_sem, *sems):
    length = tok_ref.shape[0]
    begin = Begin(proj_ref, taps_ref, heads_ref, e2_ref, x_ref, bc_ref, dt_ref, rb_ref, rt_ref, er_ref, ew_ref, d2_ref, ed_ref, state_ref, pad_ref, wd_ref)
    seq, peers = lax.axis_index("seq"), lax.axis_size("seq")
    following, previous = {"seq": lax.rem(seq + 1, peers)}, {"seq": lax.rem(seq + peers - 1, peers)}
    greet([across_bit("wt", 1), across_bit("wt", 2), across_bit("seq", 1), across_bit("seq", 2), following, previous])
    edge = pltpu.make_async_remote_copy(src_ref=tok_ref.at[length - EDGE : length, :], dst_ref=edge_ref, send_sem=edge_sem.at[0], recv_sem=edge_sem.at[1], device_id=following, device_id_type=MESH)
    edge.start()
    count = CDIM // TILE
    pieces, products, keeps = [], [], []

    def add(target, first, rows):
        pieces.append(Piece(w_ref.at[pl.ds(first, rows), :], target.at[:, PART : 2 * PART], target.at[:, :PART], target.at[:, : 2 * PART], target.at[:, 2 * PART :], rows // 2, sems, len(pieces)))
        products.append(None)

    def multiply(target, columns, skip, then):
        keep = pltpu.make_async_copy(target.at[skip:, :], all_ref.at[columns, :], sems[-1].at[len(keeps)])
        keeps.append(keep)

        def product():
            keep.start()
            proj_ref[:, columns] = nt(normed_ref[...], target[skip:, :]).astype(LOW)
            then()

        products[-1] = product

    add(last_ref, DI + CDIM + HEADS - LAST, LAST)
    multiply(last_ref, slice(count * TILE, CDIM + HEADS), LAST - (CDIM + HEADS - count * TILE), begin.sizes)
    for c in range(count):
        for first in range(c * TILE, (c + 1) * TILE, FINE):
            add(wide_ref.at[first : first + FINE, :], DI + first, FINE)
        multiply(wide_ref.at[c * TILE : (c + 1) * TILE, :], slice(c * TILE, (c + 1) * TILE), 0, lambda c=c: begin.block(c))
    for piece in pieces:
        piece.own.start()
    for piece in pieces[:AHEAD]:
        piece.x.start()

    def norm(v):
        v = v.astype(F32)
        return (v * lax.rsqrt(jnp.mean(v * v, axis=-1, keepdims=True) + EPS) * gain_ref[0:1, :]).astype(LOW)

    def place(at, v):
        for b in range(PARTS):
            normed_ref[at, pl.ds(pl.multiple_of(relative(b) * PART, LANES), PART)] = v[:, b * PART : (b + 1) * PART]

    taps_ref[...] = jnp.zeros_like(taps_ref)
    taps_ref[0:CONV, :CDIM] = kernel_ref[...]
    taps_ref[CONV : CONV + 1, :CDIM] = bias_ref[...]
    heads_ref[...] = jnp.zeros_like(heads_ref)
    heads_ref[0:1, :HEADS] = step_ref[...]
    heads_ref[1:2, :HEADS] = log_ref[...]
    place(slice(EDGE, EDGE + length), norm(tok_ref[...]))
    edge.wait()
    place(slice(0, EDGE), norm(jnp.where(seq == 0, 0.0, edge_ref[...].astype(F32))))
    travel_on(pieces, products)
    for keep in keeps:
        keep.wait()


def travel_on(pieces, products, ahead=AHEAD, between=None):
    count = len(pieces)
    for t in range(count + 2 * LAG):
        if t < count:
            pieces[t].x.wait_recv()
            pieces[t].y.start()
            if t + ahead < count:
                pieces[t + ahead].x.start()
        if 0 <= t - LAG < count:
            pieces[t - LAG].y.wait_recv()
            pieces[t - LAG].own.wait()
            pieces[t - LAG].twin.start()
        if 0 <= t - 2 * LAG < count:
            pieces[t - 2 * LAG].twin.wait_recv()
            if products[t - 2 * LAG] is not None:
                products[t - 2 * LAG]()
        if between is not None:
            between(t)
    for piece in pieces:
        piece.x.wait_send()
        piece.y.wait_send()
        piece.twin.wait_send()


def enter(tokens, gain, conv_kernel, conv_bias, step_bias, decay_log, e2, weight):
    length, columns = tokens.shape[0], CDIM + HEADS
    vmem, hbm = pl.BlockSpec(memory_space=pltpu.VMEM), pl.BlockSpec(memory_space=pl.ANY)
    shapes = [
        ((8, LONG), F32),
        ((8, LANES), F32),
        ((length + EDGE, columns), LOW),
        ((length + EDGE, DM), LOW),
        ((length, DI), LOW),
        ((length, 2 * NSTATE), LOW),
        ((length, LANES), F32),
        ((length, LANES * STEPS), F32),
        ((LANES, length), F32),
        ((length, 2 * LANES), LOW),
        ((length, 2 * LANES), LOW),
        ((length, 2 * LANES), LOW),
        ((length, 2 * LANES), LOW),
        ((NSTATE + 16, DI), LOW),
        ((columns, DM), LOW),
    ]
    return pl.pallas_call(
        enter_kernel,
        in_specs=[vmem] * 7 + [hbm],
        out_specs=[vmem] * (len(shapes) - 1) + [hbm],
        out_shape=[jax.ShapeDtypeStruct(shape, kind) for shape, kind in shapes],
        scratch_shapes=[
            pltpu.VMEM((CDIM // TILE * TILE, DM), LOW),
            pltpu.VMEM((LAST, DM), LOW),
            pltpu.VMEM((EDGE, DM), LOW),
            pltpu.VMEM((length + EDGE, WIDE), F32),
            pltpu.VMEM((length, 2 * LANES), LOW),
            pltpu.SemaphoreType.DMA((2,)),
        ]
        + gather_sems(CDIM // TILE * (TILE // FINE) + 1),
        compiler_params=pltpu.CompilerParams(vmem_limit_bytes=56 << 20, collective_id=0, has_side_effects=True),
        cost_estimate=pl.CostEstimate(flops=40 << 30, bytes_accessed=30 << 20, transcendentals=0),
        name="enter",
    )(tokens, gain, conv_kernel, conv_bias, step_bias, decay_log, e2, weight)


class Passing:
    def __init__(self, later, total, factor, reach, held, send, recv, met, send_sem, recv_sem):
        self.later, self.total, self.factor, self.reach, self.held = later, total, factor, reach, held
        self.send, self.recv, self.met, self.send_sem, self.recv_sem = send, recv, met, send_sem, recv_sem
        self.bits = seq_bits()

    def columns(self, j):
        return pl.ds(pl.multiple_of(j * WIDE, WIDE), WIDE)

    def copy(self, k, j):
        at = self.columns(j)
        return pltpu.make_async_remote_copy(src_ref=self.send.at[:, at], dst_ref=self.recv.at[k, :, at], send_sem=self.send_sem.at[k, j], recv_sem=self.recv_sem.at[k, j], device_id=across_bit("seq", self.bits[k]), device_id_type=MESH)

    def start(self, k, j):
        at = self.columns(j)
        self.send[0:NSTATE, at] = self.total[:, at].astype(LOW)
        if not self.later:
            factor = self.factor[0:1, at]
            high = factor.astype(LOW).astype(F32)
            ids = lax.broadcasted_iota(jnp.int32, (16, WIDE), 0)
            self.send[NSTATE : NSTATE + 16, at] = jnp.where(ids == 0, high, jnp.where(ids == 1, factor - high, 0.0)).astype(LOW)
        self.copy(k, j).start()

    def finish(self, k, j):
        self.copy(k, j).wait()
        at = self.columns(j)
        bit = self.bits[k]
        second = (lax.axis_index("seq") // bit) % 2
        takes = second == (0 if self.later else 1)
        other = self.recv[k, 0:NSTATE, at].astype(F32)
        if self.later:
            met = self.met[k : k + 1, at]
        else:
            rows = self.recv[k, NSTATE : NSTATE + 16, at].astype(F32)
            met = rows[0:1] + rows[1:2]
            self.met[k : k + 1, at] = met
        total, factor, reach = self.total[:, at], self.factor[0:1, at], self.reach[0:1, at]
        self.held[:, at] = self.held[:, at] + jnp.where(takes, reach, 0.0) * other
        self.reach[0:1, at] = jnp.where(takes, reach * met, reach)
        if k + 1 < len(self.bits):
            self.total[:, at] = jnp.where(takes, factor, 1.0) * other + jnp.where(takes, 1.0, met) * total
            self.factor[0:1, at] = factor * met
            self.start(k + 1, j)

    def due(self, k, j):
        last = len(self.bits) - 1
        return 2 + 3 * k + 2 * j if k < last else 2 + 3 * last + 3 * j

    def step(self, t):
        for k in range(len(self.bits)):
            for j in range(STEPS):
                if t == self.due(k, j):
                    self.finish(k, j)

    def rest(self, t):
        for late in range(t, self.due(len(self.bits) - 1, STEPS - 1) + 1):
            self.step(late)


def gates_kernel(normed_ref, up_ref, state_ref, x_ref, bc_ref, rb_ref, rt_ref, er_ref, ew_ref, d2_ref, e2_ref, w_ref, o_ref, incoming_ref, met_ref, y_out, states_out, gate_out, dno_out, wall_ref, wide_ref, deep_ref, total_ref, factor_ref, reach_ref, held_ref, send_ref, recv_ref, own_ref, y_ref, states_ref, gate_ref, dno_ref, ss_sem, sr_sem, deep_sem, stage_sem, *sems):
    stages = [Stages(ref, stage_sem.at[i]) for i, ref in enumerate((y_ref, states_ref, gate_ref, dno_ref))]
    local = Inside(x_ref, bc_ref, rb_ref, rt_ref, er_ref, ew_ref, d2_ref, e2_ref, own_ref, y_out, states_out, stages[0], stages[1])
    greet([across_bit("wt", 1), across_bit("wt", 2)] + [across_bit("seq", bit) for bit in seq_bits()])
    passing = Passing(False, total_ref, factor_ref, reach_ref, held_ref, send_ref, recv_ref, met_ref, ss_sem, sr_sem)
    total_ref[...] = state_ref[0:NSTATE, :].astype(F32)
    rows = state_ref[NSTATE : NSTATE + 16, :].astype(F32)
    factor_ref[0:1, :] = rows[0:1] + rows[1:2]
    reach_ref[...] = jnp.ones_like(reach_ref)
    held_ref[...] = jnp.zeros_like(held_ref)
    met_ref[...] = jnp.zeros_like(met_ref)
    met_ref[7:8, :] = factor_ref[0:1, :]
    for j in range(STEPS):
        passing.start(0, j)
    pieces, products, keeps = [], [], []

    for c in range(DI // FINE):
        rows = slice(c * FINE, (c + 1) * FINE)
        target = wide_ref.at[rows, :]
        pieces.append(Piece(w_ref.at[rows, :], target.at[:, PART : 2 * PART], target.at[:, :PART], target.at[:, : 2 * PART], target.at[:, 2 * PART :], FINE // 2, sems, len(pieces)))
        keeps.append(pltpu.make_async_copy(target, wall_ref.at[rows, :], sems[-1].at[c]))

        def product(rows=rows, keep=keeps[-1]):
            keep.start()
            stages[2].put(nt(normed_ref[EDGE:, :], wide_ref[rows, :]).astype(LOW), gate_out.at[:, rows])

        products.append(product)

    for c in range(OUT_PART // SHORT):
        rows = slice(c * SHORT, (c + 1) * SHORT)
        pieces.append(Piece(o_ref.at[rows, :], deep_ref.at[1, rows, :], deep_ref.at[0, rows, :], deep_ref.at[0:2, rows, :], deep_ref.at[2:4, rows, :], SHORT // 2, sems, len(pieces)))
        products.append(None)
        if (c + 1) * SHORT % FINE == 0:
            first = (c + 1) * SHORT - FINE
            mine = [pltpu.make_async_copy(deep_ref.at[b, first : first + FINE, :], wall_ref.at[pl.ds(DI + b * OUT_PART + first, FINE), :], deep_sem.at[first // FINE, b]) for b in range(PARTS)]
            keeps.extend(mine)

            def product(first=first, mine=mine):
                for b in range(PARTS):
                    mine[b].start()
                    at = b * OUT_PART + first
                    stages[3].put(nt(up_ref[...], deep_ref[b, first : first + FINE, :]), dno_out.at[:, at : at + FINE])

            products[-1] = product

    for piece in pieces:
        piece.own.start()
    for piece in pieces[:AHEAD]:
        piece.x.start()

    def between(t):
        passing.step(t)
        local.turn(t)

    travel_on(pieces, products, between=between)
    for t in range(len(pieces) + 2 * LAG, STEPS * local.blocks):
        local.turn(t)
    passing.rest(len(pieces) + 2 * LAG)
    for stage in stages:
        stage.rest()
    incoming_ref[...] = held_ref[...].astype(LOW)
    for keep in keeps:
        keep.wait()


def gates(normed, upstream, state, x, bc, rb, rt, er, ew, d2, e2, weight, out_weight):
    length = upstream.shape[0]
    bits = len(seq_bits())
    vmem, hbm = pl.BlockSpec(memory_space=pltpu.VMEM), pl.BlockSpec(memory_space=pl.ANY)
    dma = pltpu.SemaphoreType.DMA
    return pl.pallas_call(
        gates_kernel,
        in_specs=[vmem] * 11 + [hbm, hbm],
        out_specs=[vmem, vmem] + [hbm] * 5,
        out_shape=[
            jax.ShapeDtypeStruct((NSTATE, DI), LOW),
            jax.ShapeDtypeStruct((8, DI), F32),
            jax.ShapeDtypeStruct((length, DI), F32),
            jax.ShapeDtypeStruct((length // BLOCK, NSTATE, DI), LOW),
            jax.ShapeDtypeStruct((length, DI), LOW),
            jax.ShapeDtypeStruct((length, DI), F32),
            jax.ShapeDtypeStruct((2 * DI, DM), LOW),
        ],
        scratch_shapes=[
            pltpu.VMEM((DI, DM), LOW),
            pltpu.VMEM((PARTS, OUT_PART, DM), LOW),
            pltpu.VMEM((NSTATE, DI), F32),
            pltpu.VMEM((8, DI), F32),
            pltpu.VMEM((8, DI), F32),
            pltpu.VMEM((NSTATE, DI), F32),
            pltpu.VMEM((NSTATE + 16, DI), LOW),
            pltpu.VMEM((bits, NSTATE + 16, DI), LOW),
            pltpu.VMEM((NSTATE, WIDE), F32),
            pltpu.VMEM((2, BLOCK, WIDE), F32),
            pltpu.VMEM((2, NSTATE, WIDE), LOW),
            pltpu.VMEM((2, length, FINE), LOW),
            pltpu.VMEM((2, length, FINE), F32),
            dma((bits, STEPS)),
            dma((bits, STEPS)),
            dma((OUT_PART // FINE, PARTS)),
            dma((4, 2)),
        ]
        + gather_sems(DI // FINE + OUT_PART // SHORT),
        compiler_params=pltpu.CompilerParams(vmem_limit_bytes=58 << 20, collective_id=1, has_side_effects=True),
        cost_estimate=pl.CostEstimate(flops=50 << 30, bytes_accessed=50 << 20, transcendentals=0),
        name="gates",
    )(normed, upstream, state, x, bc, rb, rt, er, ew, d2, e2, weight, out_weight)


def seq_bits():
    bits, bit = [], 1
    while bit < lax.axis_size("seq"):
        bits.append(bit)
        bit *= 2
    return bits


ROWS = 128
LEAST = 16


class Reducer:
    def __init__(self, out, gate, conv, din, dout, held, core, sx, rx, near, res, load_sem, keep_sem, send_sem, recv_sem, parts):
        self.out, self.gate, self.conv, self.din, self.dout = out, gate, conv, din, dout
        self.held, self.core, self.sx, self.rx, self.near, self.res = held, core, sx, rx, near, res
        self.load_sem, self.keep_sem, self.send_sem, self.recv_sem, self.parts = load_sem, keep_sem, send_sem, recv_sem, parts
        bits = seq_bits()
        seq = lax.axis_index("seq")
        self.steps = len(bits)
        self.halved = halved_bits()
        self.partners = [across_bit("wt", 1), across_bit("wt", 2)] + [across_bit("seq", bit) for bit in bits]
        self.second = [(seq // bit) % 2 for bit in bits]
        self.bases, self.sizes = [0], [ROWS]
        for bit in bits[: self.halved]:
            size = self.sizes[-1] // 2
            self.bases.append(self.bases[-1] + ((seq // bit) % 2) * size)
            self.sizes.append(size)
        self.stages = 2 + self.steps + self.halved
        self.out_count = PARTS * (OUT_PART // ROWS)
        self.gate_count = DI // ROWS
        self.columns = CDIM + HEADS
        self.count = self.out_count + self.gate_count + -(-self.columns // ROWS)
        self.total = self.count + SLACK * self.stages + 1

    def rows_at(self, j):
        return pl.ds(pl.multiple_of(self.bases[j], LEAST), self.sizes[j])

    def kinds(self, c, act):
        first_gate, first_conv = self.out_count, self.out_count + self.gate_count

        @pl.when(c < first_gate)
        def _():
            first = pl.multiple_of((c // PARTS) * ROWS, 16)
            columns = pl.ds(pl.multiple_of((c % PARTS) * PART, LANES), PART)
            act([self.out.at[pl.ds(b * OUT_PART + first, ROWS), columns] for b in range(PARTS)], lambda: self.dout.at[pl.ds(first, ROWS), columns])

        @pl.when(jnp.logical_and(c >= first_gate, c < first_conv))
        def _():
            first = pl.multiple_of((c - first_gate) * ROWS, 16)
            act([self.gate.at[pl.ds(first, ROWS), :]], lambda: self.din.at[pl.ds(first, ROWS), :])

        @pl.when(c >= first_conv)
        def _():
            first = pl.multiple_of(jnp.minimum((c - first_conv) * ROWS, self.columns - ROWS), 16)
            act([self.conv.at[pl.ds(first, ROWS), :]], lambda: self.din.at[pl.ds(DI + first, ROWS), :])

    def load(self, c):
        few = lax.rem(c, FEW)

        def act(sources, target):
            width = DM // len(sources)
            for b, source in enumerate(sources):
                pltpu.make_async_copy(source, self.held.at[few, :, b * width : (b + 1) * width], self.load_sem.at[few]).start()

        self.kinds(c, act)

    def exchange(self, s, slot, few):
        if s == 0:
            source, target = self.held.at[few, :, 2 * PART :], self.core.at[few]
        elif s == 1:
            source, target = self.sx.at[few], self.rx.at[few]
        elif s < 2 + self.steps:
            source, target = self.parts[3 * (s - 2)].at[few], self.parts[3 * (s - 2) + 1].at[few]
        else:
            j = self.stages - 1 - s
            source = target = self.res.at[slot, self.rows_at(j + 1), :]
        partner = self.partners[s] if s < 2 + self.steps else self.partners[2 + self.stages - 1 - s]
        return pltpu.make_async_remote_copy(src_ref=source, dst_ref=target, send_sem=self.send_sem.at[s, few], recv_sem=self.recv_sem.at[s, few], device_id=partner, device_id_type=MESH)

    def loaded(self, few):
        pltpu.make_async_copy(self.gate.at[0:ROWS, :], self.held.at[few], self.load_sem.at[few]).wait()

    def kept(self, slot):
        return pltpu.make_async_copy(self.res.at[slot], self.din.at[0:ROWS, :], self.keep_sem.at[slot])

    def combine(self, s, slot, few):
        if s == 0:
            self.near[few] = self.held[few, :, :PART].astype(F32) + self.core[few, :, :PART].astype(F32)
            self.sx[few] = (self.held[few, :, PART : 2 * PART].astype(F32) + self.core[few, :, PART:].astype(F32)).astype(LOW)
        elif s == 1:
            self.lay(self.near[few] + self.rx[few].astype(F32), 0, slot, few)
        elif s < 2 + self.steps:
            j = s - 2
            mine = self.parts[3 * j + 2][few] if j < self.halved else self.parts[3 * j][few].astype(F32)
            self.lay(mine + self.parts[3 * j + 1][few].astype(F32), j + 1, slot, few)

    def lay(self, value, j, slot, few):
        if j == self.steps:
            self.res[slot, self.rows_at(self.halved), :] = value.astype(LOW)
        elif j < self.halved:
            size = self.sizes[j + 1]
            low, high = value[:size], value[size:]
            second = self.second[j] == 1
            self.parts[3 * j][few] = jnp.where(second, low, high).astype(LOW)
            self.parts[3 * j + 2][few] = jnp.where(second, high, low)
        else:
            self.parts[3 * j][few] = value.astype(LOW)

    def write(self, c, slot):
        self.kinds(c, lambda sources, target: pltpu.make_async_copy(self.res.at[slot], target(), self.keep_sem.at[slot]).start())

    def step(self, t):
        steady = jnp.logical_and(t > SLACK * self.stages, t < self.count)

        @pl.when(steady)
        def _():
            slots = [(lax.rem(t - SLACK * s, SLOTS), lax.rem(t - SLACK * s, FEW)) for s in range(self.stages + 1)]
            self.kept(lax.rem(t - SLACK * self.stages - 1, SLOTS)).wait()
            for s in range(self.stages, 0, -1):
                self.exchange(s - 1, *slots[s]).wait()
            self.loaded(slots[0][1])
            for s in range(self.stages, 0, -1):
                self.combine(s - 1, *slots[s])
            for s in range(1, self.stages):
                self.exchange(s, *slots[s]).start()
            self.exchange(0, *slots[0]).start()
            self.write(t - SLACK * self.stages, slots[self.stages][0])

        @pl.when(jnp.logical_not(steady))
        def _():
            c = t - SLACK * self.stages - 1

            @pl.when(jnp.logical_and(c >= 0, c < self.count))
            def _():
                self.kept(lax.rem(c, SLOTS)).wait()

            for s in range(self.stages, -1, -1):
                c = t - SLACK * s

                @pl.when(jnp.logical_and(c >= 0, c < self.count))
                def _(c=c, s=s):
                    slot, few = lax.rem(c, SLOTS), lax.rem(c, FEW)
                    if s > 0:
                        self.exchange(s - 1, slot, few).wait()
                        self.combine(s - 1, slot, few)
                    else:
                        self.loaded(few)
                    if s < self.stages:
                        self.exchange(s, slot, few).start()
                    else:
                        self.write(c, slot)

        @pl.when(t + 1 < self.count)
        def _():
            self.load(t + 1)


def halved_bits():
    count, rows = 0, ROWS
    while count < len(seq_bits()) and rows > LEAST:
        count, rows = count + 1, rows // 2
    return count


BLOCKS = 4
PER = 2
HALF = BLOCKS // PER
TURNS = HALF + 1
NEAR_STEPS, BACK_STEPS, EDGE_STEPS, DOT_STEPS, GATE_STEPS = STEPS * HALF, STEPS * TURNS + 1, 1, STEPS + 1, STEPS
BACK_AT = NEAR_STEPS
EDGE_AT = BACK_AT + BACK_STEPS
DOT_AT = EDGE_AT + EDGE_STEPS
PULL_AT = DOT_AT + DOT_STEPS
PULL_STEPS = 2 * GATE_STEPS + DOT_STEPS
LAST_AT = PULL_AT + PULL_STEPS
ALL_STEPS = LAST_AT + 1
PACE = ((0, NEAR_STEPS, 17), (BACK_AT, BACK_STEPS, 23), (EDGE_AT, EDGE_STEPS, 2), (DOT_AT, DOT_STEPS, 5), (PULL_AT, PULL_STEPS, 30))
DONE = sum(turns for _, _, turns in PACE)


def clip(v, low, high):
    return jnp.minimum(jnp.maximum(v, low), high)


def paced(g):
    done = 0
    for first, steps, turns in PACE:
        done = done + (turns * clip(g - first, 0, steps)) // steps
    return done


def head_block(g):
    near = jnp.minimum(g // HALF, STEPS)
    over = near // STEPS
    return near * (1 - over) + over * clip((g - BACK_AT) // TURNS, 0, STEPS - 1)


def rear_kernel(pc_ref, x_ref, dy_ref, bc_ref, rb_ref, rt_ref, er_ref, ew_ref, d2_ref, ed_ref, dt_ref, e2_ref, et_ref, states_ref, in_ref, taps_ref, skip_ref, heads_ref, met_ref, normed_ref, tok_ref, up_ref, gain_ref, sums_ref, low_ref, dgate_ref, wgate_ref, wconv_ref, din_ref, gout_ref, ggate_ref, sum_in_ref, sum_out_ref, small_ref, dtok_ref, mixed_ref, gconv_ref, pad_ref, dact_ref, dheld_ref, direct_ref, dconv_ref, dscores_ref, dbc_ref, ddt_ref, q_ref, v_ref, ends_ref, crossed_ref, stage_ref, rim_ref, rim_got_ref, one_sem, total_ref, factor_ref, reach_ref, held_ref, psend_ref, precv_ref, ps_sem, pr_sem, vsend_ref, vrecv_ref, vs_sem, vr_sem, r_held, r_core, r_sx, r_rx, r_near, r_res, load_sem, keep_sem, send_sem, recv_sem, *parts):
    g = pl.program_id(0)
    length = x_ref.shape[0]
    seq, peers = lax.axis_index("seq"), lax.axis_size("seq")
    following, previous = {"seq": lax.rem(seq + 1, peers)}, {"seq": lax.rem(seq + peers - 1, peers)}
    reducer = Reducer(gout_ref, ggate_ref, gconv_ref, sum_in_ref, sum_out_ref, r_held, r_core, r_sx, r_rx, r_near, r_res, load_sem, keep_sem, send_sem, recv_sem, parts)
    passing = Passing(True, total_ref, factor_ref, reach_ref, held_ref, psend_ref, precv_ref, met_ref, ps_sem, pr_sem)
    rounds = len(passing.bits)
    block = head_block(g)
    edge = pltpu.make_async_remote_copy(src_ref=rim_ref, dst_ref=rim_got_ref, send_sem=one_sem.at[0], recv_sem=one_sem.at[1], device_id=previous, device_id_type=MESH)

    @pl.when(g == 0)
    def _():
        greet(reducer.partners + [following, previous])
        first = pltpu.make_async_copy(din_ref, total_ref, one_sem.at[2])
        first.start()
        for ref in (dscores_ref, dbc_ref, ddt_ref, q_ref, v_ref, ends_ref, crossed_ref, held_ref):
            ref[...] = jnp.zeros_like(ref)
        reach_ref[...] = jnp.ones_like(reach_ref)
        factor_ref[0:1, :] = met_ref[7:8, :]
        first.wait()
        for j in range(STEPS):
            passing.start(0, j)
        reducer.load(jnp.int32(0))

    for k in range(rounds - 1):
        since = g - (1 + 2 * k)

        @pl.when(jnp.logical_and(since >= 0, since < STEPS))
        def _(k=k, since=since):
            passing.finish(k, since)

    def near_block(c):
        at = pl.ds(pl.multiple_of(c * BLOCK, BLOCK), BLOCK)
        ids, jds = rows_cols((BLOCK, BLOCK))
        suffix = (ids >= jds).astype(LOW)
        left = lax.broadcasted_iota(jnp.int32, (BLOCK, LANES), 1) < HDIM
        scores = jnp.where(ids <= jds, nt(bc_ref[at, :NSTATE], bc_ref[at, NSTATE:]), 0.0)
        dy = dy_ref[at, :]
        sized = x_ref[at, :].astype(F32) * nn(d2_ref[at, :], e2_ref[...])
        total = jnp.zeros((BLOCK, BLOCK), F32)
        rows = []
        for pair in range(GROUP // 2):
            lanes = slice(pair * LANES, (pair + 1) * LANES)
            piece, dpiece = sized[:, lanes], dy[:, lanes]
            both = jnp.concatenate([jnp.where(left, piece, 0.0), jnp.where(left, 0.0, piece)], axis=0).astype(LOW)
            meets = nn(both, dpiece.T)
            mixed, kept = [], []
            for half in range(2):
                head = 2 * pair + half
                spread = rt_ref[head : head + 1, at] - rb_ref[at, head : head + 1]
                decay = jnp.exp(jnp.minimum(spread, 0.0))
                meet = meets[half * BLOCK : (half + 1) * BLOCK] * decay
                total = total + meet
                mixed.append((scores * decay).astype(LOW))
                kept.append((meet * scores).astype(LOW))
            later = nn(jnp.concatenate(kept, axis=0), suffix)
            for half in range(2):
                one = later[half * BLOCK : (half + 1) * BLOCK]
                rows.append(jnp.sum(jnp.where(ids < jds, one, 0.0), axis=0, keepdims=True))
            none = jnp.zeros_like(dpiece)
            both = jnp.concatenate([jnp.where(left, dpiece, none), jnp.where(left, none, dpiece)], axis=0)
            direct_ref[block, at, lanes] = nn(jnp.concatenate(mixed, axis=1), both)
        dscores_ref[c] += total
        crossed_ref[pl.ds(pl.multiple_of(block * GROUP, GROUP), GROUP), at] = jnp.concatenate(rows, axis=0)

    @pl.when(g < NEAR_STEPS)
    def _():
        @pl.loop(0, PER)
        def _(i):
            near_block((g % HALF) * PER + i)

    turn = g - BACK_AT
    part = turn % TURNS
    going = jnp.logical_and(turn >= 0, turn < STEPS * TURNS)

    @pl.when(jnp.logical_and(going, part == 0))
    def _():
        passing.finish(rounds - 1, block)
        dheld_ref[...] = held_ref[:, passing.columns(block)]

    def back_block(c):
        at = pl.ds(pl.multiple_of(c * BLOCK, BLOCK), BLOCK)
        input_mat, output_mat = bc_ref[at, :NSTATE], bc_ref[at, NSTATE:]
        e2, et = e2_ref[...], et_ref[...]
        grow, leave, size = nn(er_ref[at, :], e2), nn(ew_ref[at, :], e2), nn(d2_ref[at, :], e2)
        prior = pl.ds(pl.multiple_of(jnp.maximum(c * BLOCK - 16, 0), 16), 16)
        reach = nn(ed_ref[prior, :], e2)[15:16, :]
        reach = jnp.where(c == 0, 1.0, reach)
        state = states_ref[c].astype(F32) + reach * in_ref[...].astype(F32)
        state_low = state.astype(LOW)
        x = x_ref[at, :].astype(F32)
        dy = dy_ref[at, :].astype(F32)
        dheld = dheld_ref[...]
        dheld_low = dheld.astype(LOW)
        grown = (dy * grow).astype(LOW)
        pulled = nn(input_mat, dheld_low) * leave
        dbc_ref[at, :NSTATE] += nt((x * size * leave).astype(LOW), dheld_low)
        dbc_ref[at, NSTATE:] += nt(grown, state_low)
        carried = nn(output_mat, state_low) * grow
        q_ref[at, :] += nn((dy * carried).astype(LOW), et)
        v_ref[at, :] += nn((x * pulled).astype(LOW), et)
        last = grow[BLOCK - 1 : BLOCK, :]
        ends = jnp.sum(state * dheld, axis=0, keepdims=True) * last
        ends_ref[c] += nn(jnp.broadcast_to(ends, (16, WIDE)).astype(LOW), et)[:8]
        dheld_ref[...] = dheld * last + tn(output_mat, grown)
        direct = direct_ref[block, at, :] + pulled
        ddt_ref[at, :] += nn((x * direct).astype(LOW), et)
        dact_ref[at, :] = size * direct + skip_ref[0:1, :] * dy

    @pl.when(jnp.logical_and(going, part < HALF))
    def _():
        @pl.loop(0, PER)
        def _(i):
            back_block(BLOCKS - 1 - (part * PER + i))

    @pl.when(turn == STEPS * TURNS)
    def _():
        ids, jds = rows_cols((BLOCK, BLOCK))
        upper = (ids <= jds).astype(F32)
        under = (ids > jds).astype(F32)
        rate = jnp.exp(heads_ref[1:2, :])
        dstep_bias = jnp.zeros((1, LANES), F32)
        ddecay_log = jnp.zeros((1, LANES), F32)
        for c in range(BLOCKS):
            at = slice(c * BLOCK, (c + 1) * BLOCK)
            dscores = jnp.where(ids <= jds, dscores_ref[c], 0.0).astype(LOW)
            dact_ref[at, :NSTATE] = dbc_ref[at, :NSTATE] + nn(dscores, bc_ref[at, NSTATE:])
            dact_ref[at, NSTATE : 2 * NSTATE] = dbc_ref[at, NSTATE:] + tn(dscores, bc_ref[at, :NSTATE])
            dt = dt_ref[at, :]
            ddecay = crossed_ref[:, at].T + exact(upper, q_ref[at, :]) + exact(under, v_ref[at, :] * dt) + ends_ref[c][0:1, :]
            draw = ddt_ref[at, :] - ddecay * rate
            ddecay_log = ddecay_log - jnp.sum(ddecay * dt, axis=0, keepdims=True) * rate
            raw = pc_ref[EDGE + c * BLOCK : EDGE + (c + 1) * BLOCK, 2 * NSTATE : 2 * NSTATE + LANES].astype(F32)
            used = lax.broadcasted_iota(jnp.int32, raw.shape, 1) < HEADS
            draw = draw * jax.nn.sigmoid(jnp.where(used, raw + heads_ref[0:1, :], 0.0))
            dstep_bias = dstep_bias + jnp.sum(draw, axis=0, keepdims=True)
            dact_ref[at, 2 * NSTATE : 2 * NSTATE + LANES] = draw
            dact_ref[at, 2 * NSTATE + LANES :] = jnp.zeros((BLOCK, LANES), F32)
        ends_ref[0] = jnp.broadcast_to(dstep_bias, (8, LANES))
        ends_ref[1] = jnp.broadcast_to(ddecay_log, (8, LANES))

    @pl.when(jnp.logical_or(jnp.logical_and(going, part == HALF), turn == STEPS * TURNS))
    def _():
        here = turn // TURNS
        at = pl.ds(pl.multiple_of(here * WIDE, WIDE), WIDE)
        taps = taps_ref[:, at]
        pad_ref[...] = pc_ref[...].astype(F32)
        summed = taps[CONV : CONV + 1]
        for k in range(CONV):
            first = EDGE - CONV + 1 + k
            summed = summed + taps[k : k + 1] * pad_ref[first : first + length, :]
        shape = jax.nn.sigmoid(summed)
        dsum = dact_ref[0:length, :] * (shape * (1.0 + summed * (1.0 - shape)))
        dtap = [jnp.sum(dsum * pad_ref[EDGE - CONV + 1 + k : EDGE - CONV + 1 + k + length, :], axis=0, keepdims=True) for k in range(CONV)]
        dtap.append(jnp.sum(dsum, axis=0, keepdims=True))
        vsend_ref[0, :, at] = jnp.concatenate(dtap + [jnp.zeros((8 - len(dtap), WIDE), F32)], axis=0)
        rim_ref[:, at] = dsum[:16].astype(LOW)
        keep = dact_ref[0:length, :]
        dact_ref[0:length, :] = dsum
        dact_ref[length:, :] = jnp.zeros_like(dact_ref[length:, :])
        result = taps[CONV - 1 : CONV] * dsum
        for k in range(CONV - 1):
            by = CONV - 1 - k
            result = result + taps[k : k + 1] * dact_ref[by : by + length, :]
        lane = lax.broadcasted_iota(jnp.int32, (1, WIDE), 1)
        raw_part = jnp.logical_and(turn == STEPS * TURNS, lane >= 2 * NSTATE)
        dconv_ref[:, at] = jnp.where(raw_part, keep, result).astype(LOW)

    @pl.when(turn == STEPS * TURNS)
    def _():
        edge.start()

    @pl.when(g == EDGE_AT)
    def _():
        edge.wait()
        bottom = slice(length - 16, length)
        inner = seq < peers - 1
        for j in range(STEPS + 1):
            at = slice(j * WIDE, min((j + 1) * WIDE, CDIM))
            got = rim_got_ref[:, at].astype(F32)
            ids = lax.broadcasted_iota(jnp.int32, got.shape, 0)
            extra = jnp.zeros_like(got)
            for i in range(CONV - 1):
                row = sum(taps_ref[k : k + 1, at] * got[i - k : i - k + 1] for k in range(i + 1))
                extra = jnp.where(ids == 16 - CONV + 1 + i, row, extra)
            extra = jnp.where(inner, extra, 0.0)
            dconv_ref[bottom, at] = (dconv_ref[bottom, at].astype(F32) + extra).astype(LOW)

    dot_turn = g - DOT_AT

    def stored(k):
        return pltpu.make_async_copy(stage_ref, gconv_ref.at[pl.ds(pl.multiple_of(k * WIDE, WIDE), WIDE), :], one_sem.at[2])

    @pl.when(jnp.logical_and(dot_turn >= 1, dot_turn <= DOT_STEPS))
    def _():
        stored(dot_turn - 1).wait()

    @pl.when(jnp.logical_and(dot_turn >= 0, dot_turn < DOT_STEPS))
    def _():
        columns = pl.ds(pl.multiple_of(dot_turn * WIDE, WIDE), WIDE)
        stage_ref[...] = tn(dconv_ref[:, columns], normed_ref[EDGE:, :]).astype(LOW)
        stored(dot_turn).start()

    pull = g - PULL_AT

    thirds = [slice(i * WIDE, (i + 1) * WIDE) for i in range(DM // WIDE)]
    mixed_out = pltpu.make_async_copy(stage_ref, mixed_ref, one_sem.at[2])

    @pl.when(pull == 0)
    def _():
        for i, at in enumerate(thirds):
            direct_ref[i] = tok_ref[:, at].astype(F32)

    @pl.when(jnp.logical_and(pull >= 0, pull < GATE_STEPS))
    def _():
        for i, at in enumerate(thirds):
            direct_ref[i] += nn(low_ref[...], wgate_ref[:, at])

    @pl.when(pull == GATE_STEPS)
    def _():
        for i, at in enumerate(thirds):
            stage_ref[:, at] = direct_ref[i].astype(LOW)
        mixed_out.start()
        direct_ref[0:PARTS] = jnp.zeros_like(direct_ref[0:PARTS])

    def add_pull(left, weight):
        for b in range(PARTS):
            direct_ref[b, :, :PART] += nn(left, weight[:, b * PART : (b + 1) * PART])

    @pl.when(jnp.logical_and(pull >= GATE_STEPS, pull < 2 * GATE_STEPS))
    def _():
        add_pull(dgate_ref[...], wgate_ref[...])

    @pl.when(jnp.logical_and(pull >= 2 * GATE_STEPS, pull < PULL_STEPS))
    def _():
        k = pull - 2 * GATE_STEPS
        columns = pl.ds(pl.multiple_of(k * WIDE, WIDE), WIDE)
        ids = lax.broadcasted_iota(jnp.int32, (WIDE, DM), 0)
        weight = wconv_ref[...]
        weight = jnp.where(ids < CDIM + HEADS - k * WIDE, weight, jnp.zeros_like(weight))
        add_pull(dconv_ref[:, columns], weight)

    def normed_out(b):
        return pltpu.make_async_copy(direct_ref.at[relative(b), :, 0:PART], dtok_ref.at[:, b * PART : (b + 1) * PART], one_sem.at[3 + b])

    meets = len(reducer.partners)

    def swap(k):
        return pltpu.make_async_remote_copy(src_ref=vsend_ref.at[k], dst_ref=vrecv_ref.at[k], send_sem=vs_sem.at[k], recv_sem=vr_sem.at[k], device_id=reducer.partners[k], device_id_type=MESH)

    @pl.when(g == LAST_AT)
    def _():
        blocks = [slice(b * PART, (b + 1) * PART) for b in range(PARTS)]
        square = jnp.zeros((length, 1), F32)
        cross = jnp.zeros((length, 1), F32)
        for b, at in enumerate(blocks):
            u = tok_ref[:, at].astype(F32)
            square = square + jnp.sum(u * u, axis=1, keepdims=True)
            cross = cross + jnp.sum(direct_ref[relative(b), :, :PART] * gain_ref[0:1, at] * u, axis=1, keepdims=True)
        rate = lax.rsqrt(square * (1.0 / DM) + EPS)
        pulled = rate * rate * rate * (cross * (1.0 / DM))
        for b, at in enumerate(blocks):
            u = tok_ref[:, at].astype(F32)
            there = relative(b)
            d_normed = direct_ref[there, :, :PART]
            vsend_ref[0, 5:6, at] = jnp.sum(d_normed * (u * rate), axis=0, keepdims=True)
            direct_ref[there, :, :PART] = up_ref[:, at].astype(F32) + rate * (d_normed * gain_ref[0:1, at]) - u * pulled
            normed_out(b).start()
        vsend_ref[0, 6:7, :DI] = sums_ref[0:1, :]
        vsend_ref[0, 7:8, :DI] = sums_ref[1:2, :]
        vsend_ref[0, 6:7, DI : DI + LANES] = ends_ref[0][0:1]
        vsend_ref[0, 7:8, DI : DI + LANES] = ends_ref[1][0:1]

        swap(0).start()

    @pl.loop(paced(g), paced(g + 1) + (g // LAST_AT) * (reducer.total - DONE))
    def _(t):
        reducer.step(t)
        for k in range(meets):

            @pl.when(t == DONE + 2 * (k + 1))
            def _(k=k):
                swap(k).wait()
                value = vsend_ref[k] + vrecv_ref[k]
                if k + 1 < meets:
                    vsend_ref[k + 1] = value
                    swap(k + 1).start()
                else:
                    small_ref[...] = value

    @pl.when(g == LAST_AT)
    def _():
        for b in range(PARTS):
            normed_out(b).wait()
        mixed_out.wait()


def rear(proj, x, dy, bc, rb, rt, er, ew, d2, ed, dt, e2, et, states, incoming, taps, skip, heads, met, normed, tokens, upstream, gain, sums, low, dgate, wide_all, conv_all, din, grad_out, grad_gate):
    length = x.shape[0]
    bits, halved = len(seq_bits()), halved_bits()
    hbm = pl.BlockSpec(memory_space=pl.ANY)
    back_block = lambda g: clip((g - BACK_AT) // TURNS, 0, STEPS)
    part_block = lambda g: clip((g - BACK_AT) // TURNS, 0, STEPS - 1)

    def whole(array):
        return pl.BlockSpec(array.shape, lambda g: (0,) * array.ndim, pipeline_mode=pl.Buffered(1))

    shares = []
    for j in range(bits):
        shape = (FEW, max(ROWS >> (j + 1), LEAST), PART)
        shares += [pltpu.VMEM(shape, LOW), pltpu.VMEM(shape, LOW), pltpu.VMEM(shape, F32)]
    dma = pltpu.SemaphoreType.DMA
    stages, meets = 2 + bits + halved, 2 + bits
    return pl.pallas_call(
        rear_kernel,
        grid=(ALL_STEPS,),
        in_specs=[
            pl.BlockSpec((length + EDGE, WIDE), lambda g: (0, back_block(g))),
            pl.BlockSpec((length, WIDE), lambda g: (0, head_block(g))),
            pl.BlockSpec((length, WIDE), lambda g: (0, head_block(g))),
            whole(bc),
            pl.BlockSpec((length, LANES), lambda g: (0, jnp.minimum(g // HALF, STEPS - 1))),
            pl.BlockSpec((GROUP, length), lambda g: (jnp.minimum(g // HALF, STEPS - 1), 0)),
            whole(er),
            whole(ew),
            whole(d2),
            whole(ed),
            whole(dt),
            pl.BlockSpec((2 * LANES, WIDE), lambda g: (0, head_block(g))),
            pl.BlockSpec((WIDE, LANES), lambda g: (part_block(g), 0)),
            pl.BlockSpec((length // BLOCK, NSTATE, WIDE), lambda g: (0, 0, part_block(g))),
            pl.BlockSpec((NSTATE, WIDE), lambda g: (0, part_block(g))),
            whole(taps),
            pl.BlockSpec((8, WIDE), lambda g: (0, part_block(g))),
            whole(heads),
            whole(met),
            whole(normed),
            whole(tokens),
            whole(upstream),
            whole(gain),
            whole(sums),
            pl.BlockSpec((length, WIDE), lambda g: (0, clip(g - PULL_AT, 0, GATE_STEPS - 1))),
            pl.BlockSpec((length, WIDE), lambda g: (0, clip(g - PULL_AT - GATE_STEPS, 0, GATE_STEPS - 1))),
            pl.BlockSpec((WIDE, DM), lambda g: ((clip(g - PULL_AT, 0, 2 * GATE_STEPS - 1) + GATE_STEPS) % (2 * GATE_STEPS), 0)),
            pl.BlockSpec((WIDE, DM), lambda g: (clip(g - PULL_AT - 2 * GATE_STEPS, 0, DOT_STEPS - 1), 0)),
            hbm,
            hbm,
            hbm,
        ],
        out_specs=[hbm, hbm, pl.BlockSpec((8, LONG), lambda g: (0, 0)), hbm, hbm, hbm],
        out_shape=[
            jax.ShapeDtypeStruct((DI + CDIM + HEADS, PART), LOW),
            jax.ShapeDtypeStruct((OUT_PART, DM), LOW),
            jax.ShapeDtypeStruct((8, LONG), F32),
            jax.ShapeDtypeStruct((length, DM), F32),
            jax.ShapeDtypeStruct((length, DM), LOW),
            jax.ShapeDtypeStruct((LONG, DM), LOW),
        ],
        scratch_shapes=[
            pltpu.VMEM((length + EDGE, WIDE), F32),
            pltpu.VMEM((length + EDGE, WIDE), F32),
            pltpu.VMEM((NSTATE, WIDE), F32),
            pltpu.VMEM((STEPS, length, WIDE), F32),
            pltpu.VMEM((length, LONG), LOW),
            pltpu.VMEM((length // BLOCK, BLOCK, BLOCK), F32),
            pltpu.VMEM((length, 2 * NSTATE), F32),
            pltpu.VMEM((length, LANES), F32),
            pltpu.VMEM((length, LANES), F32),
            pltpu.VMEM((length, LANES), F32),
            pltpu.VMEM((length // BLOCK, 8, LANES), F32),
            pltpu.VMEM((LANES, length), F32),
            pltpu.VMEM((WIDE, DM), LOW),
            pltpu.VMEM((16, LONG), LOW),
            pltpu.VMEM((16, LONG), LOW),
            dma((3 + PARTS,)),
            pltpu.VMEM((NSTATE, DI), F32),
            pltpu.VMEM((8, DI), F32),
            pltpu.VMEM((8, DI), F32),
            pltpu.VMEM((NSTATE, DI), F32),
            pltpu.VMEM((NSTATE, DI), LOW),
            pltpu.VMEM((bits, NSTATE, DI), LOW),
            dma((bits, STEPS)),
            dma((bits, STEPS)),
            pltpu.VMEM((meets, 8, LONG), F32),
            pltpu.VMEM((meets, 8, LONG), F32),
            dma((meets,)),
            dma((meets,)),
            pltpu.VMEM((FEW, ROWS, DM), LOW),
            pltpu.VMEM((FEW, ROWS, 2 * PART), LOW),
            pltpu.VMEM((FEW, ROWS, PART), LOW),
            pltpu.VMEM((FEW, ROWS, PART), LOW),
            pltpu.VMEM((FEW, ROWS, PART), F32),
            pltpu.VMEM((SLOTS, ROWS, PART), LOW),
            dma((FEW,)),
            dma((SLOTS,)),
            dma((stages, FEW)),
            dma((stages, FEW)),
        ]
        + shares,
        compiler_params=pltpu.CompilerParams(vmem_limit_bytes=62 << 20, collective_id=2, has_side_effects=True),
        cost_estimate=pl.CostEstimate(flops=200 << 30, bytes_accessed=60 << 20, transcendentals=0),
        name="rear",
    )(proj, x, dy, bc, rb, rt, er, ew, d2, ed, dt, e2, et, states, incoming, taps, skip, heads, met, normed, tokens, upstream, gain, sums, low, dgate, wide_all, conv_all, din, grad_out, grad_gate)


def shards(tokens, norm_gain, in_weight, conv_kernel, conv_bias, step_bias, decay_log, skip_gain, out_gain, out_weight, cotangent):
    length = tokens.shape[1]
    own, upstream = tokens[0], cotangent[0]
    turned = in_weight.T
    gain = norm_gain[None]
    skip = jnp.repeat(skip_gain, HDIM)[None]
    gains = jnp.concatenate([out_gain[None], skip, jnp.zeros((6, DI), F32)], axis=0)
    skip = jnp.broadcast_to(skip, (8, DI))
    lanes = np.arange(DI) // HDIM
    e2 = jnp.asarray((np.arange(2 * LANES)[:, None] % LANES == lanes[None]).astype(LOW))
    et = jnp.asarray((lanes[:, None] == np.arange(LANES)[None]).astype(LOW))

    taps, heads, proj, normed, x, bc, dt, rb, rt, er, ew, d2, ed, state, conv_all = enter(own, gain, conv_kernel, conv_bias[None], step_bias[None], decay_log[None], e2, turned)
    incoming, met, y, states, gate, dno, wide_all = gates(normed, upstream, state, x, bc, rb, rt, er, ew, d2, e2, turned, out_weight)
    low, dy, dgate, sums, din = middle(y, bc, incoming, ed, e2, x, gate, dno, gains, length)

    def product(left, right):
        return jnp.dot(left.T, right, preferred_element_type=F32).astype(LOW)

    grad_out = product(low, upstream)
    grad_gate = product(dgate, normed[EDGE:])
    sum_in, sum_out, small, d_tokens, mixed, _ = rear(proj, x, dy, bc, rb, rt, er, ew, d2, ed, dt, e2, et, states, incoming, taps, skip, heads, met, normed, own, upstream, gain, sums, low, dgate, wide_all, conv_all, din, grad_out, grad_gate)
    return (
        mixed[None],
        d_tokens[None],
        small[5, :DM],
        sum_in.astype(F32).T,
        small[:CONV, :CDIM],
        small[CONV, :CDIM],
        small[6, DI : DI + HEADS],
        small[7, DI : DI + HEADS],
        jnp.sum(small[7, :DI].reshape(HEADS, HDIM), axis=1),
        small[6, :DI],
        sum_out.astype(F32),
    )


def solution(mesh):
    spread = P("wt", "seq", None)
    return jax.shard_map(
        shards,
        mesh=mesh,
        in_specs=(spread, P(), P("wt", None), P(), P(), P(), P(), P(), P(), P("wt", None), spread),
        out_specs=(spread, spread, P(), P("wt", None), P(), P(), P(), P(), P(), P(), P("wt", None)),
        check_vma=False,
    )
```

```python
import jax
import jax.numpy as jnp
import numpy as np
from jax import lax
from jax.experimental import pallas as pl
from jax.experimental.pallas import tpu as pltpu
from jax.sharding import PartitionSpec as P

DI = 3072
HEADS = 48
HDIM = 64
NSTATE = 128
CONV = 4
CDIM = 3328
EDGE = 16
BLOCK = 128
GROUP = 8
WIDE = GROUP * HDIM
STEPS = HEADS // GROUP
LONG = (STEPS + 1) * WIDE
LANES = 128
TILE = 512
FINE = 256
SHORT = 64
AHEAD = 4
LAG = 2
LAST = 320
PARTS = 4
DM = 1536
PART = DM // PARTS
OUT_PART = DI // PARTS
SLOTS = 16
FEW = 4
SLACK = 2
MESH = pl.DeviceIdType.MESH

EPS = 1e-05
F32 = jnp.float32
LOW = jnp.bfloat16


def dot(a, b, ca, cb):
    return lax.dot_general(a, b, (((ca,), (cb,)), ((), ())), preferred_element_type=F32)


def nn(a, b):
    return dot(a, b, 1, 0)


def nt(a, b):
    return dot(a, b, 1, 1)


def tn(a, b):
    return dot(a, b, 0, 0)


def exact(a, b):
    return jnp.dot(a, b, precision=lax.Precision.HIGHEST, preferred_element_type=F32)


def halves(v):
    high = v.astype(LOW)
    return jnp.concatenate([high, (v - high.astype(F32)).astype(LOW)], axis=1)


def softplus(v):
    z = jnp.exp(-jnp.abs(v))
    small = z * (1.0 - z * (0.5 - z * (1.0 / 3.0 - z * 0.25)))
    return jnp.maximum(v, 0.0) + jnp.where(z < 0.01, small, jnp.log(1.0 + z))


def rows_cols(shape):
    return (lax.broadcasted_iota(jnp.int32, shape, 0), lax.broadcasted_iota(jnp.int32, shape, 1))


class Begin:
    def __init__(self, proj_ref, taps_ref, heads_ref, e2_ref, x_ref, bc_ref, dt_ref, rb_ref, rt_ref, er_ref, ew_ref, d2_ref, ed_ref, state_ref, pad_ref, wd_ref):
        self.proj, self.taps, self.heads, self.e2 = proj_ref, taps_ref, heads_ref, e2_ref
        self.x, self.bc, self.dt, self.rb, self.rt = x_ref, bc_ref, dt_ref, rb_ref, rt_ref
        self.er, self.ew, self.d2, self.ed, self.state = er_ref, ew_ref, d2_ref, ed_ref, state_ref
        self.pad, self.wd = pad_ref, wd_ref
        self.length = x_ref.shape[0]

    def convolved(self, first, width):
        self.pad[:, :width] = self.proj[:, first : first + width].astype(F32)
        total = self.taps[CONV : CONV + 1, first : first + WIDE]
        for k in range(CONV):
            at = EDGE - CONV + 1 + k
            total = total + self.taps[k : k + 1, first : first + WIDE] * self.pad[at : at + self.length, :]
        return total * jax.nn.sigmoid(total)

    def sizes(self):
        length = self.length
        self.pad[...] = jnp.zeros_like(self.pad)
        act = self.convolved(DI, CDIM + HEADS - DI)
        self.bc[...] = act[:, : 2 * NSTATE].astype(LOW)
        raw = self.pad[EDGE:, 2 * NSTATE : 2 * NSTATE + LANES]
        used = lax.broadcasted_iota(jnp.int32, raw.shape, 1) < HEADS
        dt = jnp.where(used, softplus(jnp.where(used, raw + self.heads[0:1, :], 0.0)), 0.0)
        self.dt[...] = dt
        self.d2[...] = halves(dt)
        decay = -dt * jnp.exp(self.heads[1:2, :])
        ids, jds = rows_cols((BLOCK, BLOCK))
        lower = (ids >= jds).astype(F32)
        before = jnp.zeros((1, LANES), F32)
        whole = []
        for c in range(length // BLOCK):
            at = slice(c * BLOCK, (c + 1) * BLOCK)
            run = exact(lower, decay[at])
            last = run[BLOCK - 1 : BLOCK]
            for j in range(STEPS):
                turned = jnp.concatenate([run[:, GROUP * j :], run[:, : GROUP * j]], axis=1) if j else run
                self.rb[at, j * LANES : (j + 1) * LANES] = turned
            self.rt[:, at] = run.T
            self.er[at, :] = halves(jnp.exp(run))
            self.ew[at, :] = halves(jnp.exp(last - run))
            whole.append(run + before)
            self.ed[at, :] = halves(jnp.exp(run + before))
            before = before + last
        for c in range(length // BLOCK):
            at = slice(c * BLOCK, (c + 1) * BLOCK)
            self.wd[at, :] = halves(jnp.exp(before - whole[c]) * dt[at])

    def block(self, j):
        at = slice(j * WIDE, (j + 1) * WIDE)
        x = self.convolved(j * WIDE, WIDE).astype(LOW)
        self.x[:, at] = x
        e2 = self.e2[:, at]
        weighed = (x.astype(F32) * nn(self.wd[...], e2)).astype(LOW)
        self.state[0:NSTATE, at] = tn(self.bc[:, :NSTATE], weighed).astype(LOW)
        decay = nn(self.ed[self.length - 16 : self.length, :], e2)[15:16, :]
        high = decay.astype(LOW).astype(F32)
        ids = lax.broadcasted_iota(jnp.int32, (16, WIDE), 0)
        self.state[NSTATE : NSTATE + 16, at] = jnp.where(ids == 0, high, jnp.where(ids == 1, decay - high, 0.0)).astype(LOW)


class Stages:
    def __init__(self, ref, sem):
        self.ref, self.sem, self.count = ref, sem, ref.shape[0]
        self.flying = [None] * self.count
        self.turn = 0

    def put(self, value, target):
        at = self.turn % self.count
        if self.flying[at] is not None:
            self.flying[at].wait()
        self.ref[at] = value
        self.flying[at] = pltpu.make_async_copy(self.ref.at[at], target, self.sem.at[at])
        self.flying[at].start()
        self.turn += 1

    def rest(self):
        for one in self.flying:
            if one is not None:
                one.wait()


class Inside:
    def __init__(self, x_ref, bc_ref, rb_ref, rt_ref, er_ref, ew_ref, d2_ref, e2_ref, held_ref, y_out, states_out, ys, states):
        self.x, self.bc, self.rb, self.rt = x_ref, bc_ref, rb_ref, rt_ref
        self.er, self.ew, self.d2, self.e2, self.held = er_ref, ew_ref, d2_ref, e2_ref, held_ref
        self.y_out, self.states_out, self.ys, self.states = y_out, states_out, ys, states
        self.blocks = x_ref.shape[0] // BLOCK

    def turn(self, at):
        if at < STEPS * self.blocks:
            self.block(at // self.blocks, at % self.blocks)

    def block(self, j, c):
        at, own = slice(c * BLOCK, (c + 1) * BLOCK), slice(j * WIDE, (j + 1) * WIDE)
        ids, jds = rows_cols((BLOCK, BLOCK))
        left = lax.broadcasted_iota(jnp.int32, (BLOCK, LANES), 1) < HDIM
        input_mat, output_mat = self.bc[at, :NSTATE], self.bc[at, NSTATE:]
        e2 = self.e2[:, own]
        grow, leave = nn(self.er[at, :], e2), nn(self.ew[at, :], e2)
        x = self.x[at, own].astype(F32) * nn(self.d2[at, :], e2)
        scores = jnp.where(ids >= jds, nt(output_mat, input_mat), 0.0)
        held = self.held[...] if c else jnp.zeros_like(self.held)
        self.states.put(held.astype(LOW), self.states_out.at[c, :, own])
        carried = grow * nn(output_mat, held.astype(LOW))
        parts = []
        for pair in range(GROUP // 2):
            lanes = slice(pair * LANES, (pair + 1) * LANES)
            piece = x[:, lanes]
            mixed = []
            for head in (2 * pair, 2 * pair + 1):
                column = self.rb[at, j * LANES + head : j * LANES + head + 1]
                spread = column - self.rt[j * GROUP + head : j * GROUP + head + 1, at]
                mixed.append((scores * jnp.exp(jnp.minimum(spread, 0.0))).astype(LOW))
            both = jnp.concatenate([jnp.where(left, piece, 0.0), jnp.where(left, 0.0, piece)], axis=0)
            parts.append(nn(jnp.concatenate(mixed, axis=1), both.astype(LOW)) + carried[:, lanes])
        self.ys.put(jnp.concatenate(parts, axis=1), self.y_out.at[at, own])
        self.held[...] = held * grow[BLOCK - 1 : BLOCK, :] + tn(input_mat, (x * leave).astype(LOW))


def middle_kernel(y_ref, bc_ref, in_ref, ed_ref, e2_ref, x_ref, gate_ref, dno_ref, gains_ref, low_ref, dy_ref, dgate_ref, sums_ref, din_ref, out_ref, gated_ref):
    @pl.when(pl.program_id(0) == 0)
    def _():
        sums_ref[...] = jnp.zeros_like(sums_ref)
        din_ref[...] = jnp.zeros_like(din_ref)

    output_mat = bc_ref[:, NSTATE:]
    part = DI // PARTS
    tiles = []
    for j in range(PARTS):
        there = relative(j)
        tiles.append((slice(j * part, (j + 1) * part), pl.ds(pl.multiple_of(there * part, LANES), part)))
    square = jnp.zeros((BLOCK, 1), F32)
    cross = jnp.zeros((BLOCK, 1), F32)
    for at, there in tiles:
        far = nn(ed_ref[...], e2_ref[:, at]) * nn(output_mat, in_ref[:, at])
        out = y_ref[:, at] + far + gains_ref[1:2, at] * x_ref[:, at].astype(F32)
        gate = gate_ref[:, at].astype(F32)
        gated = out * gate * jax.nn.sigmoid(gate)
        out_ref[:, at] = out
        gated_ref[:, at] = gated
        square = square + jnp.sum(gated * gated, axis=1, keepdims=True)
        cross = cross + jnp.sum(gated * (dno_ref[:, there] * gains_ref[0:1, at]), axis=1, keepdims=True)
    scale = lax.rsqrt(square * (1.0 / DI) + EPS)
    pull = scale * scale * scale * (cross * (1.0 / DI))
    for at, there in tiles:
        gate = gate_ref[:, at].astype(F32)
        gated, out, gain = gated_ref[:, at], out_ref[:, at], gains_ref[0:1, at]
        shape = jax.nn.sigmoid(gate)
        unit = gated * scale
        low_ref[:, there] = (unit * gain).astype(LOW)
        dno = dno_ref[:, there]
        dgated = scale * (dno * gain) - gated * pull
        dy = dgated * (gate * shape)
        dy_ref[:, at] = dy.astype(LOW)
        dgate_ref[:, at] = (dgated * out * (shape * (1.0 + gate * (1.0 - shape)))).astype(LOW)
        sums_ref[0:1, at] += jnp.sum(dno * unit, axis=0, keepdims=True)
        sums_ref[1:2, at] += jnp.sum(dy * x_ref[:, at].astype(F32), axis=0, keepdims=True)
        din_ref[:, at] += tn(output_mat, (dy * nn(ed_ref[...], e2_ref[:, at])).astype(LOW))


def middle(y, bc, incoming, ed, e2, x, gate, dno, gains, length):
    rows = lambda c: (c, 0)
    fixed = lambda c: (0, 0)
    return pl.pallas_call(
        middle_kernel,
        grid=(length // BLOCK,),
        in_specs=[
            pl.BlockSpec((BLOCK, DI), rows),
            pl.BlockSpec((BLOCK, 2 * NSTATE), rows),
            pl.BlockSpec((NSTATE, DI), fixed),
            pl.BlockSpec((BLOCK, 2 * LANES), rows),
            pl.BlockSpec((2 * LANES, DI), fixed),
            pl.BlockSpec((BLOCK, DI), rows),
            pl.BlockSpec((BLOCK, DI), rows),
            pl.BlockSpec((BLOCK, DI), rows),
            pl.BlockSpec((8, DI), fixed),
        ],
        out_specs=[
            pl.BlockSpec((BLOCK, DI), rows),
            pl.BlockSpec((BLOCK, DI), rows),
            pl.BlockSpec((BLOCK, DI), rows),
            pl.BlockSpec((8, DI), fixed),
            pl.BlockSpec((NSTATE, DI), fixed),
        ],
        out_shape=[
            jax.ShapeDtypeStruct((length, DI), LOW),
            jax.ShapeDtypeStruct((length, DI), LOW),
            jax.ShapeDtypeStruct((length, DI), LOW),
            jax.ShapeDtypeStruct((8, DI), F32),
            jax.ShapeDtypeStruct((NSTATE, DI), F32),
        ],
        scratch_shapes=[pltpu.VMEM((BLOCK, DI), F32), pltpu.VMEM((BLOCK, DI), F32)],
        compiler_params=pltpu.CompilerParams(vmem_limit_bytes=48 << 20),
        cost_estimate=pl.CostEstimate(flops=12 << 30, bytes_accessed=32 << 20, transcendentals=4 << 20),
        name="middle",
    )(y, bc, incoming, ed, e2, x, gate, dno, gains)


def spot():
    wt, seq = lax.axis_index("wt"), lax.axis_index("seq")
    return wt // 2, wt % 2, seq % 2


def relative(block):
    x, core, _ = spot()
    high, low = block // 2, block % 2
    return 2 * (core + low - 2 * core * low) + (x + high - 2 * x * high)


def across_bit(axis, bit):
    index = lax.axis_index(axis)
    return {axis: index + bit - 2 * bit * ((index // bit) % 2)}


def greet(devices):
    barrier = pltpu.get_barrier_semaphore()
    for device in devices:
        pl.semaphore_signal(barrier, inc=1, device_id=device, device_id_type=MESH)
    pl.semaphore_wait(barrier, len(devices))


class Piece:
    def __init__(self, source, near, mine, pair, twin, half, sems, at):
        bit = 1 + at % 2
        part = pl.multiple_of((lax.axis_index("seq") // bit) % 2 * half, 16)
        own, xs, xr, ys, yr, ts, tr, keep = sems
        rows = lambda ref: ref.at[pl.ds(part, half), :]
        self.own = pltpu.make_async_copy(source, mine, own.at[at])
        self.x = self.remote(rows(source), rows(near), xs.at[at], xr.at[at], across_bit("wt", 2))
        self.y = self.remote(rows(near), rows(near), ys.at[at], yr.at[at], across_bit("seq", bit))
        self.twin = self.remote(pair, twin, ts.at[at], tr.at[at], across_bit("wt", 1))

    def remote(self, source, target, send, recv, device):
        return pltpu.make_async_remote_copy(src_ref=source, dst_ref=target, send_sem=send, recv_sem=recv, device_id=device, device_id_type=MESH)


def gather_sems(count):
    return [pltpu.SemaphoreType.DMA((count,)) for _ in range(8)]


def enter_kernel(tok_ref, gain_ref, kernel_ref, bias_ref, step_ref, log_ref, e2_ref, w_ref, taps_ref, heads_ref, proj_ref, normed_ref, x_ref, bc_ref, dt_ref, rb_ref, rt_ref, er_ref, ew_ref, d2_ref, ed_ref, state_ref, all_ref, wide_ref, last_ref, edge_ref, pad_ref, wd_ref, edge_sem, *sems):
    length = tok_ref.shape[0]
    begin = Begin(proj_ref, taps_ref, heads_ref, e2_ref, x_ref, bc_ref, dt_ref, rb_ref, rt_ref, er_ref, ew_ref, d2_ref, ed_ref, state_ref, pad_ref, wd_ref)
    seq, peers = lax.axis_index("seq"), lax.axis_size("seq")
    following, previous = {"seq": lax.rem(seq + 1, peers)}, {"seq": lax.rem(seq + peers - 1, peers)}
    greet([across_bit("wt", 1), across_bit("wt", 2), across_bit("seq", 1), across_bit("seq", 2), following, previous])
    edge = pltpu.make_async_remote_copy(src_ref=tok_ref.at[length - EDGE : length, :], dst_ref=edge_ref, send_sem=edge_sem.at[0], recv_sem=edge_sem.at[1], device_id=following, device_id_type=MESH)
    edge.start()
    count = CDIM // TILE
    pieces, products, keeps = [], [], []

    def add(target, first, rows):
        pieces.append(Piece(w_ref.at[pl.ds(first, rows), :], target.at[:, PART : 2 * PART], target.at[:, :PART], target.at[:, : 2 * PART], target.at[:, 2 * PART :], rows // 2, sems, len(pieces)))
        products.append(None)

    def multiply(target, columns, skip, then):
        keep = pltpu.make_async_copy(target.at[skip:, :], all_ref.at[columns, :], sems[-1].at[len(keeps)])
        keeps.append(keep)

        def product():
            keep.start()
            proj_ref[:, columns] = nt(normed_ref[...], target[skip:, :]).astype(LOW)
            then()

        products[-1] = product

    add(last_ref, DI + CDIM + HEADS - LAST, LAST)
    multiply(last_ref, slice(count * TILE, CDIM + HEADS), LAST - (CDIM + HEADS - count * TILE), begin.sizes)
    for c in range(count):
        for first in range(c * TILE, (c + 1) * TILE, FINE):
            add(wide_ref.at[first : first + FINE, :], DI + first, FINE)
        multiply(wide_ref.at[c * TILE : (c + 1) * TILE, :], slice(c * TILE, (c + 1) * TILE), 0, lambda c=c: begin.block(c))
    for piece in pieces:
        piece.own.start()
    for piece in pieces[:AHEAD]:
        piece.x.start()

    def norm(v):
        v = v.astype(F32)
        return (v * lax.rsqrt(jnp.mean(v * v, axis=-1, keepdims=True) + EPS) * gain_ref[0:1, :]).astype(LOW)

    def place(at, v):
        for b in range(PARTS):
            normed_ref[at, pl.ds(pl.multiple_of(relative(b) * PART, LANES), PART)] = v[:, b * PART : (b + 1) * PART]

    taps_ref[...] = jnp.zeros_like(taps_ref)
    taps_ref[0:CONV, :CDIM] = kernel_ref[...]
    taps_ref[CONV : CONV + 1, :CDIM] = bias_ref[...]
    heads_ref[...] = jnp.zeros_like(heads_ref)
    heads_ref[0:1, :HEADS] = step_ref[...]
    heads_ref[1:2, :HEADS] = log_ref[...]
    place(slice(EDGE, EDGE + length), norm(tok_ref[...]))
    edge.wait()
    place(slice(0, EDGE), norm(jnp.where(seq == 0, 0.0, edge_ref[...].astype(F32))))
    travel_on(pieces, products)
    for keep in keeps:
        keep.wait()


def travel_on(pieces, products, ahead=AHEAD, between=None):
    count = len(pieces)
    for t in range(count + 2 * LAG):
        if t < count:
            pieces[t].x.wait_recv()
            pieces[t].y.start()
            if t + ahead < count:
                pieces[t + ahead].x.start()
        if 0 <= t - LAG < count:
            pieces[t - LAG].y.wait_recv()
            pieces[t - LAG].own.wait()
            pieces[t - LAG].twin.start()
        if 0 <= t - 2 * LAG < count:
            pieces[t - 2 * LAG].twin.wait_recv()
            if products[t - 2 * LAG] is not None:
                products[t - 2 * LAG]()
        if between is not None:
            between(t)
    for piece in pieces:
        piece.x.wait_send()
        piece.y.wait_send()
        piece.twin.wait_send()


def enter(tokens, gain, conv_kernel, conv_bias, step_bias, decay_log, e2, weight):
    length, columns = tokens.shape[0], CDIM + HEADS
    vmem, hbm = pl.BlockSpec(memory_space=pltpu.VMEM), pl.BlockSpec(memory_space=pl.ANY)
    shapes = [
        ((8, LONG), F32),
        ((8, LANES), F32),
        ((length + EDGE, columns), LOW),
        ((length + EDGE, DM), LOW),
        ((length, DI), LOW),
        ((length, 2 * NSTATE), LOW),
        ((length, LANES), F32),
        ((length, LANES * STEPS), F32),
        ((LANES, length), F32),
        ((length, 2 * LANES), LOW),
        ((length, 2 * LANES), LOW),
        ((length, 2 * LANES), LOW),
        ((length, 2 * LANES), LOW),
        ((NSTATE + 16, DI), LOW),
        ((columns, DM), LOW),
    ]
    return pl.pallas_call(
        enter_kernel,
        in_specs=[vmem] * 7 + [hbm],
        out_specs=[vmem] * (len(shapes) - 1) + [hbm],
        out_shape=[jax.ShapeDtypeStruct(shape, kind) for shape, kind in shapes],
        scratch_shapes=[
            pltpu.VMEM((CDIM // TILE * TILE, DM), LOW),
            pltpu.VMEM((LAST, DM), LOW),
            pltpu.VMEM((EDGE, DM), LOW),
            pltpu.VMEM((length + EDGE, WIDE), F32),
            pltpu.VMEM((length, 2 * LANES), LOW),
            pltpu.SemaphoreType.DMA((2,)),
        ]
        + gather_sems(CDIM // TILE * (TILE // FINE) + 1),
        compiler_params=pltpu.CompilerParams(vmem_limit_bytes=56 << 20, collective_id=0, has_side_effects=True),
        cost_estimate=pl.CostEstimate(flops=40 << 30, bytes_accessed=30 << 20, transcendentals=0),
        name="enter",
    )(tokens, gain, conv_kernel, conv_bias, step_bias, decay_log, e2, weight)


class Passing:
    def __init__(self, later, total, factor, reach, held, send, recv, met, send_sem, recv_sem):
        self.later, self.total, self.factor, self.reach, self.held = later, total, factor, reach, held
        self.send, self.recv, self.met, self.send_sem, self.recv_sem = send, recv, met, send_sem, recv_sem
        self.bits = seq_bits()

    def columns(self, j):
        return pl.ds(pl.multiple_of(j * WIDE, WIDE), WIDE)

    def copy(self, k, j):
        at = self.columns(j)
        return pltpu.make_async_remote_copy(src_ref=self.send.at[:, at], dst_ref=self.recv.at[k, :, at], send_sem=self.send_sem.at[k, j], recv_sem=self.recv_sem.at[k, j], device_id=across_bit("seq", self.bits[k]), device_id_type=MESH)

    def start(self, k, j):
        at = self.columns(j)
        self.send[0:NSTATE, at] = self.total[:, at].astype(LOW)
        if not self.later:
            factor = self.factor[0:1, at]
            high = factor.astype(LOW).astype(F32)
            ids = lax.broadcasted_iota(jnp.int32, (16, WIDE), 0)
            self.send[NSTATE : NSTATE + 16, at] = jnp.where(ids == 0, high, jnp.where(ids == 1, factor - high, 0.0)).astype(LOW)
        self.copy(k, j).start()

    def finish(self, k, j):
        self.copy(k, j).wait()
        at = self.columns(j)
        bit = self.bits[k]
        second = (lax.axis_index("seq") // bit) % 2
        takes = second == (0 if self.later else 1)
        other = self.recv[k, 0:NSTATE, at].astype(F32)
        if self.later:
            met = self.met[k : k + 1, at]
        else:
            rows = self.recv[k, NSTATE : NSTATE + 16, at].astype(F32)
            met = rows[0:1] + rows[1:2]
            self.met[k : k + 1, at] = met
        total, factor, reach = self.total[:, at], self.factor[0:1, at], self.reach[0:1, at]
        self.held[:, at] = self.held[:, at] + jnp.where(takes, reach, 0.0) * other
        self.reach[0:1, at] = jnp.where(takes, reach * met, reach)
        if k + 1 < len(self.bits):
            self.total[:, at] = jnp.where(takes, factor, 1.0) * other + jnp.where(takes, 1.0, met) * total
            self.factor[0:1, at] = factor * met
            self.start(k + 1, j)

    def due(self, k, j):
        last = len(self.bits) - 1
        return 4 + 4 * k + 3 * j if k < last else 5 + 4 * last + 3 * j

    def step(self, t):
        for k in range(len(self.bits)):
            for j in range(STEPS):
                if t == self.due(k, j):
                    self.finish(k, j)

    def rest(self, t):
        for late in range(t, self.due(len(self.bits) - 1, STEPS - 1) + 1):
            self.step(late)


def gates_kernel(normed_ref, up_ref, state_ref, x_ref, bc_ref, rb_ref, rt_ref, er_ref, ew_ref, d2_ref, e2_ref, w_ref, o_ref, incoming_ref, met_ref, y_out, states_out, gate_out, dno_out, wall_ref, wide_ref, deep_ref, total_ref, factor_ref, reach_ref, held_ref, send_ref, recv_ref, own_ref, y_ref, states_ref, gate_ref, dno_ref, ss_sem, sr_sem, deep_sem, stage_sem, *sems):
    stages = [Stages(ref, stage_sem.at[i]) for i, ref in enumerate((y_ref, states_ref, gate_ref, dno_ref))]
    local = Inside(x_ref, bc_ref, rb_ref, rt_ref, er_ref, ew_ref, d2_ref, e2_ref, own_ref, y_out, states_out, stages[0], stages[1])
    greet([across_bit("wt", 1), across_bit("wt", 2)] + [across_bit("seq", bit) for bit in seq_bits()])
    passing = Passing(False, total_ref, factor_ref, reach_ref, held_ref, send_ref, recv_ref, met_ref, ss_sem, sr_sem)
    total_ref[...] = state_ref[0:NSTATE, :].astype(F32)
    rows = state_ref[NSTATE : NSTATE + 16, :].astype(F32)
    factor_ref[0:1, :] = rows[0:1] + rows[1:2]
    reach_ref[...] = jnp.ones_like(reach_ref)
    held_ref[...] = jnp.zeros_like(held_ref)
    met_ref[...] = jnp.zeros_like(met_ref)
    met_ref[7:8, :] = factor_ref[0:1, :]
    for j in range(STEPS):
        passing.start(0, j)
    pieces, products, keeps = [], [], []

    for c in range(DI // FINE):
        rows = slice(c * FINE, (c + 1) * FINE)
        target = wide_ref.at[rows, :]
        pieces.append(Piece(w_ref.at[rows, :], target.at[:, PART : 2 * PART], target.at[:, :PART], target.at[:, : 2 * PART], target.at[:, 2 * PART :], FINE // 2, sems, len(pieces)))
        keeps.append(pltpu.make_async_copy(target, wall_ref.at[rows, :], sems[-1].at[c]))

        def product(rows=rows, keep=keeps[-1]):
            keep.start()
            stages[2].put(nt(normed_ref[EDGE:, :], wide_ref[rows, :]).astype(LOW), gate_out.at[:, rows])

        products.append(product)

    for c in range(OUT_PART // SHORT):
        rows = slice(c * SHORT, (c + 1) * SHORT)
        pieces.append(Piece(o_ref.at[rows, :], deep_ref.at[1, rows, :], deep_ref.at[0, rows, :], deep_ref.at[0:2, rows, :], deep_ref.at[2:4, rows, :], SHORT // 2, sems, len(pieces)))
        products.append(None)
        if (c + 1) * SHORT % FINE == 0:
            first = (c + 1) * SHORT - FINE
            mine = [pltpu.make_async_copy(deep_ref.at[b, first : first + FINE, :], wall_ref.at[pl.ds(DI + b * OUT_PART + first, FINE), :], deep_sem.at[first // FINE, b]) for b in range(PARTS)]
            keeps.extend(mine)

            def product(first=first, mine=mine):
                for b in range(PARTS):
                    mine[b].start()
                    at = b * OUT_PART + first
                    stages[3].put(nt(up_ref[...], deep_ref[b, first : first + FINE, :]), dno_out.at[:, at : at + FINE])

            products[-1] = product

    for piece in pieces:
        piece.own.start()
    for piece in pieces[: 2 * AHEAD - 2]:
        piece.x.start()

    def between(t):
        passing.step(t)
        local.turn(t)

    travel_on(pieces, products, ahead=2 * AHEAD - 2, between=between)
    for t in range(len(pieces) + 2 * LAG, STEPS * local.blocks):
        local.turn(t)
    passing.rest(len(pieces) + 2 * LAG)
    for stage in stages:
        stage.rest()
    incoming_ref[...] = held_ref[...].astype(LOW)
    for keep in keeps:
        keep.wait()


def gates(normed, upstream, state, x, bc, rb, rt, er, ew, d2, e2, weight, out_weight):
    length = upstream.shape[0]
    bits = len(seq_bits())
    vmem, hbm = pl.BlockSpec(memory_space=pltpu.VMEM), pl.BlockSpec(memory_space=pl.ANY)
    dma = pltpu.SemaphoreType.DMA
    return pl.pallas_call(
        gates_kernel,
        in_specs=[vmem] * 11 + [hbm, hbm],
        out_specs=[vmem, vmem] + [hbm] * 5,
        out_shape=[
            jax.ShapeDtypeStruct((NSTATE, DI), LOW),
            jax.ShapeDtypeStruct((8, DI), F32),
            jax.ShapeDtypeStruct((length, DI), F32),
            jax.ShapeDtypeStruct((length // BLOCK, NSTATE, DI), LOW),
            jax.ShapeDtypeStruct((length, DI), LOW),
            jax.ShapeDtypeStruct((length, DI), F32),
            jax.ShapeDtypeStruct((2 * DI, DM), LOW),
        ],
        scratch_shapes=[
            pltpu.VMEM((DI, DM), LOW),
            pltpu.VMEM((PARTS, OUT_PART, DM), LOW),
            pltpu.VMEM((NSTATE, DI), F32),
            pltpu.VMEM((8, DI), F32),
            pltpu.VMEM((8, DI), F32),
            pltpu.VMEM((NSTATE, DI), F32),
            pltpu.VMEM((NSTATE + 16, DI), LOW),
            pltpu.VMEM((bits, NSTATE + 16, DI), LOW),
            pltpu.VMEM((NSTATE, WIDE), F32),
            pltpu.VMEM((2, BLOCK, WIDE), F32),
            pltpu.VMEM((2, NSTATE, WIDE), LOW),
            pltpu.VMEM((2, length, FINE), LOW),
            pltpu.VMEM((2, length, FINE), F32),
            dma((bits, STEPS)),
            dma((bits, STEPS)),
            dma((OUT_PART // FINE, PARTS)),
            dma((4, 2)),
        ]
        + gather_sems(DI // FINE + OUT_PART // SHORT),
        compiler_params=pltpu.CompilerParams(vmem_limit_bytes=58 << 20, collective_id=1, has_side_effects=True),
        cost_estimate=pl.CostEstimate(flops=50 << 30, bytes_accessed=50 << 20, transcendentals=0),
        name="gates",
    )(normed, upstream, state, x, bc, rb, rt, er, ew, d2, e2, weight, out_weight)


def seq_bits():
    bits, bit = [], 1
    while bit < lax.axis_size("seq"):
        bits.append(bit)
        bit *= 2
    return bits


ROWS = 128
LEAST = 16


class Reducer:
    def __init__(self, out, gate, conv, din, dout, held, core, sx, rx, near, res, load_sem, keep_sem, send_sem, recv_sem, parts):
        self.out, self.gate, self.conv, self.din, self.dout = out, gate, conv, din, dout
        self.held, self.core, self.sx, self.rx, self.near, self.res = held, core, sx, rx, near, res
        self.load_sem, self.keep_sem, self.send_sem, self.recv_sem, self.parts = load_sem, keep_sem, send_sem, recv_sem, parts
        bits = seq_bits()
        seq = lax.axis_index("seq")
        self.steps = len(bits)
        self.halved = halved_bits()
        self.partners = [across_bit("wt", 1), across_bit("wt", 2)] + [across_bit("seq", bit) for bit in bits]
        self.second = [(seq // bit) % 2 for bit in bits]
        self.bases, self.sizes = [0], [ROWS]
        for bit in bits[: self.halved]:
            size = self.sizes[-1] // 2
            self.bases.append(self.bases[-1] + ((seq // bit) % 2) * size)
            self.sizes.append(size)
        self.stages = 2 + self.steps + self.halved
        self.out_count = PARTS * (OUT_PART // ROWS)
        self.gate_count = DI // ROWS
        self.columns = CDIM + HEADS
        self.count = self.out_count + self.gate_count + -(-self.columns // ROWS)
        self.total = self.count + SLACK * self.stages + 1

    def rows_at(self, j):
        return pl.ds(pl.multiple_of(self.bases[j], LEAST), self.sizes[j])

    def kinds(self, c, act):
        first_gate, first_conv = self.out_count, self.out_count + self.gate_count

        @pl.when(c < first_gate)
        def _():
            first = pl.multiple_of((c // PARTS) * ROWS, 16)
            columns = pl.ds(pl.multiple_of((c % PARTS) * PART, LANES), PART)
            act([self.out.at[pl.ds(b * OUT_PART + first, ROWS), columns] for b in range(PARTS)], lambda: self.dout.at[pl.ds(first, ROWS), columns])

        @pl.when(jnp.logical_and(c >= first_gate, c < first_conv))
        def _():
            first = pl.multiple_of((c - first_gate) * ROWS, 16)
            act([self.gate.at[pl.ds(first, ROWS), :]], lambda: self.din.at[pl.ds(first, ROWS), :])

        @pl.when(c >= first_conv)
        def _():
            first = pl.multiple_of(jnp.minimum((c - first_conv) * ROWS, self.columns - ROWS), 16)
            act([self.conv.at[pl.ds(first, ROWS), :]], lambda: self.din.at[pl.ds(DI + first, ROWS), :])

    def load(self, c):
        few = lax.rem(c, FEW)

        def act(sources, target):
            width = DM // len(sources)
            for b, source in enumerate(sources):
                pltpu.make_async_copy(source, self.held.at[few, :, b * width : (b + 1) * width], self.load_sem.at[few]).start()

        self.kinds(c, act)

    def exchange(self, s, slot, few):
        if s == 0:
            source, target = self.held.at[few, :, 2 * PART :], self.core.at[few]
        elif s == 1:
            source, target = self.sx.at[few], self.rx.at[few]
        elif s < 2 + self.steps:
            source, target = self.parts[3 * (s - 2)].at[few], self.parts[3 * (s - 2) + 1].at[few]
        else:
            j = self.stages - 1 - s
            source = target = self.res.at[slot, self.rows_at(j + 1), :]
        partner = self.partners[s] if s < 2 + self.steps else self.partners[2 + self.stages - 1 - s]
        return pltpu.make_async_remote_copy(src_ref=source, dst_ref=target, send_sem=self.send_sem.at[s, few], recv_sem=self.recv_sem.at[s, few], device_id=partner, device_id_type=MESH)

    def loaded(self, few):
        pltpu.make_async_copy(self.gate.at[0:ROWS, :], self.held.at[few], self.load_sem.at[few]).wait()

    def kept(self, slot):
        return pltpu.make_async_copy(self.res.at[slot], self.din.at[0:ROWS, :], self.keep_sem.at[slot])

    def combine(self, s, slot, few):
        if s == 0:
            self.near[few] = self.held[few, :, :PART].astype(F32) + self.core[few, :, :PART].astype(F32)
            self.sx[few] = (self.held[few, :, PART : 2 * PART].astype(F32) + self.core[few, :, PART:].astype(F32)).astype(LOW)
        elif s == 1:
            self.lay(self.near[few] + self.rx[few].astype(F32), 0, slot, few)
        elif s < 2 + self.steps:
            j = s - 2
            mine = self.parts[3 * j + 2][few] if j < self.halved else self.parts[3 * j][few].astype(F32)
            self.lay(mine + self.parts[3 * j + 1][few].astype(F32), j + 1, slot, few)

    def lay(self, value, j, slot, few):
        if j == self.steps:
            self.res[slot, self.rows_at(self.halved), :] = value.astype(LOW)
        elif j < self.halved:
            size = self.sizes[j + 1]
            low, high = value[:size], value[size:]
            second = self.second[j] == 1
            self.parts[3 * j][few] = jnp.where(second, low, high).astype(LOW)
            self.parts[3 * j + 2][few] = jnp.where(second, high, low)
        else:
            self.parts[3 * j][few] = value.astype(LOW)

    def write(self, c, slot):
        self.kinds(c, lambda sources, target: pltpu.make_async_copy(self.res.at[slot], target(), self.keep_sem.at[slot]).start())

    def step(self, t):
        steady = jnp.logical_and(t > SLACK * self.stages, t < self.count)

        @pl.when(steady)
        def _():
            slots = [(lax.rem(t - SLACK * s, SLOTS), lax.rem(t - SLACK * s, FEW)) for s in range(self.stages + 1)]
            self.kept(lax.rem(t - SLACK * self.stages - 1, SLOTS)).wait()
            for s in range(self.stages, 0, -1):
                self.exchange(s - 1, *slots[s]).wait()
            self.loaded(slots[0][1])
            for s in range(self.stages, 0, -1):
                self.combine(s - 1, *slots[s])
            for s in range(1, self.stages):
                self.exchange(s, *slots[s]).start()
            self.exchange(0, *slots[0]).start()
            self.write(t - SLACK * self.stages, slots[self.stages][0])

        @pl.when(jnp.logical_not(steady))
        def _():
            c = t - SLACK * self.stages - 1

            @pl.when(jnp.logical_and(c >= 0, c < self.count))
            def _():
                self.kept(lax.rem(c, SLOTS)).wait()

            for s in range(self.stages, -1, -1):
                c = t - SLACK * s

                @pl.when(jnp.logical_and(c >= 0, c < self.count))
                def _(c=c, s=s):
                    slot, few = lax.rem(c, SLOTS), lax.rem(c, FEW)
                    if s > 0:
                        self.exchange(s - 1, slot, few).wait()
                        self.combine(s - 1, slot, few)
                    else:
                        self.loaded(few)
                    if s < self.stages:
                        self.exchange(s, slot, few).start()
                    else:
                        self.write(c, slot)

        @pl.when(t + 1 < self.count)
        def _():
            self.load(t + 1)


def halved_bits():
    count, rows = 0, ROWS
    while count < len(seq_bits()) and rows > LEAST:
        count, rows = count + 1, rows // 2
    return count


BLOCKS = 4
PER = 2
HALF = BLOCKS // PER
TURNS = HALF + 1
FILL_STEPS, NEAR_STEPS, BACK_STEPS, EDGE_STEPS, GATE_STEPS = STEPS, STEPS * HALF, STEPS * TURNS + 1, 1, STEPS
NEAR_AT = FILL_STEPS
BACK_AT = NEAR_AT + NEAR_STEPS
EDGE_AT = BACK_AT + BACK_STEPS
PULL_AT = EDGE_AT + EDGE_STEPS
DOT_STEPS = STEPS + 1
PULL_STEPS = 2 * GATE_STEPS + DOT_STEPS
LAST_AT = PULL_AT + PULL_STEPS
ALL_STEPS = LAST_AT + 1
PACE = ((1, FILL_STEPS - 1, 9), (NEAR_AT, NEAR_STEPS, 17), (BACK_AT, BACK_STEPS, 26), (EDGE_AT, EDGE_STEPS, 3), (PULL_AT, PULL_STEPS, 24))
DONE = sum(turns for _, _, turns in PACE)


def clip(v, low, high):
    return jnp.minimum(jnp.maximum(v, low), high)


def paced(g):
    done = 0
    for first, steps, turns in PACE:
        done = done + (turns * clip(g - first, 0, steps)) // steps
    return done


def head_block(g):
    near = clip(g - NEAR_AT, 0, NEAR_STEPS) // HALF
    over = near // STEPS
    return near * (1 - over) + over * clip((g - BACK_AT) // TURNS, 0, STEPS - 1)


def gate_block(g):
    over = clip(g - FILL_STEPS + 1, 0, 1)
    return jnp.minimum(g, FILL_STEPS - 1) * (1 - over) + over * clip(g - PULL_AT - GATE_STEPS, 0, GATE_STEPS - 1)


def near_block_at(g):
    return jnp.minimum(clip(g - NEAR_AT, 0, NEAR_STEPS) // HALF, STEPS - 1)


def rear_kernel(pc_ref, x_ref, dy_ref, bc_ref, rb_ref, rt_ref, er_ref, ew_ref, d2_ref, ed_ref, dt_ref, e2_ref, et_ref, states_ref, in_ref, taps_ref, skip_ref, heads_ref, met_ref, normed_ref, tok_ref, up_ref, gain_ref, sums_ref, low0_ref, low1_ref, low2_ref, low3_ref, low_ref, dgate_ref, wgate_ref, wconv_ref, din_ref, sum_in_ref, sum_out_ref, small_ref, dtok_ref, mixed_ref, gconv_ref, gout_ref, ggate_ref, pad_ref, dact_ref, dheld_ref, direct_ref, dconv_ref, dscores_ref, dbc_ref, ddt_ref, q_ref, v_ref, ends_ref, crossed_ref, stage_ref, second_ref, rim_ref, rim_got_ref, one_sem, fill_sem, rim_sem, total_ref, factor_ref, reach_ref, held_ref, psend_ref, precv_ref, ps_sem, pr_sem, vsend_ref, vrecv_ref, vs_sem, vr_sem, r_held, r_core, r_sx, r_rx, r_near, r_res, load_sem, keep_sem, send_sem, recv_sem, *parts):
    g = pl.program_id(0)
    length = x_ref.shape[0]
    seq, peers = lax.axis_index("seq"), lax.axis_size("seq")
    following, previous = {"seq": lax.rem(seq + 1, peers)}, {"seq": lax.rem(seq + peers - 1, peers)}
    reducer = Reducer(gout_ref, ggate_ref, gconv_ref, sum_in_ref, sum_out_ref, r_held, r_core, r_sx, r_rx, r_near, r_res, load_sem, keep_sem, send_sem, recv_sem, parts)
    passing = Passing(True, total_ref, factor_ref, reach_ref, held_ref, psend_ref, precv_ref, met_ref, ps_sem, pr_sem)
    rounds = len(passing.bits)
    block = head_block(g)

    def columns_of(j):
        return pl.ds(pl.multiple_of(j * WIDE, WIDE), WIDE)

    def edge(j):
        return pltpu.make_async_remote_copy(src_ref=rim_ref.at[:, columns_of(j)], dst_ref=rim_got_ref.at[:, columns_of(j)], send_sem=rim_sem.at[0, j], recv_sem=rim_sem.at[1, j], device_id=previous, device_id_type=MESH)

    @pl.when(g == 0)
    def _():
        greet(reducer.partners + [following, previous])
        first = pltpu.make_async_copy(din_ref, total_ref, one_sem.at[2])
        first.start()
        for ref in (dscores_ref, dbc_ref, ddt_ref, q_ref, v_ref, ends_ref, crossed_ref, held_ref):
            ref[...] = jnp.zeros_like(ref)
        reach_ref[...] = jnp.ones_like(reach_ref)
        factor_ref[0:1, :] = met_ref[7:8, :]
        first.wait()
        for j in range(STEPS):
            passing.start(0, j)

    lows = (low0_ref, low1_ref, low2_ref, low3_ref)

    def filled(i):
        copies = []
        for b in range(PARTS):
            rows = pl.ds(pl.multiple_of(b * OUT_PART + i * ROWS, ROWS), ROWS)
            copies.append(pltpu.make_async_copy(stage_ref.at[b * ROWS : (b + 1) * ROWS, :], gout_ref.at[rows, :], fill_sem.at[b]))
        copies.append(pltpu.make_async_copy(second_ref, ggate_ref.at[columns_of(i), :], fill_sem.at[PARTS]))
        return copies

    @pl.when(jnp.logical_and(g >= 1, g <= FILL_STEPS))
    def _():
        for copy in filled(g - 1):
            copy.wait()

    @pl.when(g < FILL_STEPS)
    def _():
        for b in range(PARTS):
            stage_ref[b * ROWS : (b + 1) * ROWS, :] = tn(lows[b][...], up_ref[...]).astype(LOW)
        second_ref[...] = tn(dgate_ref[...], normed_ref[EDGE:, :]).astype(LOW)
        for copy in filled(g):
            copy.start()

    @pl.when(g == 1)
    def _():
        reducer.load(jnp.int32(0))

    for k in range(rounds - 1):
        since = g - (1 + 2 * k)

        @pl.when(jnp.logical_and(since >= 0, since < STEPS))
        def _(k=k, since=since):
            passing.finish(k, since)

    def near_block(c):
        at = pl.ds(pl.multiple_of(c * BLOCK, BLOCK), BLOCK)
        ids, jds = rows_cols((BLOCK, BLOCK))
        suffix = (ids >= jds).astype(LOW)
        left = lax.broadcasted_iota(jnp.int32, (BLOCK, LANES), 1) < HDIM
        scores = jnp.where(ids <= jds, nt(bc_ref[at, :NSTATE], bc_ref[at, NSTATE:]), 0.0)
        dy = dy_ref[at, :]
        sized = x_ref[at, :].astype(F32) * nn(d2_ref[at, :], e2_ref[...])
        total = jnp.zeros((BLOCK, BLOCK), F32)
        rows = []
        for pair in range(GROUP // 2):
            lanes = slice(pair * LANES, (pair + 1) * LANES)
            piece, dpiece = sized[:, lanes], dy[:, lanes]
            both = jnp.concatenate([jnp.where(left, piece, 0.0), jnp.where(left, 0.0, piece)], axis=0).astype(LOW)
            meets = nn(both, dpiece.T)
            mixed, kept = [], []
            for half in range(2):
                head = 2 * pair + half
                spread = rt_ref[head : head + 1, at] - rb_ref[at, head : head + 1]
                decay = jnp.exp(jnp.minimum(spread, 0.0))
                meet = meets[half * BLOCK : (half + 1) * BLOCK] * decay
                total = total + meet
                mixed.append((scores * decay).astype(LOW))
                kept.append((meet * scores).astype(LOW))
            later = nn(jnp.concatenate(kept, axis=0), suffix)
            for half in range(2):
                one = later[half * BLOCK : (half + 1) * BLOCK]
                rows.append(jnp.sum(jnp.where(ids < jds, one, 0.0), axis=0, keepdims=True))
            none = jnp.zeros_like(dpiece)
            both = jnp.concatenate([jnp.where(left, dpiece, none), jnp.where(left, none, dpiece)], axis=0)
            direct_ref[block, at, lanes] = nn(jnp.concatenate(mixed, axis=1), both)
        dscores_ref[c] += total
        crossed_ref[pl.ds(pl.multiple_of(block * GROUP, GROUP), GROUP), at] = jnp.concatenate(rows, axis=0)

    @pl.when(jnp.logical_and(g >= NEAR_AT, g < BACK_AT))
    def _():
        @pl.loop(0, PER)
        def _(i):
            near_block(((g - NEAR_AT) % HALF) * PER + i)

    turn = g - BACK_AT
    part = turn % TURNS
    going = jnp.logical_and(turn >= 0, turn < STEPS * TURNS)

    @pl.when(jnp.logical_and(going, part == 0))
    def _():
        passing.finish(rounds - 1, block)
        dheld_ref[...] = held_ref[:, passing.columns(block)]

    def back_block(c):
        at = pl.ds(pl.multiple_of(c * BLOCK, BLOCK), BLOCK)
        input_mat, output_mat = bc_ref[at, :NSTATE], bc_ref[at, NSTATE:]
        e2, et = e2_ref[...], et_ref[...]
        grow, leave, size = nn(er_ref[at, :], e2), nn(ew_ref[at, :], e2), nn(d2_ref[at, :], e2)
        prior = pl.ds(pl.multiple_of(jnp.maximum(c * BLOCK - 16, 0), 16), 16)
        reach = nn(ed_ref[prior, :], e2)[15:16, :]
        reach = jnp.where(c == 0, 1.0, reach)
        state = states_ref[c].astype(F32) + reach * in_ref[...].astype(F32)
        state_low = state.astype(LOW)
        x = x_ref[at, :].astype(F32)
        dy = dy_ref[at, :].astype(F32)
        dheld = dheld_ref[...]
        dheld_low = dheld.astype(LOW)
        grown = (dy * grow).astype(LOW)
        pulled = nn(input_mat, dheld_low) * leave
        dbc_ref[at, :NSTATE] += nt((x * size * leave).astype(LOW), dheld_low)
        dbc_ref[at, NSTATE:] += nt(grown, state_low)
        carried = nn(output_mat, state_low) * grow
        q_ref[at, :] += nn((dy * carried).astype(LOW), et)
        v_ref[at, :] += nn((x * pulled).astype(LOW), et)
        last = grow[BLOCK - 1 : BLOCK, :]
        ends = jnp.sum(state * dheld, axis=0, keepdims=True) * last
        ends_ref[c] += nn(jnp.broadcast_to(ends, (16, WIDE)).astype(LOW), et)[:8]
        dheld_ref[...] = dheld * last + tn(output_mat, grown)
        direct = direct_ref[block, at, :] + pulled
        ddt_ref[at, :] += nn((x * direct).astype(LOW), et)
        dact_ref[at, :] = size * direct + skip_ref[0:1, :] * dy

    @pl.when(jnp.logical_and(going, part < HALF))
    def _():
        @pl.loop(0, PER)
        def _(i):
            back_block(BLOCKS - 1 - (part * PER + i))

    @pl.when(turn == STEPS * TURNS)
    def _():
        ids, jds = rows_cols((BLOCK, BLOCK))
        upper = (ids <= jds).astype(F32)
        under = (ids > jds).astype(F32)
        rate = jnp.exp(heads_ref[1:2, :])
        dstep_bias = jnp.zeros((1, LANES), F32)
        ddecay_log = jnp.zeros((1, LANES), F32)
        for c in range(BLOCKS):
            at = slice(c * BLOCK, (c + 1) * BLOCK)
            dscores = jnp.where(ids <= jds, dscores_ref[c], 0.0).astype(LOW)
            dact_ref[at, :NSTATE] = dbc_ref[at, :NSTATE] + nn(dscores, bc_ref[at, NSTATE:])
            dact_ref[at, NSTATE : 2 * NSTATE] = dbc_ref[at, NSTATE:] + tn(dscores, bc_ref[at, :NSTATE])
            dt = dt_ref[at, :]
            ddecay = crossed_ref[:, at].T + exact(upper, q_ref[at, :]) + exact(under, v_ref[at, :] * dt) + ends_ref[c][0:1, :]
            draw = ddt_ref[at, :] - ddecay * rate
            ddecay_log = ddecay_log - jnp.sum(ddecay * dt, axis=0, keepdims=True) * rate
            raw = pc_ref[EDGE + c * BLOCK : EDGE + (c + 1) * BLOCK, 2 * NSTATE : 2 * NSTATE + LANES].astype(F32)
            used = lax.broadcasted_iota(jnp.int32, raw.shape, 1) < HEADS
            draw = draw * jax.nn.sigmoid(jnp.where(used, raw + heads_ref[0:1, :], 0.0))
            dstep_bias = dstep_bias + jnp.sum(draw, axis=0, keepdims=True)
            dact_ref[at, 2 * NSTATE : 2 * NSTATE + LANES] = draw
            dact_ref[at, 2 * NSTATE + LANES :] = jnp.zeros((BLOCK, LANES), F32)
        ends_ref[0] = jnp.broadcast_to(dstep_bias, (8, LANES))
        ends_ref[1] = jnp.broadcast_to(ddecay_log, (8, LANES))

    @pl.when(jnp.logical_or(jnp.logical_and(going, part == HALF), turn == STEPS * TURNS))
    def _():
        here = turn // TURNS
        at = pl.ds(pl.multiple_of(here * WIDE, WIDE), WIDE)
        taps = taps_ref[:, at]
        pad_ref[...] = pc_ref[...].astype(F32)
        summed = taps[CONV : CONV + 1]
        for k in range(CONV):
            first = EDGE - CONV + 1 + k
            summed = summed + taps[k : k + 1] * pad_ref[first : first + length, :]
        shape = jax.nn.sigmoid(summed)
        dsum = dact_ref[0:length, :] * (shape * (1.0 + summed * (1.0 - shape)))
        dtap = [jnp.sum(dsum * pad_ref[EDGE - CONV + 1 + k : EDGE - CONV + 1 + k + length, :], axis=0, keepdims=True) for k in range(CONV)]
        dtap.append(jnp.sum(dsum, axis=0, keepdims=True))
        vsend_ref[0, :, at] = jnp.concatenate(dtap + [jnp.zeros((8 - len(dtap), WIDE), F32)], axis=0)
        rim_ref[:, at] = dsum[:16].astype(LOW)
        keep = dact_ref[0:length, :]
        dact_ref[0:length, :] = dsum
        dact_ref[length:, :] = jnp.zeros_like(dact_ref[length:, :])
        result = taps[CONV - 1 : CONV] * dsum
        for k in range(CONV - 1):
            by = CONV - 1 - k
            result = result + taps[k : k + 1] * dact_ref[by : by + length, :]
        lane = lax.broadcasted_iota(jnp.int32, (1, WIDE), 1)
        raw_part = jnp.logical_and(turn == STEPS * TURNS, lane >= 2 * NSTATE)
        dconv_ref[:, at] = jnp.where(raw_part, keep, result).astype(LOW)

    def stored(k):
        return pltpu.make_async_copy(stage_ref, gconv_ref.at[columns_of(k), :], one_sem.at[2])

    def settle(j):
        edge(j).wait()

        @pl.when(j >= 1)
        def _():
            stored(j - 1).wait()

        at = columns_of(j)
        bottom = slice(length - 16, length)
        got, taps = rim_got_ref[:, at].astype(F32), taps_ref[:, at]
        ids, jds = rows_cols(got.shape)
        extra = jnp.zeros_like(got)
        for i in range(CONV - 1):
            row = sum(taps[k : k + 1] * got[i - k : i - k + 1] for k in range(i + 1))
            extra = jnp.where(ids == 16 - CONV + 1 + i, row, extra)
        takes = jnp.logical_and(jds < CDIM - j * WIDE, seq < peers - 1)
        dconv_ref[bottom, at] = (dconv_ref[bottom, at].astype(F32) + jnp.where(takes, extra, 0.0)).astype(LOW)
        stage_ref[...] = tn(dconv_ref[:, at], normed_ref[EDGE:, :]).astype(LOW)
        stored(j).start()

    convolves = jnp.logical_or(jnp.logical_and(going, part == HALF), turn == STEPS * TURNS)

    @pl.when(convolves)
    def _():
        edge(turn // TURNS).start()

    @pl.when(jnp.logical_or(jnp.logical_and(convolves, turn >= TURNS), g == EDGE_AT))
    def _():
        settle(jnp.where(g == EDGE_AT, STEPS, turn // TURNS - 1))

    @pl.when(g == PULL_AT)
    def _():
        stored(STEPS).wait()

    pull = g - PULL_AT

    thirds = [slice(i * WIDE, (i + 1) * WIDE) for i in range(DM // WIDE)]
    mixed_out = pltpu.make_async_copy(stage_ref, mixed_ref, one_sem.at[2])

    @pl.when(pull == 0)
    def _():
        for i, at in enumerate(thirds):
            direct_ref[i] = tok_ref[:, at].astype(F32)

    @pl.when(jnp.logical_and(pull >= 0, pull < GATE_STEPS))
    def _():
        for i, at in enumerate(thirds):
            direct_ref[i] += nn(low_ref[...], wgate_ref[:, at])

    @pl.when(pull == GATE_STEPS)
    def _():
        for i, at in enumerate(thirds):
            stage_ref[:, at] = direct_ref[i].astype(LOW)
        mixed_out.start()
        direct_ref[0:PARTS] = jnp.zeros_like(direct_ref[0:PARTS])

    def add_pull(left, weight):
        for b in range(PARTS):
            direct_ref[b, :, :PART] += nn(left, weight[:, b * PART : (b + 1) * PART])

    @pl.when(jnp.logical_and(pull >= GATE_STEPS, pull < 2 * GATE_STEPS))
    def _():
        add_pull(dgate_ref[...], wgate_ref[...])

    @pl.when(jnp.logical_and(pull >= 2 * GATE_STEPS, pull < PULL_STEPS))
    def _():
        k = pull - 2 * GATE_STEPS
        columns = pl.ds(pl.multiple_of(k * WIDE, WIDE), WIDE)
        ids = lax.broadcasted_iota(jnp.int32, (WIDE, DM), 0)
        weight = wconv_ref[...]
        weight = jnp.where(ids < CDIM + HEADS - k * WIDE, weight, jnp.zeros_like(weight))
        add_pull(dconv_ref[:, columns], weight)

    def normed_out(b):
        return pltpu.make_async_copy(direct_ref.at[relative(b), :, 0:PART], dtok_ref.at[:, b * PART : (b + 1) * PART], one_sem.at[3 + b])

    meets = len(reducer.partners)

    def swap(k):
        return pltpu.make_async_remote_copy(src_ref=vsend_ref.at[k], dst_ref=vrecv_ref.at[k], send_sem=vs_sem.at[k], recv_sem=vr_sem.at[k], device_id=reducer.partners[k], device_id_type=MESH)

    @pl.when(g == LAST_AT)
    def _():
        blocks = [slice(b * PART, (b + 1) * PART) for b in range(PARTS)]
        square = jnp.zeros((length, 1), F32)
        cross = jnp.zeros((length, 1), F32)
        for b, at in enumerate(blocks):
            u = tok_ref[:, at].astype(F32)
            square = square + jnp.sum(u * u, axis=1, keepdims=True)
            cross = cross + jnp.sum(direct_ref[relative(b), :, :PART] * gain_ref[0:1, at] * u, axis=1, keepdims=True)
        rate = lax.rsqrt(square * (1.0 / DM) + EPS)
        pulled = rate * rate * rate * (cross * (1.0 / DM))
        for b, at in enumerate(blocks):
            u = tok_ref[:, at].astype(F32)
            there = relative(b)
            d_normed = direct_ref[there, :, :PART]
            vsend_ref[0, 5:6, at] = jnp.sum(d_normed * (u * rate), axis=0, keepdims=True)
            direct_ref[there, :, :PART] = up_ref[:, at].astype(F32) + rate * (d_normed * gain_ref[0:1, at]) - u * pulled
            normed_out(b).start()
        vsend_ref[0, 6:7, :DI] = sums_ref[0:1, :]
        vsend_ref[0, 7:8, :DI] = sums_ref[1:2, :]
        vsend_ref[0, 6:7, DI : DI + LANES] = ends_ref[0][0:1]
        vsend_ref[0, 7:8, DI : DI + LANES] = ends_ref[1][0:1]

        swap(0).start()

    @pl.loop(paced(g), paced(g + 1) + (g // LAST_AT) * (reducer.total - DONE))
    def _(t):
        reducer.step(t)
        for k in range(meets):

            @pl.when(t == DONE + 2 * (k + 1))
            def _(k=k):
                swap(k).wait()
                value = vsend_ref[k] + vrecv_ref[k]
                if k + 1 < meets:
                    vsend_ref[k + 1] = value
                    swap(k + 1).start()
                else:
                    small_ref[...] = value

    @pl.when(g == LAST_AT)
    def _():
        for b in range(PARTS):
            normed_out(b).wait()
        mixed_out.wait()


def rear(proj, x, dy, bc, rb, rt, er, ew, d2, ed, dt, e2, et, states, incoming, taps, skip, heads, met, normed, tokens, upstream, gain, sums, low, dgate, wide_all, conv_all, din):
    length = x.shape[0]
    bits, halved = len(seq_bits()), halved_bits()
    hbm = pl.BlockSpec(memory_space=pl.ANY)
    back_block = lambda g: clip((g - BACK_AT) // TURNS, 0, STEPS)
    part_block = lambda g: clip((g - BACK_AT) // TURNS, 0, STEPS - 1)

    def whole(array):
        return pl.BlockSpec(array.shape, lambda g: (0,) * array.ndim, pipeline_mode=pl.Buffered(1))

    shares = []
    for j in range(bits):
        shape = (FEW, max(ROWS >> (j + 1), LEAST), PART)
        shares += [pltpu.VMEM(shape, LOW), pltpu.VMEM(shape, LOW), pltpu.VMEM(shape, F32)]
    dma = pltpu.SemaphoreType.DMA
    stages, meets = 2 + bits + halved, 2 + bits
    return pl.pallas_call(
        rear_kernel,
        grid=(ALL_STEPS,),
        in_specs=[
            pl.BlockSpec((length + EDGE, WIDE), lambda g: (0, back_block(g))),
            pl.BlockSpec((length, WIDE), lambda g: (0, head_block(g))),
            pl.BlockSpec((length, WIDE), lambda g: (0, head_block(g))),
            whole(bc),
            pl.BlockSpec((length, LANES), lambda g: (0, near_block_at(g))),
            pl.BlockSpec((GROUP, length), lambda g: (near_block_at(g), 0)),
            whole(er),
            whole(ew),
            whole(d2),
            whole(ed),
            whole(dt),
            pl.BlockSpec((2 * LANES, WIDE), lambda g: (0, head_block(g))),
            pl.BlockSpec((WIDE, LANES), lambda g: (part_block(g), 0)),
            pl.BlockSpec((length // BLOCK, NSTATE, WIDE), lambda g: (0, 0, part_block(g))),
            pl.BlockSpec((NSTATE, WIDE), lambda g: (0, part_block(g))),
            whole(taps),
            pl.BlockSpec((8, WIDE), lambda g: (0, part_block(g))),
            whole(heads),
            whole(met),
            whole(normed),
            whole(tokens),
            whole(upstream),
            whole(gain),
            whole(sums),
        ]
        + [pl.BlockSpec((length, ROWS), lambda g, b=b: (0, b * (OUT_PART // ROWS) + jnp.minimum(g, FILL_STEPS - 1))) for b in range(PARTS)]
        + [
            pl.BlockSpec((length, WIDE), lambda g: (0, clip(g - PULL_AT, 0, GATE_STEPS - 1))),
            pl.BlockSpec((length, WIDE), lambda g: (0, gate_block(g))),
            pl.BlockSpec((WIDE, DM), lambda g: ((clip(g - PULL_AT, 0, 2 * GATE_STEPS - 1) + GATE_STEPS) % (2 * GATE_STEPS), 0)),
            pl.BlockSpec((WIDE, DM), lambda g: (clip(g - PULL_AT - 2 * GATE_STEPS, 0, DOT_STEPS - 1), 0)),
            hbm,
        ],
        out_specs=[hbm, hbm, pl.BlockSpec((8, LONG), lambda g: (0, 0)), hbm, hbm, hbm, hbm, hbm],
        out_shape=[
            jax.ShapeDtypeStruct((DI + CDIM + HEADS, PART), LOW),
            jax.ShapeDtypeStruct((OUT_PART, DM), LOW),
            jax.ShapeDtypeStruct((8, LONG), F32),
            jax.ShapeDtypeStruct((length, DM), F32),
            jax.ShapeDtypeStruct((length, DM), LOW),
            jax.ShapeDtypeStruct((LONG, DM), LOW),
            jax.ShapeDtypeStruct((DI, DM), LOW),
            jax.ShapeDtypeStruct((DI, DM), LOW),
        ],
        scratch_shapes=[
            pltpu.VMEM((length + EDGE, WIDE), F32),
            pltpu.VMEM((length + EDGE, WIDE), F32),
            pltpu.VMEM((NSTATE, WIDE), F32),
            pltpu.VMEM((STEPS, length, WIDE), F32),
            pltpu.VMEM((length, LONG), LOW),
            pltpu.VMEM((length // BLOCK, BLOCK, BLOCK), F32),
            pltpu.VMEM((length, 2 * NSTATE), F32),
            pltpu.VMEM((length, LANES), F32),
            pltpu.VMEM((length, LANES), F32),
            pltpu.VMEM((length, LANES), F32),
            pltpu.VMEM((length // BLOCK, 8, LANES), F32),
            pltpu.VMEM((LANES, length), F32),
            pltpu.VMEM((WIDE, DM), LOW),
            pltpu.VMEM((WIDE, DM), LOW),
            pltpu.VMEM((16, LONG), LOW),
            pltpu.VMEM((16, LONG), LOW),
            dma((3 + PARTS,)),
            dma((PARTS + 1,)),
            dma((2, STEPS + 1)),
            pltpu.VMEM((NSTATE, DI), F32),
            pltpu.VMEM((8, DI), F32),
            pltpu.VMEM((8, DI), F32),
            pltpu.VMEM((NSTATE, DI), F32),
            pltpu.VMEM((NSTATE, DI), LOW),
            pltpu.VMEM((bits, NSTATE, DI), LOW),
            dma((bits, STEPS)),
            dma((bits, STEPS)),
            pltpu.VMEM((meets, 8, LONG), F32),
            pltpu.VMEM((meets, 8, LONG), F32),
            dma((meets,)),
            dma((meets,)),
            pltpu.VMEM((FEW, ROWS, DM), LOW),
            pltpu.VMEM((FEW, ROWS, 2 * PART), LOW),
            pltpu.VMEM((FEW, ROWS, PART), LOW),
            pltpu.VMEM((FEW, ROWS, PART), LOW),
            pltpu.VMEM((FEW, ROWS, PART), F32),
            pltpu.VMEM((SLOTS, ROWS, PART), LOW),
            dma((FEW,)),
            dma((SLOTS,)),
            dma((stages, FEW)),
            dma((stages, FEW)),
        ]
        + shares,
        compiler_params=pltpu.CompilerParams(vmem_limit_bytes=62 << 20, collective_id=2, has_side_effects=True),
        cost_estimate=pl.CostEstimate(flops=200 << 30, bytes_accessed=60 << 20, transcendentals=0),
        name="rear",
    )(proj, x, dy, bc, rb, rt, er, ew, d2, ed, dt, e2, et, states, incoming, taps, skip, heads, met, normed, tokens, upstream, gain, sums, low, low, low, low, low, dgate, wide_all, conv_all, din)


def shards(tokens, norm_gain, in_weight, conv_kernel, conv_bias, step_bias, decay_log, skip_gain, out_gain, out_weight, cotangent):
    length = tokens.shape[1]
    own, upstream = tokens[0], cotangent[0]
    turned = in_weight.T
    gain = norm_gain[None]
    skip = jnp.repeat(skip_gain, HDIM)[None]
    gains = jnp.concatenate([out_gain[None], skip, jnp.zeros((6, DI), F32)], axis=0)
    skip = jnp.broadcast_to(skip, (8, DI))
    lanes = np.arange(DI) // HDIM
    e2 = jnp.asarray((np.arange(2 * LANES)[:, None] % LANES == lanes[None]).astype(LOW))
    et = jnp.asarray((lanes[:, None] == np.arange(LANES)[None]).astype(LOW))

    taps, heads, proj, normed, x, bc, dt, rb, rt, er, ew, d2, ed, state, conv_all = enter(own, gain, conv_kernel, conv_bias[None], step_bias[None], decay_log[None], e2, turned)
    incoming, met, y, states, gate, dno, wide_all = gates(normed, upstream, state, x, bc, rb, rt, er, ew, d2, e2, turned, out_weight)
    low, dy, dgate, sums, din = middle(y, bc, incoming, ed, e2, x, gate, dno, gains, length)

    sum_in, sum_out, small, d_tokens, mixed, *_ = rear(proj, x, dy, bc, rb, rt, er, ew, d2, ed, dt, e2, et, states, incoming, taps, skip, heads, met, normed, own, upstream, gain, sums, low, dgate, wide_all, conv_all, din)
    return (
        mixed[None],
        d_tokens[None],
        small[5, :DM],
        sum_in.astype(F32).T,
        small[:CONV, :CDIM],
        small[CONV, :CDIM],
        small[6, DI : DI + HEADS],
        small[7, DI : DI + HEADS],
        jnp.sum(small[7, :DI].reshape(HEADS, HDIM), axis=1),
        small[6, :DI],
        sum_out.astype(F32),
    )


def solution(mesh):
    spread = P("wt", "seq", None)
    return jax.shard_map(
        shards,
        mesh=mesh,
        in_specs=(spread, P(), P("wt", None), P(), P(), P(), P(), P(), P(), P("wt", None), spread),
        out_specs=(spread, spread, P(), P("wt", None), P(), P(), P(), P(), P(), P(), P("wt", None)),
        check_vma=False,
    )
```

```python
import jax
import jax.numpy as jnp
import numpy as np
from jax import lax
from jax.experimental import pallas as pl
from jax.experimental.pallas import tpu as pltpu
from jax.sharding import PartitionSpec as P

DI = 3072
HEADS = 48
HDIM = 64
NSTATE = 128
CONV = 4
CDIM = 3328
EDGE = 16
BLOCK = 128
GROUP = 8
WIDE = GROUP * HDIM
STEPS = HEADS // GROUP
LONG = (STEPS + 1) * WIDE
LANES = 128
TILE = 512
FINE = 256
SHORT = 128
AHEAD = 4
LAG = 2
LAST = 320
PARTS = 4
DM = 1536
PART = DM // PARTS
OUT_PART = DI // PARTS
SLOTS = 16
FEW = 4
SLACK = 2
MESH = pl.DeviceIdType.MESH

EPS = 1e-05
F32 = jnp.float32
LOW = jnp.bfloat16


def dot(a, b, ca, cb):
    return lax.dot_general(a, b, (((ca,), (cb,)), ((), ())), preferred_element_type=F32)


def nn(a, b):
    return dot(a, b, 1, 0)


def nt(a, b):
    return dot(a, b, 1, 1)


def tn(a, b):
    return dot(a, b, 0, 0)


def exact(a, b):
    return jnp.dot(a, b, precision=lax.Precision.HIGHEST, preferred_element_type=F32)


def halves(v):
    high = v.astype(LOW)
    return jnp.concatenate([high, (v - high.astype(F32)).astype(LOW)], axis=1)


def softplus(v):
    z = jnp.exp(-jnp.abs(v))
    small = z * (1.0 - z * (0.5 - z * (1.0 / 3.0 - z * 0.25)))
    return jnp.maximum(v, 0.0) + jnp.where(z < 0.01, small, jnp.log(1.0 + z))


def rows_cols(shape):
    return (lax.broadcasted_iota(jnp.int32, shape, 0), lax.broadcasted_iota(jnp.int32, shape, 1))


class Begin:
    def __init__(self, proj_ref, taps_ref, heads_ref, e2_ref, x_ref, bc_ref, dt_ref, rb_ref, rt_ref, er_ref, ew_ref, d2_ref, ed_ref, state_ref, pad_ref, wd_ref):
        self.proj, self.taps, self.heads, self.e2 = proj_ref, taps_ref, heads_ref, e2_ref
        self.x, self.bc, self.dt, self.rb, self.rt = x_ref, bc_ref, dt_ref, rb_ref, rt_ref
        self.er, self.ew, self.d2, self.ed, self.state = er_ref, ew_ref, d2_ref, ed_ref, state_ref
        self.pad, self.wd = pad_ref, wd_ref
        self.length = x_ref.shape[0]

    def convolved(self, first, width):
        self.pad[:, :width] = self.proj[:, first : first + width].astype(F32)
        total = self.taps[CONV : CONV + 1, first : first + WIDE]
        for k in range(CONV):
            at = EDGE - CONV + 1 + k
            total = total + self.taps[k : k + 1, first : first + WIDE] * self.pad[at : at + self.length, :]
        return total * jax.nn.sigmoid(total)

    def sizes(self):
        length = self.length
        self.pad[...] = jnp.zeros_like(self.pad)
        act = self.convolved(DI, CDIM + HEADS - DI)
        self.bc[...] = act[:, : 2 * NSTATE].astype(LOW)
        raw = self.pad[EDGE:, 2 * NSTATE : 2 * NSTATE + LANES]
        used = lax.broadcasted_iota(jnp.int32, raw.shape, 1) < HEADS
        dt = jnp.where(used, softplus(jnp.where(used, raw + self.heads[0:1, :], 0.0)), 0.0)
        self.dt[...] = dt
        self.d2[...] = halves(dt)
        decay = -dt * jnp.exp(self.heads[1:2, :])
        ids, jds = rows_cols((BLOCK, BLOCK))
        lower = (ids >= jds).astype(F32)
        before = jnp.zeros((1, LANES), F32)
        whole = []
        for c in range(length // BLOCK):
            at = slice(c * BLOCK, (c + 1) * BLOCK)
            run = exact(lower, decay[at])
            last = run[BLOCK - 1 : BLOCK]
            for j in range(STEPS):
                turned = jnp.concatenate([run[:, GROUP * j :], run[:, : GROUP * j]], axis=1) if j else run
                self.rb[at, j * LANES : (j + 1) * LANES] = turned
            self.rt[:, at] = run.T
            self.er[at, :] = halves(jnp.exp(run))
            self.ew[at, :] = halves(jnp.exp(last - run))
            whole.append(run + before)
            self.ed[at, :] = halves(jnp.exp(run + before))
            before = before + last
        for c in range(length // BLOCK):
            at = slice(c * BLOCK, (c + 1) * BLOCK)
            self.wd[at, :] = halves(jnp.exp(before - whole[c]) * dt[at])

    def block(self, j):
        at = slice(j * WIDE, (j + 1) * WIDE)
        x = self.convolved(j * WIDE, WIDE).astype(LOW)
        self.x[:, at] = x
        e2 = self.e2[:, at]
        weighed = (x.astype(F32) * nn(self.wd[...], e2)).astype(LOW)
        self.state[0:NSTATE, at] = tn(self.bc[:, :NSTATE], weighed).astype(LOW)
        decay = nn(self.ed[self.length - 16 : self.length, :], e2)[15:16, :]
        high = decay.astype(LOW).astype(F32)
        ids = lax.broadcasted_iota(jnp.int32, (16, WIDE), 0)
        self.state[NSTATE : NSTATE + 16, at] = jnp.where(ids == 0, high, jnp.where(ids == 1, decay - high, 0.0)).astype(LOW)


class Stages:
    def __init__(self, ref, sem):
        self.ref, self.sem, self.count = ref, sem, ref.shape[0]
        self.flying = [None] * self.count
        self.turn = 0

    def put(self, value, target):
        at = self.turn % self.count
        if self.flying[at] is not None:
            self.flying[at].wait()
        self.ref[at] = value
        self.flying[at] = pltpu.make_async_copy(self.ref.at[at], target, self.sem.at[at])
        self.flying[at].start()
        self.turn += 1

    def rest(self):
        for one in self.flying:
            if one is not None:
                one.wait()


class Inside:
    def __init__(self, x_ref, bc_ref, rb_ref, rt_ref, er_ref, ew_ref, d2_ref, e2_ref, held_ref, y_out, states_out, ys, states):
        self.x, self.bc, self.rb, self.rt = x_ref, bc_ref, rb_ref, rt_ref
        self.er, self.ew, self.d2, self.e2, self.held = er_ref, ew_ref, d2_ref, e2_ref, held_ref
        self.y_out, self.states_out, self.ys, self.states = y_out, states_out, ys, states
        self.blocks = x_ref.shape[0] // BLOCK

    def turn(self, at):
        if at < STEPS * self.blocks:
            self.block(at // self.blocks, at % self.blocks)

    def block(self, j, c):
        at, own = slice(c * BLOCK, (c + 1) * BLOCK), slice(j * WIDE, (j + 1) * WIDE)
        ids, jds = rows_cols((BLOCK, BLOCK))
        left = lax.broadcasted_iota(jnp.int32, (BLOCK, LANES), 1) < HDIM
        input_mat, output_mat = self.bc[at, :NSTATE], self.bc[at, NSTATE:]
        e2 = self.e2[:, own]
        grow, leave = nn(self.er[at, :], e2), nn(self.ew[at, :], e2)
        x = self.x[at, own].astype(F32) * nn(self.d2[at, :], e2)
        scores = jnp.where(ids >= jds, nt(output_mat, input_mat), 0.0)
        held = self.held[...] if c else jnp.zeros_like(self.held)
        self.states.put(held.astype(LOW), self.states_out.at[c, :, own])
        carried = grow * nn(output_mat, held.astype(LOW))
        parts = []
        for pair in range(GROUP // 2):
            lanes = slice(pair * LANES, (pair + 1) * LANES)
            piece = x[:, lanes]
            mixed = []
            for head in (2 * pair, 2 * pair + 1):
                column = self.rb[at, j * LANES + head : j * LANES + head + 1]
                spread = column - self.rt[j * GROUP + head : j * GROUP + head + 1, at]
                mixed.append((scores * jnp.exp(jnp.minimum(spread, 0.0))).astype(LOW))
            both = jnp.concatenate([jnp.where(left, piece, 0.0), jnp.where(left, 0.0, piece)], axis=0)
            parts.append(nn(jnp.concatenate(mixed, axis=1), both.astype(LOW)) + carried[:, lanes])
        self.ys.put(jnp.concatenate(parts, axis=1), self.y_out.at[at, own])
        self.held[...] = held * grow[BLOCK - 1 : BLOCK, :] + tn(input_mat, (x * leave).astype(LOW))


def middle_kernel(y_ref, bc_ref, in_ref, ed_ref, e2_ref, x_ref, gate_ref, dno_ref, gains_ref, low_ref, dy_ref, dgate_ref, sums_ref, din_ref, out_ref, gated_ref):
    @pl.when(pl.program_id(0) == 0)
    def _():
        sums_ref[...] = jnp.zeros_like(sums_ref)
        din_ref[...] = jnp.zeros_like(din_ref)

    output_mat = bc_ref[:, NSTATE:]
    part = DI // PARTS
    tiles = []
    for j in range(PARTS):
        there = relative(j)
        tiles.append((slice(j * part, (j + 1) * part), pl.ds(pl.multiple_of(there * part, LANES), part)))
    square = jnp.zeros((BLOCK, 1), F32)
    cross = jnp.zeros((BLOCK, 1), F32)
    for at, there in tiles:
        far = nn(ed_ref[...], e2_ref[:, at]) * nn(output_mat, in_ref[:, at])
        out = y_ref[:, at] + far + gains_ref[1:2, at] * x_ref[:, at].astype(F32)
        gate = gate_ref[:, at].astype(F32)
        gated = out * gate * jax.nn.sigmoid(gate)
        out_ref[:, at] = out
        gated_ref[:, at] = gated
        square = square + jnp.sum(gated * gated, axis=1, keepdims=True)
        cross = cross + jnp.sum(gated * (dno_ref[:, there] * gains_ref[0:1, at]), axis=1, keepdims=True)
    scale = lax.rsqrt(square * (1.0 / DI) + EPS)
    pull = scale * scale * scale * (cross * (1.0 / DI))
    for at, there in tiles:
        gate = gate_ref[:, at].astype(F32)
        gated, out, gain = gated_ref[:, at], out_ref[:, at], gains_ref[0:1, at]
        shape = jax.nn.sigmoid(gate)
        unit = gated * scale
        low_ref[:, there] = (unit * gain).astype(LOW)
        dno = dno_ref[:, there]
        dgated = scale * (dno * gain) - gated * pull
        dy = dgated * (gate * shape)
        dy_ref[:, at] = dy.astype(LOW)
        dgate_ref[:, at] = (dgated * out * (shape * (1.0 + gate * (1.0 - shape)))).astype(LOW)
        sums_ref[0:1, at] += jnp.sum(dno * unit, axis=0, keepdims=True)
        sums_ref[1:2, at] += jnp.sum(dy * x_ref[:, at].astype(F32), axis=0, keepdims=True)
        din_ref[:, at] += tn(output_mat, (dy * nn(ed_ref[...], e2_ref[:, at])).astype(LOW))


def middle(y, bc, incoming, ed, e2, x, gate, dno, gains, length):
    rows = lambda c: (c, 0)
    fixed = lambda c: (0, 0)
    return pl.pallas_call(
        middle_kernel,
        grid=(length // BLOCK,),
        in_specs=[
            pl.BlockSpec((BLOCK, DI), rows),
            pl.BlockSpec((BLOCK, 2 * NSTATE), rows),
            pl.BlockSpec((NSTATE, DI), fixed),
            pl.BlockSpec((BLOCK, 2 * LANES), rows),
            pl.BlockSpec((2 * LANES, DI), fixed),
            pl.BlockSpec((BLOCK, DI), rows),
            pl.BlockSpec((BLOCK, DI), rows),
            pl.BlockSpec((BLOCK, DI), rows),
            pl.BlockSpec((8, DI), fixed),
        ],
        out_specs=[
            pl.BlockSpec((BLOCK, DI), rows),
            pl.BlockSpec((BLOCK, DI), rows),
            pl.BlockSpec((BLOCK, DI), rows),
            pl.BlockSpec((8, DI), fixed),
            pl.BlockSpec((NSTATE, DI), fixed),
        ],
        out_shape=[
            jax.ShapeDtypeStruct((length, DI), LOW),
            jax.ShapeDtypeStruct((length, DI), LOW),
            jax.ShapeDtypeStruct((length, DI), LOW),
            jax.ShapeDtypeStruct((8, DI), F32),
            jax.ShapeDtypeStruct((NSTATE, DI), F32),
        ],
        scratch_shapes=[pltpu.VMEM((BLOCK, DI), F32), pltpu.VMEM((BLOCK, DI), F32)],
        compiler_params=pltpu.CompilerParams(vmem_limit_bytes=48 << 20),
        cost_estimate=pl.CostEstimate(flops=12 << 30, bytes_accessed=32 << 20, transcendentals=4 << 20),
        name="middle",
    )(y, bc, incoming, ed, e2, x, gate, dno, gains)


def spot():
    wt, seq = lax.axis_index("wt"), lax.axis_index("seq")
    return wt // 2, wt % 2, seq % 2


def relative(block):
    x, core, _ = spot()
    high, low = block // 2, block % 2
    return 2 * (core + low - 2 * core * low) + (x + high - 2 * x * high)


def across_bit(axis, bit):
    index = lax.axis_index(axis)
    return {axis: index + bit - 2 * bit * ((index // bit) % 2)}


def greet(devices):
    barrier = pltpu.get_barrier_semaphore()
    for device in devices:
        pl.semaphore_signal(barrier, inc=1, device_id=device, device_id_type=MESH)
    pl.semaphore_wait(barrier, len(devices))


class Piece:
    def __init__(self, source, near, mine, pair, twin, half, sems, at):
        bit = 1 + at % 2
        part = pl.multiple_of((lax.axis_index("seq") // bit) % 2 * half, 16)
        own, xs, xr, ys, yr, ts, tr, keep = sems
        rows = lambda ref: ref.at[pl.ds(part, half), :]
        self.own = pltpu.make_async_copy(source, mine, own.at[at])
        self.x = self.remote(rows(source), rows(near), xs.at[at], xr.at[at], across_bit("wt", 2))
        self.y = self.remote(rows(near), rows(near), ys.at[at], yr.at[at], across_bit("seq", bit))
        self.twin = self.remote(pair, twin, ts.at[at], tr.at[at], across_bit("wt", 1))

    def remote(self, source, target, send, recv, device):
        return pltpu.make_async_remote_copy(src_ref=source, dst_ref=target, send_sem=send, recv_sem=recv, device_id=device, device_id_type=MESH)


def gather_sems(count):
    return [pltpu.SemaphoreType.DMA((count,)) for _ in range(8)]


def enter_kernel(tok_ref, gain_ref, kernel_ref, bias_ref, step_ref, log_ref, e2_ref, w_ref, taps_ref, heads_ref, proj_ref, normed_ref, x_ref, bc_ref, dt_ref, rb_ref, rt_ref, er_ref, ew_ref, d2_ref, ed_ref, state_ref, all_ref, wide_ref, last_ref, edge_ref, pad_ref, wd_ref, edge_sem, *sems):
    length = tok_ref.shape[0]
    begin = Begin(proj_ref, taps_ref, heads_ref, e2_ref, x_ref, bc_ref, dt_ref, rb_ref, rt_ref, er_ref, ew_ref, d2_ref, ed_ref, state_ref, pad_ref, wd_ref)
    seq, peers = lax.axis_index("seq"), lax.axis_size("seq")
    following, previous = {"seq": lax.rem(seq + 1, peers)}, {"seq": lax.rem(seq + peers - 1, peers)}
    greet([across_bit("wt", 1), across_bit("wt", 2), across_bit("seq", 1), across_bit("seq", 2), following, previous])
    edge = pltpu.make_async_remote_copy(src_ref=tok_ref.at[length - EDGE : length, :], dst_ref=edge_ref, send_sem=edge_sem.at[0], recv_sem=edge_sem.at[1], device_id=following, device_id_type=MESH)
    edge.start()
    count = CDIM // TILE
    pieces, products, keeps = [], [], []

    def add(target, first, rows):
        pieces.append(Piece(w_ref.at[pl.ds(first, rows), :], target.at[:, PART : 2 * PART], target.at[:, :PART], target.at[:, : 2 * PART], target.at[:, 2 * PART :], rows // 2, sems, len(pieces)))
        products.append(None)

    def multiply(target, columns, skip, then):
        keep = pltpu.make_async_copy(target.at[skip:, :], all_ref.at[columns, :], sems[-1].at[len(keeps)])
        keeps.append(keep)

        def product():
            keep.start()
            proj_ref[:, columns] = nt(normed_ref[...], target[skip:, :]).astype(LOW)
            then()

        products[-1] = product

    add(last_ref, DI + CDIM + HEADS - LAST, LAST)
    multiply(last_ref, slice(count * TILE, CDIM + HEADS), LAST - (CDIM + HEADS - count * TILE), begin.sizes)
    for c in range(count):
        for first in range(c * TILE, (c + 1) * TILE, FINE):
            add(wide_ref.at[first : first + FINE, :], DI + first, FINE)
        multiply(wide_ref.at[c * TILE : (c + 1) * TILE, :], slice(c * TILE, (c + 1) * TILE), 0, lambda c=c: begin.block(c))
    for piece in pieces:
        piece.own.start()
    for piece in pieces[:AHEAD]:
        piece.x.start()

    def norm(v):
        v = v.astype(F32)
        return (v * lax.rsqrt(jnp.mean(v * v, axis=-1, keepdims=True) + EPS) * gain_ref[0:1, :]).astype(LOW)

    def place(at, v):
        for b in range(PARTS):
            normed_ref[at, pl.ds(pl.multiple_of(relative(b) * PART, LANES), PART)] = v[:, b * PART : (b + 1) * PART]

    taps_ref[...] = jnp.zeros_like(taps_ref)
    taps_ref[0:CONV, :CDIM] = kernel_ref[...]
    taps_ref[CONV : CONV + 1, :CDIM] = bias_ref[...]
    heads_ref[...] = jnp.zeros_like(heads_ref)
    heads_ref[0:1, :HEADS] = step_ref[...]
    heads_ref[1:2, :HEADS] = log_ref[...]
    place(slice(EDGE, EDGE + length), norm(tok_ref[...]))
    edge.wait()
    place(slice(0, EDGE), norm(jnp.where(seq == 0, 0.0, edge_ref[...].astype(F32))))
    travel_on(pieces, products)
    for keep in keeps:
        keep.wait()


def travel_on(pieces, products, ahead=AHEAD, lag=LAG, between=None):
    count = len(pieces)
    for t in range(count + 2 * lag):
        if t < count:
            pieces[t].x.wait_recv()
            pieces[t].y.start()
            if t + ahead < count:
                pieces[t + ahead].x.start()
        if 0 <= t - lag < count:
            pieces[t - lag].y.wait_recv()
            pieces[t - lag].own.wait()
            pieces[t - lag].twin.start()
        if 0 <= t - 2 * lag < count:
            pieces[t - 2 * lag].twin.wait_recv()
            if products[t - 2 * lag] is not None:
                products[t - 2 * lag]()
        if between is not None:
            between(t)
    for piece in pieces:
        piece.x.wait_send()
        piece.y.wait_send()
        piece.twin.wait_send()


def enter(tokens, gain, conv_kernel, conv_bias, step_bias, decay_log, e2, weight):
    length, columns = tokens.shape[0], CDIM + HEADS
    vmem, hbm = pl.BlockSpec(memory_space=pltpu.VMEM), pl.BlockSpec(memory_space=pl.ANY)
    shapes = [
        ((8, LONG), F32),
        ((8, LANES), F32),
        ((length + EDGE, columns), LOW),
        ((length + EDGE, DM), LOW),
        ((length, DI), LOW),
        ((length, 2 * NSTATE), LOW),
        ((length, LANES), F32),
        ((length, LANES * STEPS), F32),
        ((LANES, length), F32),
        ((length, 2 * LANES), LOW),
        ((length, 2 * LANES), LOW),
        ((length, 2 * LANES), LOW),
        ((length, 2 * LANES), LOW),
        ((NSTATE + 16, DI), LOW),
        ((columns, DM), LOW),
    ]
    return pl.pallas_call(
        enter_kernel,
        in_specs=[vmem] * 7 + [hbm],
        out_specs=[vmem] * (len(shapes) - 1) + [hbm],
        out_shape=[jax.ShapeDtypeStruct(shape, kind) for shape, kind in shapes],
        scratch_shapes=[
            pltpu.VMEM((CDIM // TILE * TILE, DM), LOW),
            pltpu.VMEM((LAST, DM), LOW),
            pltpu.VMEM((EDGE, DM), LOW),
            pltpu.VMEM((length + EDGE, WIDE), F32),
            pltpu.VMEM((length, 2 * LANES), LOW),
            pltpu.SemaphoreType.DMA((2,)),
        ]
        + gather_sems(CDIM // TILE * (TILE // FINE) + 1),
        compiler_params=pltpu.CompilerParams(vmem_limit_bytes=56 << 20, collective_id=0, has_side_effects=True),
        cost_estimate=pl.CostEstimate(flops=40 << 30, bytes_accessed=30 << 20, transcendentals=0),
        name="enter",
    )(tokens, gain, conv_kernel, conv_bias, step_bias, decay_log, e2, weight)


class Passing:
    def __init__(self, later, total, factor, reach, held, send, recv, met, send_sem, recv_sem):
        self.later, self.total, self.factor, self.reach, self.held = later, total, factor, reach, held
        self.send, self.recv, self.met, self.send_sem, self.recv_sem = send, recv, met, send_sem, recv_sem
        self.bits = seq_bits()

    def columns(self, j):
        return pl.ds(pl.multiple_of(j * WIDE, WIDE), WIDE)

    def copy(self, k, j):
        at = self.columns(j)
        return pltpu.make_async_remote_copy(src_ref=self.send.at[:, at], dst_ref=self.recv.at[k, :, at], send_sem=self.send_sem.at[k, j], recv_sem=self.recv_sem.at[k, j], device_id=across_bit("seq", self.bits[k]), device_id_type=MESH)

    def start(self, k, j):
        at = self.columns(j)
        self.send[0:NSTATE, at] = self.total[:, at].astype(LOW)
        if not self.later:
            factor = self.factor[0:1, at]
            high = factor.astype(LOW).astype(F32)
            ids = lax.broadcasted_iota(jnp.int32, (16, WIDE), 0)
            self.send[NSTATE : NSTATE + 16, at] = jnp.where(ids == 0, high, jnp.where(ids == 1, factor - high, 0.0)).astype(LOW)
        self.copy(k, j).start()

    def finish(self, k, j):
        self.copy(k, j).wait()
        at = self.columns(j)
        bit = self.bits[k]
        second = (lax.axis_index("seq") // bit) % 2
        takes = second == (0 if self.later else 1)
        other = self.recv[k, 0:NSTATE, at].astype(F32)
        if self.later:
            met = self.met[k : k + 1, at]
        else:
            rows = self.recv[k, NSTATE : NSTATE + 16, at].astype(F32)
            met = rows[0:1] + rows[1:2]
            self.met[k : k + 1, at] = met
        total, factor, reach = self.total[:, at], self.factor[0:1, at], self.reach[0:1, at]
        self.held[:, at] = self.held[:, at] + jnp.where(takes, reach, 0.0) * other
        self.reach[0:1, at] = jnp.where(takes, reach * met, reach)
        if k + 1 < len(self.bits):
            self.total[:, at] = jnp.where(takes, factor, 1.0) * other + jnp.where(takes, 1.0, met) * total
            self.factor[0:1, at] = factor * met
            self.start(k + 1, j)

    def due(self, k, j):
        last = len(self.bits) - 1
        return 1 + 2 * k + j if k < last else 2 + 2 * last + j

    def step(self, t):
        for k in range(len(self.bits)):
            for j in range(STEPS):
                if t == self.due(k, j):
                    self.finish(k, j)

    def rest(self, t):
        for late in range(t, self.due(len(self.bits) - 1, STEPS - 1) + 1):
            self.step(late)


def gates_kernel(normed_ref, up_ref, state_ref, x_ref, bc_ref, rb_ref, rt_ref, er_ref, ew_ref, d2_ref, e2_ref, w_ref, o_ref, incoming_ref, met_ref, y_out, states_out, gate_out, dno_out, wall_ref, wide_ref, deep_ref, total_ref, factor_ref, reach_ref, held_ref, send_ref, recv_ref, own_ref, y_ref, states_ref, gate_ref, dno_ref, ss_sem, sr_sem, deep_sem, stage_sem, *sems):
    stages = [Stages(ref, stage_sem.at[i]) for i, ref in enumerate((y_ref, states_ref, gate_ref, dno_ref))]
    local = Inside(x_ref, bc_ref, rb_ref, rt_ref, er_ref, ew_ref, d2_ref, e2_ref, own_ref, y_out, states_out, stages[0], stages[1])
    greet([across_bit("wt", 1), across_bit("wt", 2)] + [across_bit("seq", bit) for bit in seq_bits()])
    passing = Passing(False, total_ref, factor_ref, reach_ref, held_ref, send_ref, recv_ref, met_ref, ss_sem, sr_sem)
    total_ref[...] = state_ref[0:NSTATE, :].astype(F32)
    rows = state_ref[NSTATE : NSTATE + 16, :].astype(F32)
    factor_ref[0:1, :] = rows[0:1] + rows[1:2]
    reach_ref[...] = jnp.ones_like(reach_ref)
    held_ref[...] = jnp.zeros_like(held_ref)
    met_ref[...] = jnp.zeros_like(met_ref)
    met_ref[7:8, :] = factor_ref[0:1, :]
    for j in range(STEPS):
        passing.start(0, j)
    pieces, products, keeps = [], [], []

    for c in range(DI // TILE):
        rows = slice(c * TILE, (c + 1) * TILE)
        target = wide_ref.at[rows, :]
        pieces.append(Piece(w_ref.at[rows, :], target.at[:, PART : 2 * PART], target.at[:, :PART], target.at[:, : 2 * PART], target.at[:, 2 * PART :], TILE // 2, sems, len(pieces)))
        keeps.append(pltpu.make_async_copy(target, wall_ref.at[rows, :], sems[-1].at[c]))

        def product(rows=rows, keep=keeps[-1]):
            keep.start()
            for first in (rows.start, rows.start + FINE):
                at = slice(first, first + FINE)
                stages[2].put(nt(normed_ref[EDGE:, :], wide_ref[at, :]).astype(LOW), gate_out.at[:, at])

        products.append(product)

    for c in range(OUT_PART // SHORT):
        rows = slice(c * SHORT, (c + 1) * SHORT)
        pieces.append(Piece(o_ref.at[rows, :], deep_ref.at[1, rows, :], deep_ref.at[0, rows, :], deep_ref.at[0:2, rows, :], deep_ref.at[2:4, rows, :], SHORT // 2, sems, len(pieces)))
        products.append(None)
        if (c + 1) * SHORT % FINE == 0:
            first = (c + 1) * SHORT - FINE
            mine = [pltpu.make_async_copy(deep_ref.at[b, first : first + FINE, :], wall_ref.at[pl.ds(DI + b * OUT_PART + first, FINE), :], deep_sem.at[first // FINE, b]) for b in range(PARTS)]
            keeps.extend(mine)

            def product(first=first, mine=mine):
                for b in range(PARTS):
                    mine[b].start()
                    at = b * OUT_PART + first
                    stages[3].put(nt(up_ref[...], deep_ref[b, first : first + FINE, :]), dno_out.at[:, at : at + FINE])

            products[-1] = product

    for piece in pieces:
        piece.own.start()
    for piece in pieces[:AHEAD]:
        piece.x.start()

    def between(t):
        passing.step(t)
        local.turn(2 * t)
        local.turn(2 * t + 1)

    travel_on(pieces, products, lag=1, between=between)
    for turn in range(2 * (len(pieces) + 2), STEPS * local.blocks):
        local.turn(turn)
    passing.rest(len(pieces) + 2)
    for stage in stages:
        stage.rest()
    incoming_ref[...] = held_ref[...].astype(LOW)
    for keep in keeps:
        keep.wait()


def gates(normed, upstream, state, x, bc, rb, rt, er, ew, d2, e2, weight, out_weight):
    length = upstream.shape[0]
    bits = len(seq_bits())
    vmem, hbm = pl.BlockSpec(memory_space=pltpu.VMEM), pl.BlockSpec(memory_space=pl.ANY)
    dma = pltpu.SemaphoreType.DMA
    return pl.pallas_call(
        gates_kernel,
        in_specs=[vmem] * 11 + [hbm, hbm],
        out_specs=[vmem, vmem] + [hbm] * 5,
        out_shape=[
            jax.ShapeDtypeStruct((NSTATE, DI), LOW),
            jax.ShapeDtypeStruct((8, DI), F32),
            jax.ShapeDtypeStruct((length, DI), F32),
            jax.ShapeDtypeStruct((length // BLOCK, NSTATE, DI), LOW),
            jax.ShapeDtypeStruct((length, DI), LOW),
            jax.ShapeDtypeStruct((length, DI), F32),
            jax.ShapeDtypeStruct((2 * DI, DM), LOW),
        ],
        scratch_shapes=[
            pltpu.VMEM((DI, DM), LOW),
            pltpu.VMEM((PARTS, OUT_PART, DM), LOW),
            pltpu.VMEM((NSTATE, DI), F32),
            pltpu.VMEM((8, DI), F32),
            pltpu.VMEM((8, DI), F32),
            pltpu.VMEM((NSTATE, DI), F32),
            pltpu.VMEM((NSTATE + 16, DI), LOW),
            pltpu.VMEM((bits, NSTATE + 16, DI), LOW),
            pltpu.VMEM((NSTATE, WIDE), F32),
            pltpu.VMEM((2, BLOCK, WIDE), F32),
            pltpu.VMEM((2, NSTATE, WIDE), LOW),
            pltpu.VMEM((2, length, FINE), LOW),
            pltpu.VMEM((2, length, FINE), F32),
            dma((bits, STEPS)),
            dma((bits, STEPS)),
            dma((OUT_PART // FINE, PARTS)),
            dma((4, 2)),
        ]
        + gather_sems(DI // TILE + OUT_PART // SHORT),
        compiler_params=pltpu.CompilerParams(vmem_limit_bytes=58 << 20, collective_id=1, has_side_effects=True),
        cost_estimate=pl.CostEstimate(flops=50 << 30, bytes_accessed=50 << 20, transcendentals=0),
        name="gates",
    )(normed, upstream, state, x, bc, rb, rt, er, ew, d2, e2, weight, out_weight)


def seq_bits():
    bits, bit = [], 1
    while bit < lax.axis_size("seq"):
        bits.append(bit)
        bit *= 2
    return bits


ROWS = 128
LEAST = 16


class Reducer:
    def __init__(self, out, gate, conv, din, dout, held, core, sx, rx, near, res, blank, load_sem, keep_sem, send_sem, recv_sem, all_sem, parts):
        self.out, self.gate, self.conv, self.din, self.dout = out, gate, conv, din, dout
        self.held, self.core, self.sx, self.rx, self.near, self.res = held, core, sx, rx, near, res
        self.load_sem, self.keep_sem, self.send_sem, self.recv_sem, self.parts = load_sem, keep_sem, send_sem, recv_sem, parts
        self.blank, self.all_sem = blank, all_sem
        bits = seq_bits()
        seq = lax.axis_index("seq")
        self.steps = len(bits)
        self.halved = halved_bits()
        self.partners = [across_bit("wt", 1), across_bit("wt", 2)] + [across_bit("seq", bit) for bit in bits]
        self.second = [(seq // bit) % 2 for bit in bits]
        self.bases, self.sizes = [0], [ROWS]
        for bit in bits[: self.halved]:
            size = self.sizes[-1] // 2
            self.bases.append(self.bases[-1] + ((seq // bit) % 2) * size)
            self.sizes.append(size)
        self.stages = 2 + self.steps + self.halved
        self.out_count = PARTS * (OUT_PART // ROWS)
        self.gate_count = DI // ROWS
        self.columns = CDIM + HEADS
        self.count = self.out_count + self.gate_count + -(-self.columns // ROWS)
        self.total = self.count + SLACK * self.stages + 1

    def rows_at(self, j):
        return pl.ds(pl.multiple_of(self.bases[j], LEAST), self.sizes[j])

    def kinds(self, c, act):
        first_gate, first_conv = self.out_count, self.out_count + self.gate_count

        @pl.when(c < first_gate)
        def _():
            first = pl.multiple_of((c // PARTS) * ROWS, 16)
            columns = pl.ds(pl.multiple_of((c % PARTS) * PART, LANES), PART)
            act([self.out.at[pl.ds(b * OUT_PART + first, ROWS), columns] for b in range(PARTS)], lambda: self.dout.at[pl.ds(first, ROWS), columns])

        @pl.when(jnp.logical_and(c >= first_gate, c < first_conv))
        def _():
            first = pl.multiple_of((c - first_gate) * ROWS, 16)
            act([self.gate.at[pl.ds(first, ROWS), :]], lambda: self.din.at[pl.ds(first, ROWS), :])

        @pl.when(c >= first_conv)
        def _():
            first = pl.multiple_of(jnp.minimum((c - first_conv) * ROWS, self.columns - ROWS), 16)
            act([self.conv.at[pl.ds(first, ROWS), :]], lambda: self.din.at[pl.ds(DI + first, ROWS), :])

    def load(self, c):
        few = lax.rem(c, FEW)

        def act(sources, target):
            width = DM // len(sources)
            for b, source in enumerate(sources):
                pltpu.make_async_copy(source, self.held.at[few, :, b * width : (b + 1) * width], self.load_sem.at[few]).start()

        self.kinds(c, act)

    def exchange(self, s, slot, few, group=None):
        if s == 0:
            source, target = self.held.at[few, :, 2 * PART :], self.core.at[few]
        elif s == 1:
            source, target = self.sx.at[few], self.rx.at[few]
        elif s < 2 + self.steps:
            source, target = self.parts[3 * (s - 2)].at[few], self.parts[3 * (s - 2) + 1].at[few]
        else:
            j = self.stages - 1 - s
            source = target = self.res.at[slot, self.rows_at(j + 1), :]
        partner = self.partners[s] if s < 2 + self.steps else self.partners[2 + self.stages - 1 - s]
        send, recv = self.send_sem.at[s, few], self.recv_sem.at[s, few]
        if group is not None:
            send, recv = self.all_sem.at[0, group], self.all_sem.at[1, group]
        return pltpu.make_async_remote_copy(src_ref=source, dst_ref=target, send_sem=send, recv_sem=recv, device_id=partner, device_id_type=MESH)

    def grouped(self, t):
        return jnp.logical_and(t >= SLACK * (self.stages - 1), t < self.count)

    def all_done(self, t):
        group = lax.rem(t, FEW)
        for i in range(2):
            pltpu.make_async_copy(self.blank, self.blank, self.all_sem.at[i, group]).wait()

    def loaded(self, few):
        pltpu.make_async_copy(self.gate.at[0:ROWS, :], self.held.at[few], self.load_sem.at[few]).wait()

    def kept(self, slot):
        return pltpu.make_async_copy(self.res.at[slot], self.din.at[0:ROWS, :], self.keep_sem.at[slot])

    def combine(self, s, slot, few):
        if s == 0:
            self.near[few] = self.held[few, :, :PART].astype(F32) + self.core[few, :, :PART].astype(F32)
            self.sx[few] = (self.held[few, :, PART : 2 * PART].astype(F32) + self.core[few, :, PART:].astype(F32)).astype(LOW)
        elif s == 1:
            self.lay(self.near[few] + self.rx[few].astype(F32), 0, slot, few)
        elif s < 2 + self.steps:
            j = s - 2
            mine = self.parts[3 * j + 2][few] if j < self.halved else self.parts[3 * j][few].astype(F32)
            self.lay(mine + self.parts[3 * j + 1][few].astype(F32), j + 1, slot, few)

    def lay(self, value, j, slot, few):
        if j == self.steps:
            self.res[slot, self.rows_at(self.halved), :] = value.astype(LOW)
        elif j < self.halved:
            size = self.sizes[j + 1]
            low, high = value[:size], value[size:]
            second = self.second[j] == 1
            self.parts[3 * j][few] = jnp.where(second, low, high).astype(LOW)
            self.parts[3 * j + 2][few] = jnp.where(second, high, low)
        else:
            self.parts[3 * j][few] = value.astype(LOW)

    def write(self, c, slot):
        self.kinds(c, lambda sources, target: pltpu.make_async_copy(self.res.at[slot], target(), self.keep_sem.at[slot]).start())

    def step(self, t):
        steady = jnp.logical_and(t > SLACK * self.stages, t < self.count)

        @pl.when(steady)
        def _():
            slots = [(lax.rem(t - SLACK * s, SLOTS), lax.rem(t - SLACK * s, FEW)) for s in range(self.stages + 1)]
            self.kept(lax.rem(t - SLACK * self.stages - 1, SLOTS)).wait()
            self.all_done(t - SLACK)
            self.loaded(slots[0][1])
            for s in range(self.stages, 0, -1):
                self.combine(s - 1, *slots[s])
            group = lax.rem(t, FEW)
            for s in range(1, self.stages):
                self.exchange(s, *slots[s], group).start()
            self.exchange(0, *slots[0], group).start()
            self.write(t - SLACK * self.stages, slots[self.stages][0])

        @pl.when(jnp.logical_not(steady))
        def _():
            c = t - SLACK * self.stages - 1

            @pl.when(jnp.logical_and(c >= 0, c < self.count))
            def _():
                self.kept(lax.rem(c, SLOTS)).wait()

            were, are = self.grouped(t - SLACK), self.grouped(t)

            @pl.when(were)
            def _():
                self.all_done(t - SLACK)

            for s in range(self.stages, -1, -1):
                c = t - SLACK * s

                @pl.when(jnp.logical_and(c >= 0, c < self.count))
                def _(c=c, s=s):
                    slot, few = lax.rem(c, SLOTS), lax.rem(c, FEW)
                    if s > 0:

                        @pl.when(jnp.logical_not(were))
                        def _():
                            self.exchange(s - 1, slot, few).wait()

                        self.combine(s - 1, slot, few)
                    else:
                        self.loaded(few)
                    if s < self.stages:

                        @pl.when(are)
                        def _():
                            self.exchange(s, slot, few, lax.rem(t, FEW)).start()

                        @pl.when(jnp.logical_not(are))
                        def _():
                            self.exchange(s, slot, few).start()

                    else:
                        self.write(c, slot)

        @pl.when(t + 1 < self.count)
        def _():
            self.load(t + 1)


def halved_bits():
    count, rows = 0, ROWS
    while count < len(seq_bits()) and rows > LEAST:
        count, rows = count + 1, rows // 2
    return count


BLOCKS = 4
PER = 2
HALF = BLOCKS // PER
TURNS = HALF + 1
FILL_STEPS, NEAR_STEPS, BACK_STEPS, EDGE_STEPS, GATE_STEPS = STEPS, STEPS * HALF, STEPS * TURNS + 1, 1, STEPS
NEAR_AT = FILL_STEPS
BACK_AT = NEAR_AT + NEAR_STEPS
EDGE_AT = BACK_AT + BACK_STEPS
PULL_AT = EDGE_AT + EDGE_STEPS
DOT_STEPS = STEPS + 1
PULL_STEPS = 2 * GATE_STEPS + DOT_STEPS
LAST_AT = PULL_AT + PULL_STEPS
ALL_STEPS = LAST_AT + 1
PACE = ((1, FILL_STEPS - 1, 9), (NEAR_AT, NEAR_STEPS, 17), (BACK_AT, BACK_STEPS, 26), (EDGE_AT, EDGE_STEPS, 3), (PULL_AT, PULL_STEPS, 24))
DONE = sum(turns for _, _, turns in PACE)


def clip(v, low, high):
    return jnp.minimum(jnp.maximum(v, low), high)


def paced(g):
    done = 0
    for first, steps, turns in PACE:
        done = done + (turns * clip(g - first, 0, steps)) // steps
    return done


def head_block(g):
    near = clip(g - NEAR_AT, 0, NEAR_STEPS) // HALF
    over = near // STEPS
    return near * (1 - over) + over * clip((g - BACK_AT) // TURNS, 0, STEPS - 1)


def gate_block(g):
    over = clip(g - FILL_STEPS + 1, 0, 1)
    return jnp.minimum(g, FILL_STEPS - 1) * (1 - over) + over * clip(g - PULL_AT - GATE_STEPS, 0, GATE_STEPS - 1)


def near_block_at(g):
    return jnp.minimum(clip(g - NEAR_AT, 0, NEAR_STEPS) // HALF, STEPS - 1)


def rear_kernel(pc_ref, x_ref, dy_ref, bc_ref, rb_ref, rt_ref, er_ref, ew_ref, d2_ref, ed_ref, dt_ref, e2_ref, et_ref, states_ref, in_ref, taps_ref, skip_ref, heads_ref, met_ref, normed_ref, tok_ref, up_ref, gain_ref, sums_ref, low0_ref, low1_ref, low2_ref, low3_ref, low_ref, dgate_ref, wgate_ref, wconv_ref, din_ref, sum_in_ref, sum_out_ref, small_ref, dtok_ref, mixed_ref, gconv_ref, gout_ref, ggate_ref, pad_ref, dact_ref, dheld_ref, direct_ref, dconv_ref, dscores_ref, dbc_ref, ddt_ref, q_ref, v_ref, ends_ref, crossed_ref, stage_ref, second_ref, rim_ref, rim_got_ref, one_sem, fill_sem, rim_sem, total_ref, factor_ref, reach_ref, held_ref, psend_ref, precv_ref, ps_sem, pr_sem, vsend_ref, vrecv_ref, vs_sem, vr_sem, r_held, r_core, r_sx, r_rx, r_near, r_res, r_blank, load_sem, keep_sem, send_sem, recv_sem, all_sem, *parts):
    g = pl.program_id(0)
    length = x_ref.shape[0]
    seq, peers = lax.axis_index("seq"), lax.axis_size("seq")
    following, previous = {"seq": lax.rem(seq + 1, peers)}, {"seq": lax.rem(seq + peers - 1, peers)}
    reducer = Reducer(gout_ref, ggate_ref, gconv_ref, sum_in_ref, sum_out_ref, r_held, r_core, r_sx, r_rx, r_near, r_res, r_blank, load_sem, keep_sem, send_sem, recv_sem, all_sem, parts)
    passing = Passing(True, total_ref, factor_ref, reach_ref, held_ref, psend_ref, precv_ref, met_ref, ps_sem, pr_sem)
    rounds = len(passing.bits)
    block = head_block(g)

    def columns_of(j):
        return pl.ds(pl.multiple_of(j * WIDE, WIDE), WIDE)

    def edge(j):
        return pltpu.make_async_remote_copy(src_ref=rim_ref.at[:, columns_of(j)], dst_ref=rim_got_ref.at[:, columns_of(j)], send_sem=rim_sem.at[0, j], recv_sem=rim_sem.at[1, j], device_id=previous, device_id_type=MESH)

    @pl.when(g == 0)
    def _():
        greet(reducer.partners + [following, previous])
        first = pltpu.make_async_copy(din_ref, total_ref, one_sem.at[2])
        first.start()
        for ref in (dscores_ref, dbc_ref, ddt_ref, q_ref, v_ref, ends_ref, crossed_ref, held_ref):
            ref[...] = jnp.zeros_like(ref)
        reach_ref[...] = jnp.ones_like(reach_ref)
        factor_ref[0:1, :] = met_ref[7:8, :]
        first.wait()
        for j in range(STEPS):
            passing.start(0, j)

    lows = (low0_ref, low1_ref, low2_ref, low3_ref)

    def filled(i):
        copies = []
        for b in range(PARTS):
            rows = pl.ds(pl.multiple_of(b * OUT_PART + i * ROWS, ROWS), ROWS)
            copies.append(pltpu.make_async_copy(stage_ref.at[b * ROWS : (b + 1) * ROWS, :], gout_ref.at[rows, :], fill_sem.at[b]))
        copies.append(pltpu.make_async_copy(second_ref, ggate_ref.at[columns_of(i), :], fill_sem.at[PARTS]))
        return copies

    @pl.when(jnp.logical_and(g >= 1, g <= FILL_STEPS))
    def _():
        for copy in filled(g - 1):
            copy.wait()

    @pl.when(g < FILL_STEPS)
    def _():
        for b in range(PARTS):
            stage_ref[b * ROWS : (b + 1) * ROWS, :] = tn(lows[b][...], up_ref[...]).astype(LOW)
        second_ref[...] = tn(dgate_ref[...], normed_ref[EDGE:, :]).astype(LOW)
        for copy in filled(g):
            copy.start()

    @pl.when(g == 1)
    def _():
        reducer.load(jnp.int32(0))

    for k in range(rounds - 1):
        since = g - (1 + 2 * k)

        @pl.when(jnp.logical_and(since >= 0, since < STEPS))
        def _(k=k, since=since):
            passing.finish(k, since)

    def near_block(c):
        at = pl.ds(pl.multiple_of(c * BLOCK, BLOCK), BLOCK)
        ids, jds = rows_cols((BLOCK, BLOCK))
        suffix = (ids >= jds).astype(LOW)
        left = lax.broadcasted_iota(jnp.int32, (BLOCK, LANES), 1) < HDIM
        scores = jnp.where(ids <= jds, nt(bc_ref[at, :NSTATE], bc_ref[at, NSTATE:]), 0.0)
        dy = dy_ref[at, :]
        sized = x_ref[at, :].astype(F32) * nn(d2_ref[at, :], e2_ref[...])
        total = jnp.zeros((BLOCK, BLOCK), F32)
        rows = []
        for pair in range(GROUP // 2):
            lanes = slice(pair * LANES, (pair + 1) * LANES)
            piece, dpiece = sized[:, lanes], dy[:, lanes]
            both = jnp.concatenate([jnp.where(left, piece, 0.0), jnp.where(left, 0.0, piece)], axis=0).astype(LOW)
            meets = nn(both, dpiece.T)
            mixed, kept = [], []
            for half in range(2):
                head = 2 * pair + half
                spread = rt_ref[head : head + 1, at] - rb_ref[at, head : head + 1]
                decay = jnp.exp(jnp.minimum(spread, 0.0))
                meet = meets[half * BLOCK : (half + 1) * BLOCK] * decay
                total = total + meet
                mixed.append((scores * decay).astype(LOW))
                kept.append((meet * scores).astype(LOW))
            later = nn(jnp.concatenate(kept, axis=0), suffix)
            for half in range(2):
                one = later[half * BLOCK : (half + 1) * BLOCK]
                rows.append(jnp.sum(jnp.where(ids < jds, one, 0.0), axis=0, keepdims=True))
            none = jnp.zeros_like(dpiece)
            both = jnp.concatenate([jnp.where(left, dpiece, none), jnp.where(left, none, dpiece)], axis=0)
            direct_ref[block, at, lanes] = nn(jnp.concatenate(mixed, axis=1), both)
        dscores_ref[c] += total
        crossed_ref[pl.ds(pl.multiple_of(block * GROUP, GROUP), GROUP), at] = jnp.concatenate(rows, axis=0)

    @pl.when(jnp.logical_and(g >= NEAR_AT, g < BACK_AT))
    def _():
        @pl.loop(0, PER)
        def _(i):
            near_block(((g - NEAR_AT) % HALF) * PER + i)

    turn = g - BACK_AT
    part = turn % TURNS
    going = jnp.logical_and(turn >= 0, turn < STEPS * TURNS)

    @pl.when(jnp.logical_and(going, part == 0))
    def _():
        passing.finish(rounds - 1, block)
        dheld_ref[...] = held_ref[:, passing.columns(block)]

    def back_block(c):
        at = pl.ds(pl.multiple_of(c * BLOCK, BLOCK), BLOCK)
        input_mat, output_mat = bc_ref[at, :NSTATE], bc_ref[at, NSTATE:]
        e2, et = e2_ref[...], et_ref[...]
        grow, leave, size = nn(er_ref[at, :], e2), nn(ew_ref[at, :], e2), nn(d2_ref[at, :], e2)
        prior = pl.ds(pl.multiple_of(jnp.maximum(c * BLOCK - 16, 0), 16), 16)
        reach = nn(ed_ref[prior, :], e2)[15:16, :]
        reach = jnp.where(c == 0, 1.0, reach)
        state = states_ref[c].astype(F32) + reach * in_ref[...].astype(F32)
        state_low = state.astype(LOW)
        x = x_ref[at, :].astype(F32)
        dy = dy_ref[at, :].astype(F32)
        dheld = dheld_ref[...]
        dheld_low = dheld.astype(LOW)
        grown = (dy * grow).astype(LOW)
        pulled = nn(input_mat, dheld_low) * leave
        dbc_ref[at, :NSTATE] += nt((x * size * leave).astype(LOW), dheld_low)
        dbc_ref[at, NSTATE:] += nt(grown, state_low)
        carried = nn(output_mat, state_low) * grow
        q_ref[at, :] += nn((dy * carried).astype(LOW), et)
        v_ref[at, :] += nn((x * pulled).astype(LOW), et)
        last = grow[BLOCK - 1 : BLOCK, :]
        ends = jnp.sum(state * dheld, axis=0, keepdims=True) * last
        ends_ref[c] += nn(jnp.broadcast_to(ends, (16, WIDE)).astype(LOW), et)[:8]
        dheld_ref[...] = dheld * last + tn(output_mat, grown)
        direct = direct_ref[block, at, :] + pulled
        ddt_ref[at, :] += nn((x * direct).astype(LOW), et)
        dact_ref[at, :] = size * direct + skip_ref[0:1, :] * dy

    @pl.when(jnp.logical_and(going, part < HALF))
    def _():
        @pl.loop(0, PER)
        def _(i):
            back_block(BLOCKS - 1 - (part * PER + i))

    @pl.when(turn == STEPS * TURNS)
    def _():
        ids, jds = rows_cols((BLOCK, BLOCK))
        upper = (ids <= jds).astype(F32)
        under = (ids > jds).astype(F32)
        rate = jnp.exp(heads_ref[1:2, :])
        dstep_bias = jnp.zeros((1, LANES), F32)
        ddecay_log = jnp.zeros((1, LANES), F32)
        for c in range(BLOCKS):
            at = slice(c * BLOCK, (c + 1) * BLOCK)
            dscores = jnp.where(ids <= jds, dscores_ref[c], 0.0).astype(LOW)
            dact_ref[at, :NSTATE] = dbc_ref[at, :NSTATE] + nn(dscores, bc_ref[at, NSTATE:])
            dact_ref[at, NSTATE : 2 * NSTATE] = dbc_ref[at, NSTATE:] + tn(dscores, bc_ref[at, :NSTATE])
            dt = dt_ref[at, :]
            ddecay = crossed_ref[:, at].T + exact(upper, q_ref[at, :]) + exact(under, v_ref[at, :] * dt) + ends_ref[c][0:1, :]
            draw = ddt_ref[at, :] - ddecay * rate
            ddecay_log = ddecay_log - jnp.sum(ddecay * dt, axis=0, keepdims=True) * rate
            raw = pc_ref[EDGE + c * BLOCK : EDGE + (c + 1) * BLOCK, 2 * NSTATE : 2 * NSTATE + LANES].astype(F32)
            used = lax.broadcasted_iota(jnp.int32, raw.shape, 1) < HEADS
            draw = draw * jax.nn.sigmoid(jnp.where(used, raw + heads_ref[0:1, :], 0.0))
            dstep_bias = dstep_bias + jnp.sum(draw, axis=0, keepdims=True)
            dact_ref[at, 2 * NSTATE : 2 * NSTATE + LANES] = draw
            dact_ref[at, 2 * NSTATE + LANES :] = jnp.zeros((BLOCK, LANES), F32)
        ends_ref[0] = jnp.broadcast_to(dstep_bias, (8, LANES))
        ends_ref[1] = jnp.broadcast_to(ddecay_log, (8, LANES))

    @pl.when(jnp.logical_or(jnp.logical_and(going, part == HALF), turn == STEPS * TURNS))
    def _():
        here = turn // TURNS
        at = pl.ds(pl.multiple_of(here * WIDE, WIDE), WIDE)
        taps = taps_ref[:, at]
        pad_ref[...] = pc_ref[...].astype(F32)
        summed = taps[CONV : CONV + 1]
        for k in range(CONV):
            first = EDGE - CONV + 1 + k
            summed = summed + taps[k : k + 1] * pad_ref[first : first + length, :]
        shape = jax.nn.sigmoid(summed)
        dsum = dact_ref[0:length, :] * (shape * (1.0 + summed * (1.0 - shape)))
        dtap = [jnp.sum(dsum * pad_ref[EDGE - CONV + 1 + k : EDGE - CONV + 1 + k + length, :], axis=0, keepdims=True) for k in range(CONV)]
        dtap.append(jnp.sum(dsum, axis=0, keepdims=True))
        vsend_ref[0, :, at] = jnp.concatenate(dtap + [jnp.zeros((8 - len(dtap), WIDE), F32)], axis=0)
        rim_ref[:, at] = dsum[:16].astype(LOW)
        keep = dact_ref[0:length, :]
        dact_ref[0:length, :] = dsum
        dact_ref[length:, :] = jnp.zeros_like(dact_ref[length:, :])
        result = taps[CONV - 1 : CONV] * dsum
        for k in range(CONV - 1):
            by = CONV - 1 - k
            result = result + taps[k : k + 1] * dact_ref[by : by + length, :]
        lane = lax.broadcasted_iota(jnp.int32, (1, WIDE), 1)
        raw_part = jnp.logical_and(turn == STEPS * TURNS, lane >= 2 * NSTATE)
        dconv_ref[:, at] = jnp.where(raw_part, keep, result).astype(LOW)

    def stored(k):
        return pltpu.make_async_copy(stage_ref, gconv_ref.at[columns_of(k), :], one_sem.at[2])

    def settle(j):
        edge(j).wait()

        @pl.when(j >= 1)
        def _():
            stored(j - 1).wait()

        at = columns_of(j)
        bottom = slice(length - 16, length)
        got, taps = rim_got_ref[:, at].astype(F32), taps_ref[:, at]
        ids, jds = rows_cols(got.shape)
        extra = jnp.zeros_like(got)
        for i in range(CONV - 1):
            row = sum(taps[k : k + 1] * got[i - k : i - k + 1] for k in range(i + 1))
            extra = jnp.where(ids == 16 - CONV + 1 + i, row, extra)
        takes = jnp.logical_and(jds < CDIM - j * WIDE, seq < peers - 1)
        dconv_ref[bottom, at] = (dconv_ref[bottom, at].astype(F32) + jnp.where(takes, extra, 0.0)).astype(LOW)
        stage_ref[...] = tn(dconv_ref[:, at], normed_ref[EDGE:, :]).astype(LOW)
        stored(j).start()

    convolves = jnp.logical_or(jnp.logical_and(going, part == HALF), turn == STEPS * TURNS)

    @pl.when(convolves)
    def _():
        edge(turn // TURNS).start()

    @pl.when(jnp.logical_or(jnp.logical_and(convolves, turn >= TURNS), g == EDGE_AT))
    def _():
        settle(jnp.where(g == EDGE_AT, STEPS, turn // TURNS - 1))

    @pl.when(g == PULL_AT)
    def _():
        stored(STEPS).wait()

    pull = g - PULL_AT

    thirds = [slice(i * WIDE, (i + 1) * WIDE) for i in range(DM // WIDE)]
    mixed_out = pltpu.make_async_copy(stage_ref, mixed_ref, one_sem.at[2])

    @pl.when(pull == 0)
    def _():
        for i, at in enumerate(thirds):
            direct_ref[i] = tok_ref[:, at].astype(F32)

    @pl.when(jnp.logical_and(pull >= 0, pull < GATE_STEPS))
    def _():
        for i, at in enumerate(thirds):
            direct_ref[i] += nn(low_ref[...], wgate_ref[:, at])

    @pl.when(pull == GATE_STEPS)
    def _():
        for i, at in enumerate(thirds):
            stage_ref[:, at] = direct_ref[i].astype(LOW)
        mixed_out.start()
        direct_ref[0:PARTS] = jnp.zeros_like(direct_ref[0:PARTS])

    def add_pull(left, weight):
        for b in range(PARTS):
            direct_ref[b, :, :PART] += nn(left, weight[:, b * PART : (b + 1) * PART])

    @pl.when(jnp.logical_and(pull >= GATE_STEPS, pull < 2 * GATE_STEPS))
    def _():
        add_pull(dgate_ref[...], wgate_ref[...])

    @pl.when(jnp.logical_and(pull >= 2 * GATE_STEPS, pull < PULL_STEPS))
    def _():
        k = pull - 2 * GATE_STEPS
        columns = pl.ds(pl.multiple_of(k * WIDE, WIDE), WIDE)
        ids = lax.broadcasted_iota(jnp.int32, (WIDE, DM), 0)
        weight = wconv_ref[...]
        weight = jnp.where(ids < CDIM + HEADS - k * WIDE, weight, jnp.zeros_like(weight))
        add_pull(dconv_ref[:, columns], weight)

    def normed_out(b):
        return pltpu.make_async_copy(direct_ref.at[relative(b), :, 0:PART], dtok_ref.at[:, b * PART : (b + 1) * PART], one_sem.at[3 + b])

    meets = len(reducer.partners)

    def swap(k):
        return pltpu.make_async_remote_copy(src_ref=vsend_ref.at[k], dst_ref=vrecv_ref.at[k], send_sem=vs_sem.at[k], recv_sem=vr_sem.at[k], device_id=reducer.partners[k], device_id_type=MESH)

    @pl.when(g == LAST_AT)
    def _():
        blocks = [slice(b * PART, (b + 1) * PART) for b in range(PARTS)]
        square = jnp.zeros((length, 1), F32)
        cross = jnp.zeros((length, 1), F32)
        for b, at in enumerate(blocks):
            u = tok_ref[:, at].astype(F32)
            square = square + jnp.sum(u * u, axis=1, keepdims=True)
            cross = cross + jnp.sum(direct_ref[relative(b), :, :PART] * gain_ref[0:1, at] * u, axis=1, keepdims=True)
        rate = lax.rsqrt(square * (1.0 / DM) + EPS)
        pulled = rate * rate * rate * (cross * (1.0 / DM))
        for b, at in enumerate(blocks):
            u = tok_ref[:, at].astype(F32)
            there = relative(b)
            d_normed = direct_ref[there, :, :PART]
            vsend_ref[0, 5:6, at] = jnp.sum(d_normed * (u * rate), axis=0, keepdims=True)
            direct_ref[there, :, :PART] = up_ref[:, at].astype(F32) + rate * (d_normed * gain_ref[0:1, at]) - u * pulled
            normed_out(b).start()
        vsend_ref[0, 6:7, :DI] = sums_ref[0:1, :]
        vsend_ref[0, 7:8, :DI] = sums_ref[1:2, :]
        vsend_ref[0, 6:7, DI : DI + LANES] = ends_ref[0][0:1]
        vsend_ref[0, 7:8, DI : DI + LANES] = ends_ref[1][0:1]

        swap(0).start()

    @pl.loop(paced(g), paced(g + 1) + (g // LAST_AT) * (reducer.total - DONE))
    def _(t):
        reducer.step(t)
        for k in range(meets):

            @pl.when(t == DONE + 2 * (k + 1))
            def _(k=k):
                swap(k).wait()
                value = vsend_ref[k] + vrecv_ref[k]
                if k + 1 < meets:
                    vsend_ref[k + 1] = value
                    swap(k + 1).start()
                else:
                    small_ref[...] = value

    @pl.when(g == LAST_AT)
    def _():
        for b in range(PARTS):
            normed_out(b).wait()
        mixed_out.wait()


def rear(proj, x, dy, bc, rb, rt, er, ew, d2, ed, dt, e2, et, states, incoming, taps, skip, heads, met, normed, tokens, upstream, gain, sums, low, dgate, wide_all, conv_all, din):
    length = x.shape[0]
    bits, halved = len(seq_bits()), halved_bits()
    hbm = pl.BlockSpec(memory_space=pl.ANY)
    back_block = lambda g: clip((g - BACK_AT) // TURNS, 0, STEPS)
    part_block = lambda g: clip((g - BACK_AT) // TURNS, 0, STEPS - 1)

    def whole(array):
        return pl.BlockSpec(array.shape, lambda g: (0,) * array.ndim, pipeline_mode=pl.Buffered(1))

    shares = []
    for j in range(bits):
        shape = (FEW, max(ROWS >> (j + 1), LEAST), PART)
        shares += [pltpu.VMEM(shape, LOW), pltpu.VMEM(shape, LOW), pltpu.VMEM(shape, F32)]
    dma = pltpu.SemaphoreType.DMA
    stages, meets = 2 + bits + halved, 2 + bits
    moved = 3 * ROWS + 2 * sum(ROWS >> (j + 1) for j in range(halved)) + LEAST * (bits - halved)
    return pl.pallas_call(
        rear_kernel,
        grid=(ALL_STEPS,),
        in_specs=[
            pl.BlockSpec((length + EDGE, WIDE), lambda g: (0, back_block(g))),
            pl.BlockSpec((length, WIDE), lambda g: (0, head_block(g))),
            pl.BlockSpec((length, WIDE), lambda g: (0, head_block(g))),
            whole(bc),
            pl.BlockSpec((length, LANES), lambda g: (0, near_block_at(g))),
            pl.BlockSpec((GROUP, length), lambda g: (near_block_at(g), 0)),
            whole(er),
            whole(ew),
            whole(d2),
            whole(ed),
            whole(dt),
            pl.BlockSpec((2 * LANES, WIDE), lambda g: (0, head_block(g))),
            pl.BlockSpec((WIDE, LANES), lambda g: (part_block(g), 0)),
            pl.BlockSpec((length // BLOCK, NSTATE, WIDE), lambda g: (0, 0, part_block(g))),
            pl.BlockSpec((NSTATE, WIDE), lambda g: (0, part_block(g))),
            whole(taps),
            pl.BlockSpec((8, WIDE), lambda g: (0, part_block(g))),
            whole(heads),
            whole(met),
            whole(normed),
            whole(tokens),
            whole(upstream),
            whole(gain),
            whole(sums),
        ]
        + [pl.BlockSpec((length, ROWS), lambda g, b=b: (0, b * (OUT_PART // ROWS) + jnp.minimum(g, FILL_STEPS - 1))) for b in range(PARTS)]
        + [
            pl.BlockSpec((length, WIDE), lambda g: (0, clip(g - PULL_AT, 0, GATE_STEPS - 1))),
            pl.BlockSpec((length, WIDE), lambda g: (0, gate_block(g))),
            pl.BlockSpec((WIDE, DM), lambda g: ((clip(g - PULL_AT, 0, 2 * GATE_STEPS - 1) + GATE_STEPS) % (2 * GATE_STEPS), 0)),
            pl.BlockSpec((WIDE, DM), lambda g: (clip(g - PULL_AT - 2 * GATE_STEPS, 0, DOT_STEPS - 1), 0)),
            hbm,
        ],
        out_specs=[hbm, hbm, pl.BlockSpec((8, LONG), lambda g: (0, 0)), hbm, hbm, hbm, hbm, hbm],
        out_shape=[
            jax.ShapeDtypeStruct((DI + CDIM + HEADS, PART), LOW),
            jax.ShapeDtypeStruct((OUT_PART, DM), LOW),
            jax.ShapeDtypeStruct((8, LONG), F32),
            jax.ShapeDtypeStruct((length, DM), F32),
            jax.ShapeDtypeStruct((length, DM), LOW),
            jax.ShapeDtypeStruct((LONG, DM), LOW),
            jax.ShapeDtypeStruct((DI, DM), LOW),
            jax.ShapeDtypeStruct((DI, DM), LOW),
        ],
        scratch_shapes=[
            pltpu.VMEM((length + EDGE, WIDE), F32),
            pltpu.VMEM((length + EDGE, WIDE), F32),
            pltpu.VMEM((NSTATE, WIDE), F32),
            pltpu.VMEM((STEPS, length, WIDE), F32),
            pltpu.VMEM((length, LONG), LOW),
            pltpu.VMEM((length // BLOCK, BLOCK, BLOCK), F32),
            pltpu.VMEM((length, 2 * NSTATE), F32),
            pltpu.VMEM((length, LANES), F32),
            pltpu.VMEM((length, LANES), F32),
            pltpu.VMEM((length, LANES), F32),
            pltpu.VMEM((length // BLOCK, 8, LANES), F32),
            pltpu.VMEM((LANES, length), F32),
            pltpu.VMEM((WIDE, DM), LOW),
            pltpu.VMEM((WIDE, DM), LOW),
            pltpu.VMEM((16, LONG), LOW),
            pltpu.VMEM((16, LONG), LOW),
            dma((3 + PARTS,)),
            dma((PARTS + 1,)),
            dma((2, STEPS + 1)),
            pltpu.VMEM((NSTATE, DI), F32),
            pltpu.VMEM((8, DI), F32),
            pltpu.VMEM((8, DI), F32),
            pltpu.VMEM((NSTATE, DI), F32),
            pltpu.VMEM((NSTATE, DI), LOW),
            pltpu.VMEM((bits, NSTATE, DI), LOW),
            dma((bits, STEPS)),
            dma((bits, STEPS)),
            pltpu.VMEM((meets, 8, LONG), F32),
            pltpu.VMEM((meets, 8, LONG), F32),
            dma((meets,)),
            dma((meets,)),
            pltpu.VMEM((FEW, ROWS, DM), LOW),
            pltpu.VMEM((FEW, ROWS, 2 * PART), LOW),
            pltpu.VMEM((FEW, ROWS, PART), LOW),
            pltpu.VMEM((FEW, ROWS, PART), LOW),
            pltpu.VMEM((FEW, ROWS, PART), F32),
            pltpu.VMEM((SLOTS, ROWS, PART), LOW),
            pltpu.VMEM((moved, PART), LOW),
            dma((FEW,)),
            dma((SLOTS,)),
            dma((stages, FEW)),
            dma((stages, FEW)),
            dma((2, FEW)),
        ]
        + shares,
        compiler_params=pltpu.CompilerParams(vmem_limit_bytes=62 << 20, collective_id=2, has_side_effects=True),
        cost_estimate=pl.CostEstimate(flops=200 << 30, bytes_accessed=60 << 20, transcendentals=0),
        name="rear",
    )(proj, x, dy, bc, rb, rt, er, ew, d2, ed, dt, e2, et, states, incoming, taps, skip, heads, met, normed, tokens, upstream, gain, sums, low, low, low, low, low, dgate, wide_all, conv_all, din)


def shards(tokens, norm_gain, in_weight, conv_kernel, conv_bias, step_bias, decay_log, skip_gain, out_gain, out_weight, cotangent):
    length = tokens.shape[1]
    own, upstream = tokens[0], cotangent[0]
    turned = in_weight.T
    gain = norm_gain[None]
    skip = jnp.repeat(skip_gain, HDIM)[None]
    gains = jnp.concatenate([out_gain[None], skip, jnp.zeros((6, DI), F32)], axis=0)
    skip = jnp.broadcast_to(skip, (8, DI))
    lanes = np.arange(DI) // HDIM
    e2 = jnp.asarray((np.arange(2 * LANES)[:, None] % LANES == lanes[None]).astype(LOW))
    et = jnp.asarray((lanes[:, None] == np.arange(LANES)[None]).astype(LOW))

    taps, heads, proj, normed, x, bc, dt, rb, rt, er, ew, d2, ed, state, conv_all = enter(own, gain, conv_kernel, conv_bias[None], step_bias[None], decay_log[None], e2, turned)
    incoming, met, y, states, gate, dno, wide_all = gates(normed, upstream, state, x, bc, rb, rt, er, ew, d2, e2, turned, out_weight)
    low, dy, dgate, sums, din = middle(y, bc, incoming, ed, e2, x, gate, dno, gains, length)

    sum_in, sum_out, small, d_tokens, mixed, *_ = rear(proj, x, dy, bc, rb, rt, er, ew, d2, ed, dt, e2, et, states, incoming, taps, skip, heads, met, normed, own, upstream, gain, sums, low, dgate, wide_all, conv_all, din)
    return (
        mixed[None],
        d_tokens[None],
        small[5, :DM],
        sum_in.astype(F32).T,
        small[:CONV, :CDIM],
        small[CONV, :CDIM],
        small[6, DI : DI + HEADS],
        small[7, DI : DI + HEADS],
        jnp.sum(small[7, :DI].reshape(HEADS, HDIM), axis=1),
        small[6, :DI],
        sum_out.astype(F32),
    )


def solution(mesh):
    spread = P("wt", "seq", None)
    return jax.shard_map(
        shards,
        mesh=mesh,
        in_specs=(spread, P(), P("wt", None), P(), P(), P(), P(), P(), P(), P("wt", None), spread),
        out_specs=(spread, spread, P(), P("wt", None), P(), P(), P(), P(), P(), P(), P("wt", None)),
        check_vma=False,
    )
```

```python
import jax
import jax.numpy as jnp
import numpy as np
from jax import lax
from jax.experimental import pallas as pl
from jax.experimental.pallas import tpu as pltpu
from jax.sharding import PartitionSpec as P

DI = 3072
HEADS = 48
HDIM = 64
NSTATE = 128
CONV = 4
CDIM = 3328
EDGE = 16
BLOCK = 128
GROUP = 8
WIDE = GROUP * HDIM
STEPS = HEADS // GROUP
LONG = (STEPS + 1) * WIDE
LANES = 128
TILE = 512
FINE = 256
SHORT = 128
AHEAD = 4
LAG = 2
LAST = 320
PARTS = 4
DM = 1536
PART = DM // PARTS
OUT_PART = DI // PARTS
SLOTS = 16
FEW = 4
SLACK = 2
MESH = pl.DeviceIdType.MESH

EPS = 1e-05
F32 = jnp.float32
LOW = jnp.bfloat16


def dot(a, b, ca, cb):
    return lax.dot_general(a, b, (((ca,), (cb,)), ((), ())), preferred_element_type=F32)


def nn(a, b):
    return dot(a, b, 1, 0)


def nt(a, b):
    return dot(a, b, 1, 1)


def tn(a, b):
    return dot(a, b, 0, 0)


def exact(a, b):
    return jnp.dot(a, b, precision=lax.Precision.HIGHEST, preferred_element_type=F32)


def halves(v):
    high = v.astype(LOW)
    return jnp.concatenate([high, (v - high.astype(F32)).astype(LOW)], axis=1)


def softplus(v):
    z = jnp.exp(-jnp.abs(v))
    small = z * (1.0 - z * (0.5 - z * (1.0 / 3.0 - z * 0.25)))
    return jnp.maximum(v, 0.0) + jnp.where(z < 0.01, small, jnp.log(1.0 + z))


def rows_cols(shape):
    return (lax.broadcasted_iota(jnp.int32, shape, 0), lax.broadcasted_iota(jnp.int32, shape, 1))


class Begin:
    def __init__(self, proj_ref, taps_ref, heads_ref, e2_ref, x_ref, bc_ref, dt_ref, rb_ref, rt_ref, er_ref, ew_ref, d2_ref, ed_ref, state_ref, pad_ref, wd_ref):
        self.proj, self.taps, self.heads, self.e2 = proj_ref, taps_ref, heads_ref, e2_ref
        self.x, self.bc, self.dt, self.rb, self.rt = x_ref, bc_ref, dt_ref, rb_ref, rt_ref
        self.er, self.ew, self.d2, self.ed, self.state = er_ref, ew_ref, d2_ref, ed_ref, state_ref
        self.pad, self.wd = pad_ref, wd_ref
        self.length = x_ref.shape[0]

    def convolved(self, first, width):
        self.pad[:, :width] = self.proj[:, first : first + width].astype(F32)
        total = self.taps[CONV : CONV + 1, first : first + WIDE]
        for k in range(CONV):
            at = EDGE - CONV + 1 + k
            total = total + self.taps[k : k + 1, first : first + WIDE] * self.pad[at : at + self.length, :]
        return total * jax.nn.sigmoid(total)

    def sizes(self):
        length = self.length
        self.pad[...] = jnp.zeros_like(self.pad)
        act = self.convolved(DI, CDIM + HEADS - DI)
        self.bc[...] = act[:, : 2 * NSTATE].astype(LOW)
        raw = self.pad[EDGE:, 2 * NSTATE : 2 * NSTATE + LANES]
        used = lax.broadcasted_iota(jnp.int32, raw.shape, 1) < HEADS
        dt = jnp.where(used, softplus(jnp.where(used, raw + self.heads[0:1, :], 0.0)), 0.0)
        self.dt[...] = dt
        self.d2[...] = halves(dt)
        decay = -dt * jnp.exp(self.heads[1:2, :])
        ids, jds = rows_cols((BLOCK, BLOCK))
        lower = (ids >= jds).astype(F32)
        before = jnp.zeros((1, LANES), F32)
        whole = []
        for c in range(length // BLOCK):
            at = slice(c * BLOCK, (c + 1) * BLOCK)
            run = exact(lower, decay[at])
            last = run[BLOCK - 1 : BLOCK]
            for j in range(STEPS):
                turned = jnp.concatenate([run[:, GROUP * j :], run[:, : GROUP * j]], axis=1) if j else run
                self.rb[at, j * LANES : (j + 1) * LANES] = turned
            self.rt[:, at] = run.T
            self.er[at, :] = halves(jnp.exp(run))
            self.ew[at, :] = halves(jnp.exp(last - run))
            whole.append(run + before)
            self.ed[at, :] = halves(jnp.exp(run + before))
            before = before + last
        for c in range(length // BLOCK):
            at = slice(c * BLOCK, (c + 1) * BLOCK)
            self.wd[at, :] = halves(jnp.exp(before - whole[c]) * dt[at])

    def block(self, j):
        at = slice(j * WIDE, (j + 1) * WIDE)
        x = self.convolved(j * WIDE, WIDE).astype(LOW)
        self.x[:, at] = x
        e2 = self.e2[:, at]
        weighed = (x.astype(F32) * nn(self.wd[...], e2)).astype(LOW)
        self.state[0:NSTATE, at] = tn(self.bc[:, :NSTATE], weighed).astype(LOW)
        decay = nn(self.ed[self.length - 16 : self.length, :], e2)[15:16, :]
        high = decay.astype(LOW).astype(F32)
        ids = lax.broadcasted_iota(jnp.int32, (16, WIDE), 0)
        self.state[NSTATE : NSTATE + 16, at] = jnp.where(ids == 0, high, jnp.where(ids == 1, decay - high, 0.0)).astype(LOW)


class Stages:
    def __init__(self, ref, sem):
        self.ref, self.sem, self.count = ref, sem, ref.shape[0]
        self.flying = [None] * self.count
        self.turn = 0

    def put(self, value, target):
        at = self.turn % self.count
        if self.flying[at] is not None:
            self.flying[at].wait()
        self.ref[at] = value
        self.flying[at] = pltpu.make_async_copy(self.ref.at[at], target, self.sem.at[at])
        self.flying[at].start()
        self.turn += 1

    def rest(self):
        for one in self.flying:
            if one is not None:
                one.wait()


class Inside:
    def __init__(self, x_ref, bc_ref, rb_ref, rt_ref, er_ref, ew_ref, d2_ref, e2_ref, held_ref, y_out, states_out, ys, states):
        self.x, self.bc, self.rb, self.rt = x_ref, bc_ref, rb_ref, rt_ref
        self.er, self.ew, self.d2, self.e2, self.held = er_ref, ew_ref, d2_ref, e2_ref, held_ref
        self.y_out, self.states_out, self.ys, self.states = y_out, states_out, ys, states
        self.blocks = x_ref.shape[0] // BLOCK

    def turn(self, at):
        if at < STEPS * self.blocks:
            self.block(at // self.blocks, at % self.blocks)

    def block(self, j, c):
        at, own = slice(c * BLOCK, (c + 1) * BLOCK), slice(j * WIDE, (j + 1) * WIDE)
        ids, jds = rows_cols((BLOCK, BLOCK))
        left = lax.broadcasted_iota(jnp.int32, (BLOCK, LANES), 1) < HDIM
        input_mat, output_mat = self.bc[at, :NSTATE], self.bc[at, NSTATE:]
        e2 = self.e2[:, own]
        grow, leave = nn(self.er[at, :], e2), nn(self.ew[at, :], e2)
        x = self.x[at, own].astype(F32) * nn(self.d2[at, :], e2)
        scores = jnp.where(ids >= jds, nt(output_mat, input_mat), 0.0)
        held = self.held[...] if c else jnp.zeros_like(self.held)
        self.states.put(held.astype(LOW), self.states_out.at[c, :, own])
        carried = grow * nn(output_mat, held.astype(LOW))
        parts = []
        for pair in range(GROUP // 2):
            lanes = slice(pair * LANES, (pair + 1) * LANES)
            piece = x[:, lanes]
            mixed = []
            for head in (2 * pair, 2 * pair + 1):
                column = self.rb[at, j * LANES + head : j * LANES + head + 1]
                spread = column - self.rt[j * GROUP + head : j * GROUP + head + 1, at]
                mixed.append((scores * jnp.exp(jnp.minimum(spread, 0.0))).astype(LOW))
            both = jnp.concatenate([jnp.where(left, piece, 0.0), jnp.where(left, 0.0, piece)], axis=0)
            parts.append(nn(jnp.concatenate(mixed, axis=1), both.astype(LOW)) + carried[:, lanes])
        self.ys.put(jnp.concatenate(parts, axis=1), self.y_out.at[at, own])
        self.held[...] = held * grow[BLOCK - 1 : BLOCK, :] + tn(input_mat, (x * leave).astype(LOW))


def middle_kernel(y_ref, bc_ref, in_ref, ed_ref, e2_ref, x_ref, gate_ref, dno_ref, gains_ref, low_ref, dy_ref, dgate_ref, sums_ref, din_ref, out_ref, gated_ref):
    @pl.when(pl.program_id(0) == 0)
    def _():
        sums_ref[...] = jnp.zeros_like(sums_ref)
        din_ref[...] = jnp.zeros_like(din_ref)

    output_mat = bc_ref[:, NSTATE:]
    part = DI // PARTS
    tiles = []
    for j in range(PARTS):
        there = relative(j)
        tiles.append((slice(j * part, (j + 1) * part), pl.ds(pl.multiple_of(there * part, LANES), part)))
    square = jnp.zeros((BLOCK, 1), F32)
    cross = jnp.zeros((BLOCK, 1), F32)
    for at, there in tiles:
        far = nn(ed_ref[...], e2_ref[:, at]) * nn(output_mat, in_ref[:, at])
        out = y_ref[:, at] + far + gains_ref[1:2, at] * x_ref[:, at].astype(F32)
        gate = gate_ref[:, at].astype(F32)
        gated = out * gate * jax.nn.sigmoid(gate)
        out_ref[:, at] = out
        gated_ref[:, at] = gated
        square = square + jnp.sum(gated * gated, axis=1, keepdims=True)
        cross = cross + jnp.sum(gated * (dno_ref[:, there] * gains_ref[0:1, at]), axis=1, keepdims=True)
    scale = lax.rsqrt(square * (1.0 / DI) + EPS)
    pull = scale * scale * scale * (cross * (1.0 / DI))
    for at, there in tiles:
        gate = gate_ref[:, at].astype(F32)
        gated, out, gain = gated_ref[:, at], out_ref[:, at], gains_ref[0:1, at]
        shape = jax.nn.sigmoid(gate)
        unit = gated * scale
        low_ref[:, there] = (unit * gain).astype(LOW)
        dno = dno_ref[:, there]
        dgated = scale * (dno * gain) - gated * pull
        dy = dgated * (gate * shape)
        dy_ref[:, at] = dy.astype(LOW)
        dgate_ref[:, at] = (dgated * out * (shape * (1.0 + gate * (1.0 - shape)))).astype(LOW)
        sums_ref[0:1, at] += jnp.sum(dno * unit, axis=0, keepdims=True)
        sums_ref[1:2, at] += jnp.sum(dy * x_ref[:, at].astype(F32), axis=0, keepdims=True)
        din_ref[:, at] += tn(output_mat, (dy * nn(ed_ref[...], e2_ref[:, at])).astype(LOW))


def middle(y, bc, incoming, ed, e2, x, gate, dno, gains, length):
    rows = lambda c: (c, 0)
    fixed = lambda c: (0, 0)
    return pl.pallas_call(
        middle_kernel,
        grid=(length // BLOCK,),
        in_specs=[
            pl.BlockSpec((BLOCK, DI), rows),
            pl.BlockSpec((BLOCK, 2 * NSTATE), rows),
            pl.BlockSpec((NSTATE, DI), fixed),
            pl.BlockSpec((BLOCK, 2 * LANES), rows),
            pl.BlockSpec((2 * LANES, DI), fixed),
            pl.BlockSpec((BLOCK, DI), rows),
            pl.BlockSpec((BLOCK, DI), rows),
            pl.BlockSpec((BLOCK, DI), rows),
            pl.BlockSpec((8, DI), fixed),
        ],
        out_specs=[
            pl.BlockSpec((BLOCK, DI), rows),
            pl.BlockSpec((BLOCK, DI), rows),
            pl.BlockSpec((BLOCK, DI), rows),
            pl.BlockSpec((8, DI), fixed),
            pl.BlockSpec((NSTATE, DI), fixed),
        ],
        out_shape=[
            jax.ShapeDtypeStruct((length, DI), LOW),
            jax.ShapeDtypeStruct((length, DI), LOW),
            jax.ShapeDtypeStruct((length, DI), LOW),
            jax.ShapeDtypeStruct((8, DI), F32),
            jax.ShapeDtypeStruct((NSTATE, DI), F32),
        ],
        scratch_shapes=[pltpu.VMEM((BLOCK, DI), F32), pltpu.VMEM((BLOCK, DI), F32)],
        compiler_params=pltpu.CompilerParams(vmem_limit_bytes=48 << 20),
        cost_estimate=pl.CostEstimate(flops=12 << 30, bytes_accessed=32 << 20, transcendentals=4 << 20),
        name="middle",
    )(y, bc, incoming, ed, e2, x, gate, dno, gains)


def spot():
    wt, seq = lax.axis_index("wt"), lax.axis_index("seq")
    return wt // 2, wt % 2, seq % 2


def relative(block):
    x, core, _ = spot()
    high, low = block // 2, block % 2
    return 2 * (core + low - 2 * core * low) + (x + high - 2 * x * high)


def across_bit(axis, bit):
    index = lax.axis_index(axis)
    return {axis: index + bit - 2 * bit * ((index // bit) % 2)}


def greet(devices):
    barrier = pltpu.get_barrier_semaphore()
    for device in devices:
        pl.semaphore_signal(barrier, inc=1, device_id=device, device_id_type=MESH)
    pl.semaphore_wait(barrier, len(devices))


class Piece:
    def __init__(self, source, near, mine, pair, twin, half, sems, at, bit):
        part = pl.multiple_of((lax.axis_index("seq") // bit) % 2 * half, 16)
        own, xs, xr, ys, yr, ts, tr, keep = sems
        rows = lambda ref: ref.at[pl.ds(part, half), :]
        self.own = pltpu.make_async_copy(source, mine, own.at[at])
        self.x = self.remote(rows(source), rows(near), xs.at[at], xr.at[at], across_bit("wt", 2))
        self.y = self.remote(rows(near), rows(near), ys.at[at], yr.at[at], across_bit("seq", bit))
        self.twin = self.remote(pair, twin, ts.at[at], tr.at[at], across_bit("wt", 1))

    def remote(self, source, target, send, recv, device):
        return pltpu.make_async_remote_copy(src_ref=source, dst_ref=target, send_sem=send, recv_sem=recv, device_id=device, device_id_type=MESH)


def gather_sems(count):
    return [pltpu.SemaphoreType.DMA((count,)) for _ in range(8)]


def enter_kernel(tok_ref, gain_ref, kernel_ref, bias_ref, step_ref, log_ref, e2_ref, w_ref, taps_ref, heads_ref, proj_ref, normed_ref, x_ref, bc_ref, dt_ref, rb_ref, rt_ref, er_ref, ew_ref, d2_ref, ed_ref, state_ref, all_ref, wide_ref, last_ref, edge_ref, pad_ref, wd_ref, edge_sem, *sems):
    length = tok_ref.shape[0]
    begin = Begin(proj_ref, taps_ref, heads_ref, e2_ref, x_ref, bc_ref, dt_ref, rb_ref, rt_ref, er_ref, ew_ref, d2_ref, ed_ref, state_ref, pad_ref, wd_ref)
    seq, peers = lax.axis_index("seq"), lax.axis_size("seq")
    following, previous = {"seq": lax.rem(seq + 1, peers)}, {"seq": lax.rem(seq + peers - 1, peers)}
    greet([across_bit("wt", 1), across_bit("wt", 2), across_bit("seq", 1), across_bit("seq", 2), following, previous])
    edge = pltpu.make_async_remote_copy(src_ref=tok_ref.at[length - EDGE : length, :], dst_ref=edge_ref, send_sem=edge_sem.at[0], recv_sem=edge_sem.at[1], device_id=following, device_id_type=MESH)
    edge.start()
    count = CDIM // TILE
    pieces, products, keeps = [], [], []

    def add(target, first, rows):
        pieces.append(Piece(w_ref.at[pl.ds(first, rows), :], target.at[:, PART : 2 * PART], target.at[:, :PART], target.at[:, : 2 * PART], target.at[:, 2 * PART :], rows // 2, sems, len(pieces), 1 + len(pieces) % 2))
        products.append(None)

    def multiply(target, columns, skip, then):
        keep = pltpu.make_async_copy(target.at[skip:, :], all_ref.at[columns, :], sems[-1].at[len(keeps)])
        keeps.append(keep)

        def product():
            keep.start()
            proj_ref[:, columns] = nt(normed_ref[...], target[skip:, :]).astype(LOW)
            then()

        products[-1] = product

    add(last_ref, DI + CDIM + HEADS - LAST, LAST)
    multiply(last_ref, slice(count * TILE, CDIM + HEADS), LAST - (CDIM + HEADS - count * TILE), begin.sizes)
    for c in range(count):
        for first in range(c * TILE, (c + 1) * TILE, FINE):
            add(wide_ref.at[first : first + FINE, :], DI + first, FINE)
        multiply(wide_ref.at[c * TILE : (c + 1) * TILE, :], slice(c * TILE, (c + 1) * TILE), 0, lambda c=c: begin.block(c))
    for piece in pieces:
        piece.own.start()
    for piece in pieces[:AHEAD]:
        piece.x.start()

    def norm(v):
        v = v.astype(F32)
        return (v * lax.rsqrt(jnp.mean(v * v, axis=-1, keepdims=True) + EPS) * gain_ref[0:1, :]).astype(LOW)

    def place(at, v):
        for b in range(PARTS):
            normed_ref[at, pl.ds(pl.multiple_of(relative(b) * PART, LANES), PART)] = v[:, b * PART : (b + 1) * PART]

    taps_ref[...] = jnp.zeros_like(taps_ref)
    taps_ref[0:CONV, :CDIM] = kernel_ref[...]
    taps_ref[CONV : CONV + 1, :CDIM] = bias_ref[...]
    heads_ref[...] = jnp.zeros_like(heads_ref)
    heads_ref[0:1, :HEADS] = step_ref[...]
    heads_ref[1:2, :HEADS] = log_ref[...]
    place(slice(EDGE, EDGE + length), norm(tok_ref[...]))
    edge.wait()
    place(slice(0, EDGE), norm(jnp.where(seq == 0, 0.0, edge_ref[...].astype(F32))))
    travel_on(pieces, products)
    for keep in keeps:
        keep.wait()


def arrived(pieces, t, ahead=AHEAD):
    pieces[t].x.wait_recv()
    if t + ahead < len(pieces):
        pieces[t + ahead].x.start()


def travel_on(pieces, products, ahead=AHEAD, lag=LAG, between=None, there=0):
    count = len(pieces)
    for t in range(count + 2 * lag):
        if t < count:
            if t >= there:
                arrived(pieces, t, ahead)
            pieces[t].y.start()
        if 0 <= t - lag < count:
            pieces[t - lag].y.wait_recv()
            pieces[t - lag].own.wait()
            pieces[t - lag].twin.start()
        if 0 <= t - 2 * lag < count:
            pieces[t - 2 * lag].twin.wait_recv()
            if products[t - 2 * lag] is not None:
                products[t - 2 * lag]()
        if between is not None:
            between(t)
    for piece in pieces:
        piece.x.wait_send()
        piece.y.wait_send()
        piece.twin.wait_send()


def enter(tokens, gain, conv_kernel, conv_bias, step_bias, decay_log, e2, weight):
    length, columns = tokens.shape[0], CDIM + HEADS
    vmem, hbm = pl.BlockSpec(memory_space=pltpu.VMEM), pl.BlockSpec(memory_space=pl.ANY)
    shapes = [
        ((8, LONG), F32),
        ((8, LANES), F32),
        ((length + EDGE, columns), LOW),
        ((length + EDGE, DM), LOW),
        ((length, DI), LOW),
        ((length, 2 * NSTATE), LOW),
        ((length, LANES), F32),
        ((length, LANES * STEPS), F32),
        ((LANES, length), F32),
        ((length, 2 * LANES), LOW),
        ((length, 2 * LANES), LOW),
        ((length, 2 * LANES), LOW),
        ((length, 2 * LANES), LOW),
        ((NSTATE + 16, DI), LOW),
        ((columns, DM), LOW),
    ]
    return pl.pallas_call(
        enter_kernel,
        in_specs=[vmem] * 7 + [hbm],
        out_specs=[vmem] * (len(shapes) - 1) + [hbm],
        out_shape=[jax.ShapeDtypeStruct(shape, kind) for shape, kind in shapes],
        scratch_shapes=[
            pltpu.VMEM((CDIM // TILE * TILE, DM), LOW),
            pltpu.VMEM((LAST, DM), LOW),
            pltpu.VMEM((EDGE, DM), LOW),
            pltpu.VMEM((length + EDGE, WIDE), F32),
            pltpu.VMEM((length, 2 * LANES), LOW),
            pltpu.SemaphoreType.DMA((2,)),
        ]
        + gather_sems(CDIM // TILE * (TILE // FINE) + 1),
        compiler_params=pltpu.CompilerParams(vmem_limit_bytes=56 << 20, collective_id=0, has_side_effects=True),
        cost_estimate=pl.CostEstimate(flops=40 << 30, bytes_accessed=30 << 20, transcendentals=0),
        name="enter",
    )(tokens, gain, conv_kernel, conv_bias, step_bias, decay_log, e2, weight)


class Passing:
    def __init__(self, later, total, factor, reach, held, send, recv, met, send_sem, recv_sem):
        self.later, self.total, self.factor, self.reach, self.held = later, total, factor, reach, held
        self.send, self.recv, self.met, self.send_sem, self.recv_sem = send, recv, met, send_sem, recv_sem
        self.bits = seq_bits()

    def columns(self, j):
        return pl.ds(pl.multiple_of(j * WIDE, WIDE), WIDE)

    def copy(self, k, j):
        at = self.columns(j)
        return pltpu.make_async_remote_copy(src_ref=self.send.at[:, at], dst_ref=self.recv.at[k, :, at], send_sem=self.send_sem.at[k, j], recv_sem=self.recv_sem.at[k, j], device_id=across_bit("seq", self.bits[k]), device_id_type=MESH)

    def start(self, k, j):
        at = self.columns(j)
        self.send[0:NSTATE, at] = self.total[:, at].astype(LOW)
        if not self.later:
            factor = self.factor[0:1, at]
            high = factor.astype(LOW).astype(F32)
            ids = lax.broadcasted_iota(jnp.int32, (16, WIDE), 0)
            self.send[NSTATE : NSTATE + 16, at] = jnp.where(ids == 0, high, jnp.where(ids == 1, factor - high, 0.0)).astype(LOW)
        self.copy(k, j).start()

    def finish(self, k, j):
        self.copy(k, j).wait()
        at = self.columns(j)
        bit = self.bits[k]
        second = (lax.axis_index("seq") // bit) % 2
        takes = second == (0 if self.later else 1)
        other = self.recv[k, 0:NSTATE, at].astype(F32)
        if self.later:
            met = self.met[k : k + 1, at]
        else:
            rows = self.recv[k, NSTATE : NSTATE + 16, at].astype(F32)
            met = rows[0:1] + rows[1:2]
            self.met[k : k + 1, at] = met
        total, factor, reach = self.total[:, at], self.factor[0:1, at], self.reach[0:1, at]
        self.held[:, at] = self.held[:, at] + jnp.where(takes, reach, 0.0) * other
        self.reach[0:1, at] = jnp.where(takes, reach * met, reach)
        if k + 1 < len(self.bits):
            self.total[:, at] = jnp.where(takes, factor, 1.0) * other + jnp.where(takes, 1.0, met) * total
            self.factor[0:1, at] = factor * met
            self.start(k + 1, j)


def gates_kernel(normed_ref, up_ref, state_ref, x_ref, bc_ref, rb_ref, rt_ref, er_ref, ew_ref, d2_ref, e2_ref, w_ref, o_ref, incoming_ref, met_ref, y_out, states_out, gate_out, dno_out, wall_ref, wide_ref, deep_ref, total_ref, factor_ref, reach_ref, held_ref, send_ref, recv_ref, own_ref, y_ref, states_ref, gate_ref, dno_ref, ss_sem, sr_sem, deep_sem, stage_sem, *sems):
    stages = [Stages(ref, stage_sem.at[i]) for i, ref in enumerate((y_ref, states_ref, gate_ref, dno_ref))]
    local = Inside(x_ref, bc_ref, rb_ref, rt_ref, er_ref, ew_ref, d2_ref, e2_ref, own_ref, y_out, states_out, stages[0], stages[1])
    greet([across_bit("wt", 1), across_bit("wt", 2)] + [across_bit("seq", bit) for bit in seq_bits()])
    passing = Passing(False, total_ref, factor_ref, reach_ref, held_ref, send_ref, recv_ref, met_ref, ss_sem, sr_sem)
    total_ref[...] = state_ref[0:NSTATE, :].astype(F32)
    rows = state_ref[NSTATE : NSTATE + 16, :].astype(F32)
    factor_ref[0:1, :] = rows[0:1] + rows[1:2]
    reach_ref[...] = jnp.ones_like(reach_ref)
    held_ref[...] = jnp.zeros_like(held_ref)
    met_ref[...] = jnp.zeros_like(met_ref)
    met_ref[7:8, :] = factor_ref[0:1, :]
    for j in range(STEPS):
        passing.start(0, j)
    pieces, products, keeps = [], [], []

    for c in range(DI // TILE):
        rows = slice(c * TILE, (c + 1) * TILE)
        target = wide_ref.at[rows, :]
        pieces.append(Piece(w_ref.at[rows, :], target.at[:, PART : 2 * PART], target.at[:, :PART], target.at[:, : 2 * PART], target.at[:, 2 * PART :], TILE // 2, sems, len(pieces), 1 + len(pieces) % 3 // 2))
        keeps.append(pltpu.make_async_copy(target, wall_ref.at[rows, :], sems[-1].at[c]))

        def product(rows=rows, keep=keeps[-1]):
            keep.start()
            for first in (rows.start, rows.start + FINE):
                at = slice(first, first + FINE)
                stages[2].put(nt(normed_ref[EDGE:, :], wide_ref[at, :]).astype(LOW), gate_out.at[:, at])

        products.append(product)

    for c in range(OUT_PART // SHORT):
        rows = slice(c * SHORT, (c + 1) * SHORT)
        pieces.append(Piece(o_ref.at[rows, :], deep_ref.at[1, rows, :], deep_ref.at[0, rows, :], deep_ref.at[0:2, rows, :], deep_ref.at[2:4, rows, :], SHORT // 2, sems, len(pieces), 1 + len(pieces) % 3 // 2))
        products.append(None)
        if (c + 1) * SHORT % FINE == 0:
            first = (c + 1) * SHORT - FINE
            mine = [pltpu.make_async_copy(deep_ref.at[b, first : first + FINE, :], wall_ref.at[pl.ds(DI + b * OUT_PART + first, FINE), :], deep_sem.at[first // FINE, b]) for b in range(PARTS)]
            keeps.extend(mine)

            def product(first=first, mine=mine):
                for b in range(PARTS):
                    mine[b].start()
                    at = b * OUT_PART + first
                    stages[3].put(nt(up_ref[...], deep_ref[b, first : first + FINE, :]), dno_out.at[:, at : at + FINE])

            products[-1] = product

    for piece in pieces:
        piece.own.start()
    for piece in pieces[:AHEAD]:
        piece.x.start()

    last = len(passing.bits) - 1
    first_pieces = {2: 0, 4: 1, 5: 2, 7: 3}
    turns = iter(range(STEPS * local.blocks))
    for m in range(STEPS + 2 * (last - 1)):
        for k in range(last):
            if 0 <= m - 2 * k < STEPS:
                passing.finish(k, m - 2 * k)
        if m in first_pieces:
            arrived(pieces, first_pieces[m])
        for _ in range(2):
            local.turn(next(turns, STEPS * local.blocks))

    def between(t):
        for j, due in enumerate((0, 0, 1, 3, 5, 7)):
            if t == due:
                passing.finish(last, j)
        local.turn(next(turns, STEPS * local.blocks))

    travel_on(pieces, products, between=between, there=len(first_pieces))
    for turn in turns:
        local.turn(turn)
    incoming_ref[...] = held_ref[...].astype(LOW)
    for stage in stages:
        stage.rest()
    for keep in keeps:
        keep.wait()


def gates(normed, upstream, state, x, bc, rb, rt, er, ew, d2, e2, weight, out_weight):
    length = upstream.shape[0]
    bits = len(seq_bits())
    vmem, hbm = pl.BlockSpec(memory_space=pltpu.VMEM), pl.BlockSpec(memory_space=pl.ANY)
    dma = pltpu.SemaphoreType.DMA
    return pl.pallas_call(
        gates_kernel,
        in_specs=[vmem] * 11 + [hbm, hbm],
        out_specs=[vmem, vmem] + [hbm] * 5,
        out_shape=[
            jax.ShapeDtypeStruct((NSTATE, DI), LOW),
            jax.ShapeDtypeStruct((8, DI), F32),
            jax.ShapeDtypeStruct((length, DI), F32),
            jax.ShapeDtypeStruct((length // BLOCK, NSTATE, DI), LOW),
            jax.ShapeDtypeStruct((length, DI), LOW),
            jax.ShapeDtypeStruct((length, DI), F32),
            jax.ShapeDtypeStruct((2 * DI, DM), LOW),
        ],
        scratch_shapes=[
            pltpu.VMEM((DI, DM), LOW),
            pltpu.VMEM((PARTS, OUT_PART, DM), LOW),
            pltpu.VMEM((NSTATE, DI), F32),
            pltpu.VMEM((8, DI), F32),
            pltpu.VMEM((8, DI), F32),
            pltpu.VMEM((NSTATE, DI), F32),
            pltpu.VMEM((NSTATE + 16, DI), LOW),
            pltpu.VMEM((bits, NSTATE + 16, DI), LOW),
            pltpu.VMEM((NSTATE, WIDE), F32),
            pltpu.VMEM((2, BLOCK, WIDE), F32),
            pltpu.VMEM((2, NSTATE, WIDE), LOW),
            pltpu.VMEM((2, length, FINE), LOW),
            pltpu.VMEM((2, length, FINE), F32),
            dma((bits, STEPS)),
            dma((bits, STEPS)),
            dma((OUT_PART // FINE, PARTS)),
            dma((4, 2)),
        ]
        + gather_sems(DI // TILE + OUT_PART // SHORT),
        compiler_params=pltpu.CompilerParams(vmem_limit_bytes=58 << 20, collective_id=1, has_side_effects=True),
        cost_estimate=pl.CostEstimate(flops=50 << 30, bytes_accessed=50 << 20, transcendentals=0),
        name="gates",
    )(normed, upstream, state, x, bc, rb, rt, er, ew, d2, e2, weight, out_weight)


def seq_bits():
    bits, bit = [], 1
    while bit < lax.axis_size("seq"):
        bits.append(bit)
        bit *= 2
    return bits


ROWS = 128
LEAST = 16


class Reducer:
    def __init__(self, out, gate, conv, din, dout, held, core, sx, rx, near, res, blank, load_sem, keep_sem, send_sem, recv_sem, all_sem, parts):
        self.out, self.gate, self.conv, self.din, self.dout = out, gate, conv, din, dout
        self.held, self.core, self.sx, self.rx, self.near, self.res = held, core, sx, rx, near, res
        self.load_sem, self.keep_sem, self.send_sem, self.recv_sem, self.parts = load_sem, keep_sem, send_sem, recv_sem, parts
        self.blank, self.all_sem = blank, all_sem
        bits = seq_bits()
        seq = lax.axis_index("seq")
        self.steps = len(bits)
        self.halved = halved_bits()
        self.partners = [across_bit("wt", 1), across_bit("wt", 2)] + [across_bit("seq", bit) for bit in bits]
        self.second = [(seq // bit) % 2 for bit in bits]
        self.bases, self.sizes = [0], [ROWS]
        for bit in bits[: self.halved]:
            size = self.sizes[-1] // 2
            self.bases.append(self.bases[-1] + ((seq // bit) % 2) * size)
            self.sizes.append(size)
        self.stages = 2 + self.steps + self.halved
        self.out_count = PARTS * (OUT_PART // ROWS)
        self.gate_count = DI // ROWS
        self.columns = CDIM + HEADS
        self.count = self.out_count + self.gate_count + -(-self.columns // ROWS)
        self.total = self.count + SLACK * self.stages + 1

    def rows_at(self, j):
        return pl.ds(pl.multiple_of(self.bases[j], LEAST), self.sizes[j])

    def kinds(self, c, act):
        first_gate, first_conv = self.out_count, self.out_count + self.gate_count

        @pl.when(c < first_gate)
        def _():
            first = pl.multiple_of((c // PARTS) * ROWS, 16)
            columns = pl.ds(pl.multiple_of((c % PARTS) * PART, LANES), PART)
            act([self.out.at[pl.ds(b * OUT_PART + first, ROWS), columns] for b in range(PARTS)], lambda: self.dout.at[pl.ds(first, ROWS), columns])

        @pl.when(jnp.logical_and(c >= first_gate, c < first_conv))
        def _():
            first = pl.multiple_of((c - first_gate) * ROWS, 16)
            act([self.gate.at[pl.ds(first, ROWS), :]], lambda: self.din.at[pl.ds(first, ROWS), :])

        @pl.when(c >= first_conv)
        def _():
            first = pl.multiple_of(jnp.minimum((c - first_conv) * ROWS, self.columns - ROWS), 16)
            act([self.conv.at[pl.ds(first, ROWS), :]], lambda: self.din.at[pl.ds(DI + first, ROWS), :])

    def load(self, c):
        few = lax.rem(c, FEW)

        def act(sources, target):
            width = DM // len(sources)
            for b, source in enumerate(sources):
                pltpu.make_async_copy(source, self.held.at[few, :, b * width : (b + 1) * width], self.load_sem.at[few]).start()

        self.kinds(c, act)

    def exchange(self, s, slot, few, group=None):
        if s == 0:
            source, target = self.held.at[few, :, 2 * PART :], self.core.at[few]
        elif s == 1:
            source, target = self.sx.at[few], self.rx.at[few]
        elif s < 2 + self.steps:
            source, target = self.parts[3 * (s - 2)].at[few], self.parts[3 * (s - 2) + 1].at[few]
        else:
            j = self.stages - 1 - s
            source = target = self.res.at[slot, self.rows_at(j + 1), :]
        partner = self.partners[s] if s < 2 + self.steps else self.partners[2 + self.stages - 1 - s]
        send, recv = self.send_sem.at[s, few], self.recv_sem.at[s, few]
        if group is not None:
            send, recv = self.all_sem.at[0, group], self.all_sem.at[1, group]
        return pltpu.make_async_remote_copy(src_ref=source, dst_ref=target, send_sem=send, recv_sem=recv, device_id=partner, device_id_type=MESH)

    def grouped(self, t):
        return jnp.logical_and(t >= SLACK * (self.stages - 1), t < self.count)

    def all_done(self, t):
        group = lax.rem(t, FEW)
        for i in range(2):
            pltpu.make_async_copy(self.blank, self.blank, self.all_sem.at[i, group]).wait()

    def loaded(self, few):
        pltpu.make_async_copy(self.gate.at[0:ROWS, :], self.held.at[few], self.load_sem.at[few]).wait()

    def kept(self, slot):
        return pltpu.make_async_copy(self.res.at[slot], self.din.at[0:ROWS, :], self.keep_sem.at[slot])

    def combine(self, s, slot, few):
        if s == 0:
            self.near[few] = self.held[few, :, :PART].astype(F32) + self.core[few, :, :PART].astype(F32)
            self.sx[few] = (self.held[few, :, PART : 2 * PART].astype(F32) + self.core[few, :, PART:].astype(F32)).astype(LOW)
        elif s == 1:
            self.lay(self.near[few] + self.rx[few].astype(F32), 0, slot, few)
        elif s < 2 + self.steps:
            j = s - 2
            mine = self.parts[3 * j + 2][few] if j < self.halved else self.parts[3 * j][few].astype(F32)
            self.lay(mine + self.parts[3 * j + 1][few].astype(F32), j + 1, slot, few)

    def lay(self, value, j, slot, few):
        if j == self.steps:
            self.res[slot, self.rows_at(self.halved), :] = value.astype(LOW)
        elif j < self.halved:
            size = self.sizes[j + 1]
            low, high = value[:size], value[size:]
            second = self.second[j] == 1
            self.parts[3 * j][few] = jnp.where(second, low, high).astype(LOW)
            self.parts[3 * j + 2][few] = jnp.where(second, high, low)
        else:
            self.parts[3 * j][few] = value.astype(LOW)

    def write(self, c, slot):
        self.kinds(c, lambda sources, target: pltpu.make_async_copy(self.res.at[slot], target(), self.keep_sem.at[slot]).start())

    def step(self, t):
        steady = jnp.logical_and(t > SLACK * self.stages, t < self.count)

        @pl.when(steady)
        def _():
            slots = [(lax.rem(t - SLACK * s, SLOTS), lax.rem(t - SLACK * s, FEW)) for s in range(self.stages + 1)]
            self.kept(lax.rem(t - SLACK * self.stages - 1, SLOTS)).wait()
            self.all_done(t - SLACK)
            self.loaded(slots[0][1])
            for s in range(self.stages, 0, -1):
                self.combine(s - 1, *slots[s])
            group = lax.rem(t, FEW)
            for s in range(1, self.stages):
                self.exchange(s, *slots[s], group).start()
            self.exchange(0, *slots[0], group).start()
            self.write(t - SLACK * self.stages, slots[self.stages][0])

        @pl.when(jnp.logical_not(steady))
        def _():
            c = t - SLACK * self.stages - 1

            @pl.when(jnp.logical_and(c >= 0, c < self.count))
            def _():
                self.kept(lax.rem(c, SLOTS)).wait()

            were, are = self.grouped(t - SLACK), self.grouped(t)

            @pl.when(were)
            def _():
                self.all_done(t - SLACK)

            for s in range(self.stages, -1, -1):
                c = t - SLACK * s

                @pl.when(jnp.logical_and(c >= 0, c < self.count))
                def _(c=c, s=s):
                    slot, few = lax.rem(c, SLOTS), lax.rem(c, FEW)
                    if s > 0:

                        @pl.when(jnp.logical_not(were))
                        def _():
                            self.exchange(s - 1, slot, few).wait()

                        self.combine(s - 1, slot, few)
                    else:
                        self.loaded(few)
                    if s < self.stages:

                        @pl.when(are)
                        def _():
                            self.exchange(s, slot, few, lax.rem(t, FEW)).start()

                        @pl.when(jnp.logical_not(are))
                        def _():
                            self.exchange(s, slot, few).start()

                    else:
                        self.write(c, slot)

        @pl.when(t + 1 < self.count)
        def _():
            self.load(t + 1)


def halved_bits():
    count, rows = 0, ROWS
    while count < len(seq_bits()) and rows > LEAST:
        count, rows = count + 1, rows // 2
    return count


BLOCKS = 4
PER = 2
HALF = BLOCKS // PER
TURNS = HALF + 1
FILL_STEPS, NEAR_STEPS, BACK_STEPS, EDGE_STEPS, GATE_STEPS = STEPS, STEPS * HALF, STEPS * TURNS + 1, 1, STEPS
NEAR_AT = FILL_STEPS
BACK_AT = NEAR_AT + NEAR_STEPS
EDGE_AT = BACK_AT + BACK_STEPS
PULL_AT = EDGE_AT + EDGE_STEPS
DOT_STEPS = STEPS + 1
PULL_STEPS = 2 * GATE_STEPS + DOT_STEPS
LAST_AT = PULL_AT + PULL_STEPS
ALL_STEPS = LAST_AT + 1
PACE = ((1, FILL_STEPS - 1, 9), (NEAR_AT, NEAR_STEPS, 17), (BACK_AT, BACK_STEPS, 26), (EDGE_AT, EDGE_STEPS, 3), (PULL_AT, PULL_STEPS, 24))
DONE = sum(turns for _, _, turns in PACE)


def clip(v, low, high):
    return jnp.minimum(jnp.maximum(v, low), high)


def paced(g):
    done = 0
    for first, steps, turns in PACE:
        done = done + (turns * clip(g - first, 0, steps)) // steps
    return done


def head_block(g):
    near = clip(g - NEAR_AT, 0, NEAR_STEPS) // HALF
    over = near // STEPS
    return near * (1 - over) + over * clip((g - BACK_AT) // TURNS, 0, STEPS - 1)


def gate_block(g):
    over = clip(g - FILL_STEPS + 1, 0, 1)
    return jnp.minimum(g, FILL_STEPS - 1) * (1 - over) + over * clip(g - PULL_AT - GATE_STEPS, 0, GATE_STEPS - 1)


def near_block_at(g):
    return jnp.minimum(clip(g - NEAR_AT, 0, NEAR_STEPS) // HALF, STEPS - 1)


def rear_kernel(pc_ref, x_ref, dy_ref, bc_ref, rb_ref, rt_ref, er_ref, ew_ref, d2_ref, ed_ref, dt_ref, e2_ref, et_ref, states_ref, in_ref, taps_ref, skip_ref, heads_ref, met_ref, normed_ref, tok_ref, up_ref, gain_ref, sums_ref, low0_ref, low1_ref, low2_ref, low3_ref, low_ref, dgate_ref, wgate_ref, wconv_ref, din_ref, sum_in_ref, sum_out_ref, small_ref, dtok_ref, mixed_ref, gconv_ref, gout_ref, ggate_ref, pad_ref, dact_ref, dheld_ref, direct_ref, dconv_ref, dscores_ref, dbc_ref, ddt_ref, q_ref, v_ref, ends_ref, crossed_ref, stage_ref, second_ref, rim_ref, rim_got_ref, one_sem, fill_sem, rim_sem, total_ref, factor_ref, reach_ref, held_ref, psend_ref, precv_ref, ps_sem, pr_sem, vsend_ref, vrecv_ref, vs_sem, vr_sem, r_held, r_core, r_sx, r_rx, r_near, r_res, r_blank, load_sem, keep_sem, send_sem, recv_sem, all_sem, *parts):
    g = pl.program_id(0)
    length = x_ref.shape[0]
    seq, peers = lax.axis_index("seq"), lax.axis_size("seq")
    following, previous = {"seq": lax.rem(seq + 1, peers)}, {"seq": lax.rem(seq + peers - 1, peers)}
    reducer = Reducer(gout_ref, ggate_ref, gconv_ref, sum_in_ref, sum_out_ref, r_held, r_core, r_sx, r_rx, r_near, r_res, r_blank, load_sem, keep_sem, send_sem, recv_sem, all_sem, parts)
    passing = Passing(True, total_ref, factor_ref, reach_ref, held_ref, psend_ref, precv_ref, met_ref, ps_sem, pr_sem)
    rounds = len(passing.bits)
    block = head_block(g)

    def columns_of(j):
        return pl.ds(pl.multiple_of(j * WIDE, WIDE), WIDE)

    def edge(j):
        return pltpu.make_async_remote_copy(src_ref=rim_ref.at[:, columns_of(j)], dst_ref=rim_got_ref.at[:, columns_of(j)], send_sem=rim_sem.at[0, j], recv_sem=rim_sem.at[1, j], device_id=previous, device_id_type=MESH)

    @pl.when(g == 0)
    def _():
        greet(reducer.partners + [following, previous])
        first = pltpu.make_async_copy(din_ref, total_ref, one_sem.at[2])
        first.start()
        for ref in (dscores_ref, dbc_ref, ddt_ref, q_ref, v_ref, ends_ref, crossed_ref, held_ref):
            ref[...] = jnp.zeros_like(ref)
        reach_ref[...] = jnp.ones_like(reach_ref)
        factor_ref[0:1, :] = met_ref[7:8, :]
        first.wait()
        for j in range(STEPS):
            passing.start(0, j)

    lows = (low0_ref, low1_ref, low2_ref, low3_ref)

    def filled(i):
        copies = []
        for b in range(PARTS):
            rows = pl.ds(pl.multiple_of(b * OUT_PART + i * ROWS, ROWS), ROWS)
            copies.append(pltpu.make_async_copy(stage_ref.at[b * ROWS : (b + 1) * ROWS, :], gout_ref.at[rows, :], fill_sem.at[b]))
        copies.append(pltpu.make_async_copy(second_ref, ggate_ref.at[columns_of(i), :], fill_sem.at[PARTS]))
        return copies

    @pl.when(jnp.logical_and(g >= 1, g <= FILL_STEPS))
    def _():
        for copy in filled(g - 1):
            copy.wait()

    @pl.when(g < FILL_STEPS)
    def _():
        for b in range(PARTS):
            stage_ref[b * ROWS : (b + 1) * ROWS, :] = tn(lows[b][...], up_ref[...]).astype(LOW)
        second_ref[...] = tn(dgate_ref[...], normed_ref[EDGE:, :]).astype(LOW)
        for copy in filled(g):
            copy.start()

    @pl.when(g == 1)
    def _():
        reducer.load(jnp.int32(0))

    for k in range(rounds - 1):
        since = g - (1 + 2 * k)

        @pl.when(jnp.logical_and(since >= 0, since < STEPS))
        def _(k=k, since=since):
            passing.finish(k, since)

    def near_block(c):
        at = pl.ds(pl.multiple_of(c * BLOCK, BLOCK), BLOCK)
        ids, jds = rows_cols((BLOCK, BLOCK))
        suffix = (ids >= jds).astype(LOW)
        left = lax.broadcasted_iota(jnp.int32, (BLOCK, LANES), 1) < HDIM
        scores = jnp.where(ids <= jds, nt(bc_ref[at, :NSTATE], bc_ref[at, NSTATE:]), 0.0)
        dy = dy_ref[at, :]
        sized = x_ref[at, :].astype(F32) * nn(d2_ref[at, :], e2_ref[...])
        total = jnp.zeros((BLOCK, BLOCK), F32)
        rows = []
        for pair in range(GROUP // 2):
            lanes = slice(pair * LANES, (pair + 1) * LANES)
            piece, dpiece = sized[:, lanes], dy[:, lanes]
            both = jnp.concatenate([jnp.where(left, piece, 0.0), jnp.where(left, 0.0, piece)], axis=0).astype(LOW)
            meets = nn(both, dpiece.T)
            mixed, kept = [], []
            for half in range(2):
                head = 2 * pair + half
                spread = rt_ref[head : head + 1, at] - rb_ref[at, head : head + 1]
                decay = jnp.exp(jnp.minimum(spread, 0.0))
                meet = meets[half * BLOCK : (half + 1) * BLOCK] * decay
                total = total + meet
                mixed.append((scores * decay).astype(LOW))
                kept.append((meet * scores).astype(LOW))
            later = nn(jnp.concatenate(kept, axis=0), suffix)
            for half in range(2):
                one = later[half * BLOCK : (half + 1) * BLOCK]
                rows.append(jnp.sum(jnp.where(ids < jds, one, 0.0), axis=0, keepdims=True))
            none = jnp.zeros_like(dpiece)
            both = jnp.concatenate([jnp.where(left, dpiece, none), jnp.where(left, none, dpiece)], axis=0)
            direct_ref[block, at, lanes] = nn(jnp.concatenate(mixed, axis=1), both)
        dscores_ref[c] += total
        crossed_ref[pl.ds(pl.multiple_of(block * GROUP, GROUP), GROUP), at] = jnp.concatenate(rows, axis=0)

    @pl.when(jnp.logical_and(g >= NEAR_AT, g < BACK_AT))
    def _():
        @pl.loop(0, PER)
        def _(i):
            near_block(((g - NEAR_AT) % HALF) * PER + i)

    turn = g - BACK_AT
    part = turn % TURNS
    going = jnp.logical_and(turn >= 0, turn < STEPS * TURNS)

    @pl.when(jnp.logical_and(going, part == 0))
    def _():
        passing.finish(rounds - 1, block)
        dheld_ref[...] = held_ref[:, passing.columns(block)]

    def back_block(c):
        at = pl.ds(pl.multiple_of(c * BLOCK, BLOCK), BLOCK)
        input_mat, output_mat = bc_ref[at, :NSTATE], bc_ref[at, NSTATE:]
        e2, et = e2_ref[...], et_ref[...]
        grow, leave, size = nn(er_ref[at, :], e2), nn(ew_ref[at, :], e2), nn(d2_ref[at, :], e2)
        prior = pl.ds(pl.multiple_of(jnp.maximum(c * BLOCK - 16, 0), 16), 16)
        reach = nn(ed_ref[prior, :], e2)[15:16, :]
        reach = jnp.where(c == 0, 1.0, reach)
        state = states_ref[c].astype(F32) + reach * in_ref[...].astype(F32)
        state_low = state.astype(LOW)
        x = x_ref[at, :].astype(F32)
        dy = dy_ref[at, :].astype(F32)
        dheld = dheld_ref[...]
        dheld_low = dheld.astype(LOW)
        grown = (dy * grow).astype(LOW)
        pulled = nn(input_mat, dheld_low) * leave
        dbc_ref[at, :NSTATE] += nt((x * size * leave).astype(LOW), dheld_low)
        dbc_ref[at, NSTATE:] += nt(grown, state_low)
        carried = nn(output_mat, state_low) * grow
        q_ref[at, :] += nn((dy * carried).astype(LOW), et)
        v_ref[at, :] += nn((x * pulled).astype(LOW), et)
        last = grow[BLOCK - 1 : BLOCK, :]
        ends = jnp.sum(state * dheld, axis=0, keepdims=True) * last
        ends_ref[c] += nn(jnp.broadcast_to(ends, (16, WIDE)).astype(LOW), et)[:8]
        dheld_ref[...] = dheld * last + tn(output_mat, grown)
        direct = direct_ref[block, at, :] + pulled
        ddt_ref[at, :] += nn((x * direct).astype(LOW), et)
        dact_ref[at, :] = size * direct + skip_ref[0:1, :] * dy

    @pl.when(jnp.logical_and(going, part < HALF))
    def _():
        @pl.loop(0, PER)
        def _(i):
            back_block(BLOCKS - 1 - (part * PER + i))

    @pl.when(turn == STEPS * TURNS)
    def _():
        ids, jds = rows_cols((BLOCK, BLOCK))
        upper = (ids <= jds).astype(F32)
        under = (ids > jds).astype(F32)
        rate = jnp.exp(heads_ref[1:2, :])
        dstep_bias = jnp.zeros((1, LANES), F32)
        ddecay_log = jnp.zeros((1, LANES), F32)
        for c in range(BLOCKS):
            at = slice(c * BLOCK, (c + 1) * BLOCK)
            dscores = jnp.where(ids <= jds, dscores_ref[c], 0.0).astype(LOW)
            dact_ref[at, :NSTATE] = dbc_ref[at, :NSTATE] + nn(dscores, bc_ref[at, NSTATE:])
            dact_ref[at, NSTATE : 2 * NSTATE] = dbc_ref[at, NSTATE:] + tn(dscores, bc_ref[at, :NSTATE])
            dt = dt_ref[at, :]
            ddecay = crossed_ref[:, at].T + exact(upper, q_ref[at, :]) + exact(under, v_ref[at, :] * dt) + ends_ref[c][0:1, :]
            draw = ddt_ref[at, :] - ddecay * rate
            ddecay_log = ddecay_log - jnp.sum(ddecay * dt, axis=0, keepdims=True) * rate
            raw = pc_ref[EDGE + c * BLOCK : EDGE + (c + 1) * BLOCK, 2 * NSTATE : 2 * NSTATE + LANES].astype(F32)
            used = lax.broadcasted_iota(jnp.int32, raw.shape, 1) < HEADS
            draw = draw * jax.nn.sigmoid(jnp.where(used, raw + heads_ref[0:1, :], 0.0))
            dstep_bias = dstep_bias + jnp.sum(draw, axis=0, keepdims=True)
            dact_ref[at, 2 * NSTATE : 2 * NSTATE + LANES] = draw
            dact_ref[at, 2 * NSTATE + LANES :] = jnp.zeros((BLOCK, LANES), F32)
        ends_ref[0] = jnp.broadcast_to(dstep_bias, (8, LANES))
        ends_ref[1] = jnp.broadcast_to(ddecay_log, (8, LANES))

    @pl.when(jnp.logical_or(jnp.logical_and(going, part == HALF), turn == STEPS * TURNS))
    def _():
        here = turn // TURNS
        at = pl.ds(pl.multiple_of(here * WIDE, WIDE), WIDE)
        taps = taps_ref[:, at]
        pad_ref[...] = pc_ref[...].astype(F32)
        summed = taps[CONV : CONV + 1]
        for k in range(CONV):
            first = EDGE - CONV + 1 + k
            summed = summed + taps[k : k + 1] * pad_ref[first : first + length, :]
        shape = jax.nn.sigmoid(summed)
        dsum = dact_ref[0:length, :] * (shape * (1.0 + summed * (1.0 - shape)))
        dtap = [jnp.sum(dsum * pad_ref[EDGE - CONV + 1 + k : EDGE - CONV + 1 + k + length, :], axis=0, keepdims=True) for k in range(CONV)]
        dtap.append(jnp.sum(dsum, axis=0, keepdims=True))
        vsend_ref[0, :, at] = jnp.concatenate(dtap + [jnp.zeros((8 - len(dtap), WIDE), F32)], axis=0)
        rim_ref[:, at] = dsum[:16].astype(LOW)
        keep = dact_ref[0:length, :]
        dact_ref[0:length, :] = dsum
        dact_ref[length:, :] = jnp.zeros_like(dact_ref[length:, :])
        result = taps[CONV - 1 : CONV] * dsum
        for k in range(CONV - 1):
            by = CONV - 1 - k
            result = result + taps[k : k + 1] * dact_ref[by : by + length, :]
        lane = lax.broadcasted_iota(jnp.int32, (1, WIDE), 1)
        raw_part = jnp.logical_and(turn == STEPS * TURNS, lane >= 2 * NSTATE)
        dconv_ref[:, at] = jnp.where(raw_part, keep, result).astype(LOW)

    def stored(k):
        return pltpu.make_async_copy(stage_ref, gconv_ref.at[columns_of(k), :], one_sem.at[2])

    def settle(j):
        edge(j).wait()

        @pl.when(j >= 1)
        def _():
            stored(j - 1).wait()

        at = columns_of(j)
        bottom = slice(length - 16, length)
        got, taps = rim_got_ref[:, at].astype(F32), taps_ref[:, at]
        ids, jds = rows_cols(got.shape)
        extra = jnp.zeros_like(got)
        for i in range(CONV - 1):
            row = sum(taps[k : k + 1] * got[i - k : i - k + 1] for k in range(i + 1))
            extra = jnp.where(ids == 16 - CONV + 1 + i, row, extra)
        takes = jnp.logical_and(jds < CDIM - j * WIDE, seq < peers - 1)
        dconv_ref[bottom, at] = (dconv_ref[bottom, at].astype(F32) + jnp.where(takes, extra, 0.0)).astype(LOW)
        stage_ref[...] = tn(dconv_ref[:, at], normed_ref[EDGE:, :]).astype(LOW)
        stored(j).start()

    convolves = jnp.logical_or(jnp.logical_and(going, part == HALF), turn == STEPS * TURNS)

    @pl.when(convolves)
    def _():
        edge(turn // TURNS).start()

    @pl.when(jnp.logical_or(jnp.logical_and(convolves, turn >= TURNS), g == EDGE_AT))
    def _():
        settle(jnp.where(g == EDGE_AT, STEPS, turn // TURNS - 1))

    @pl.when(g == PULL_AT)
    def _():
        stored(STEPS).wait()

    pull = g - PULL_AT

    thirds = [slice(i * WIDE, (i + 1) * WIDE) for i in range(DM // WIDE)]
    mixed_out = pltpu.make_async_copy(stage_ref, mixed_ref, one_sem.at[2])

    @pl.when(pull == 0)
    def _():
        for i, at in enumerate(thirds):
            direct_ref[i] = tok_ref[:, at].astype(F32)

    @pl.when(jnp.logical_and(pull >= 0, pull < GATE_STEPS))
    def _():
        for i, at in enumerate(thirds):
            direct_ref[i] += nn(low_ref[...], wgate_ref[:, at])

    @pl.when(pull == GATE_STEPS)
    def _():
        for i, at in enumerate(thirds):
            stage_ref[:, at] = direct_ref[i].astype(LOW)
        mixed_out.start()
        direct_ref[0:PARTS] = jnp.zeros_like(direct_ref[0:PARTS])

    def add_pull(left, weight):
        for b in range(PARTS):
            direct_ref[b, :, :PART] += nn(left, weight[:, b * PART : (b + 1) * PART])

    @pl.when(jnp.logical_and(pull >= GATE_STEPS, pull < 2 * GATE_STEPS))
    def _():
        add_pull(dgate_ref[...], wgate_ref[...])

    @pl.when(jnp.logical_and(pull >= 2 * GATE_STEPS, pull < PULL_STEPS))
    def _():
        k = pull - 2 * GATE_STEPS
        columns = pl.ds(pl.multiple_of(k * WIDE, WIDE), WIDE)
        ids = lax.broadcasted_iota(jnp.int32, (WIDE, DM), 0)
        weight = wconv_ref[...]
        weight = jnp.where(ids < CDIM + HEADS - k * WIDE, weight, jnp.zeros_like(weight))
        add_pull(dconv_ref[:, columns], weight)

    def normed_out(b):
        return pltpu.make_async_copy(direct_ref.at[relative(b), :, 0:PART], dtok_ref.at[:, b * PART : (b + 1) * PART], one_sem.at[3 + b])

    meets = len(reducer.partners)

    def swap(k):
        return pltpu.make_async_remote_copy(src_ref=vsend_ref.at[k], dst_ref=vrecv_ref.at[k], send_sem=vs_sem.at[k], recv_sem=vr_sem.at[k], device_id=reducer.partners[k], device_id_type=MESH)

    @pl.when(g == LAST_AT)
    def _():
        blocks = [slice(b * PART, (b + 1) * PART) for b in range(PARTS)]
        square = jnp.zeros((length, 1), F32)
        cross = jnp.zeros((length, 1), F32)
        for b, at in enumerate(blocks):
            u = tok_ref[:, at].astype(F32)
            square = square + jnp.sum(u * u, axis=1, keepdims=True)
            cross = cross + jnp.sum(direct_ref[relative(b), :, :PART] * gain_ref[0:1, at] * u, axis=1, keepdims=True)
        rate = lax.rsqrt(square * (1.0 / DM) + EPS)
        pulled = rate * rate * rate * (cross * (1.0 / DM))
        for b, at in enumerate(blocks):
            u = tok_ref[:, at].astype(F32)
            there = relative(b)
            d_normed = direct_ref[there, :, :PART]
            vsend_ref[0, 5:6, at] = jnp.sum(d_normed * (u * rate), axis=0, keepdims=True)
            direct_ref[there, :, :PART] = up_ref[:, at].astype(F32) + rate * (d_normed * gain_ref[0:1, at]) - u * pulled
            normed_out(b).start()
        vsend_ref[0, 6:7, :DI] = sums_ref[0:1, :]
        vsend_ref[0, 7:8, :DI] = sums_ref[1:2, :]
        vsend_ref[0, 6:7, DI : DI + LANES] = ends_ref[0][0:1]
        vsend_ref[0, 7:8, DI : DI + LANES] = ends_ref[1][0:1]

        swap(0).start()

    @pl.loop(paced(g), paced(g + 1) + (g // LAST_AT) * (reducer.total - DONE))
    def _(t):
        reducer.step(t)
        for k in range(meets):

            @pl.when(t == DONE + 2 * (k + 1))
            def _(k=k):
                swap(k).wait()
                value = vsend_ref[k] + vrecv_ref[k]
                if k + 1 < meets:
                    vsend_ref[k + 1] = value
                    swap(k + 1).start()
                else:
                    small_ref[...] = value

    @pl.when(g == LAST_AT)
    def _():
        for b in range(PARTS):
            normed_out(b).wait()
        mixed_out.wait()


def rear(proj, x, dy, bc, rb, rt, er, ew, d2, ed, dt, e2, et, states, incoming, taps, skip, heads, met, normed, tokens, upstream, gain, sums, low, dgate, wide_all, conv_all, din):
    length = x.shape[0]
    bits, halved = len(seq_bits()), halved_bits()
    hbm = pl.BlockSpec(memory_space=pl.ANY)
    back_block = lambda g: clip((g - BACK_AT) // TURNS, 0, STEPS)
    part_block = lambda g: clip((g - BACK_AT) // TURNS, 0, STEPS - 1)

    def whole(array):
        return pl.BlockSpec(array.shape, lambda g: (0,) * array.ndim, pipeline_mode=pl.Buffered(1))

    shares = []
    for j in range(bits):
        shape = (FEW, max(ROWS >> (j + 1), LEAST), PART)
        shares += [pltpu.VMEM(shape, LOW), pltpu.VMEM(shape, LOW), pltpu.VMEM(shape, F32)]
    dma = pltpu.SemaphoreType.DMA
    stages, meets = 2 + bits + halved, 2 + bits
    moved = 3 * ROWS + 2 * sum(ROWS >> (j + 1) for j in range(halved)) + LEAST * (bits - halved)
    return pl.pallas_call(
        rear_kernel,
        grid=(ALL_STEPS,),
        in_specs=[
            pl.BlockSpec((length + EDGE, WIDE), lambda g: (0, back_block(g))),
            pl.BlockSpec((length, WIDE), lambda g: (0, head_block(g))),
            pl.BlockSpec((length, WIDE), lambda g: (0, head_block(g))),
            whole(bc),
            pl.BlockSpec((length, LANES), lambda g: (0, near_block_at(g))),
            pl.BlockSpec((GROUP, length), lambda g: (near_block_at(g), 0)),
            whole(er),
            whole(ew),
            whole(d2),
            whole(ed),
            whole(dt),
            pl.BlockSpec((2 * LANES, WIDE), lambda g: (0, head_block(g))),
            pl.BlockSpec((WIDE, LANES), lambda g: (part_block(g), 0)),
            pl.BlockSpec((length // BLOCK, NSTATE, WIDE), lambda g: (0, 0, part_block(g))),
            pl.BlockSpec((NSTATE, WIDE), lambda g: (0, part_block(g))),
            whole(taps),
            pl.BlockSpec((8, WIDE), lambda g: (0, part_block(g))),
            whole(heads),
            whole(met),
            whole(normed),
            whole(tokens),
            whole(upstream),
            whole(gain),
            whole(sums),
        ]
        + [pl.BlockSpec((length, ROWS), lambda g, b=b: (0, b * (OUT_PART // ROWS) + jnp.minimum(g, FILL_STEPS - 1))) for b in range(PARTS)]
        + [
            pl.BlockSpec((length, WIDE), lambda g: (0, clip(g - PULL_AT, 0, GATE_STEPS - 1))),
            pl.BlockSpec((length, WIDE), lambda g: (0, gate_block(g))),
            pl.BlockSpec((WIDE, DM), lambda g: ((clip(g - PULL_AT, 0, 2 * GATE_STEPS - 1) + GATE_STEPS) % (2 * GATE_STEPS), 0)),
            pl.BlockSpec((WIDE, DM), lambda g: (clip(g - PULL_AT - 2 * GATE_STEPS, 0, DOT_STEPS - 1), 0)),
            hbm,
        ],
        out_specs=[hbm, hbm, pl.BlockSpec((8, LONG), lambda g: (0, 0)), hbm, hbm, hbm, hbm, hbm],
        out_shape=[
            jax.ShapeDtypeStruct((DI + CDIM + HEADS, PART), LOW),
            jax.ShapeDtypeStruct((OUT_PART, DM), LOW),
            jax.ShapeDtypeStruct((8, LONG), F32),
            jax.ShapeDtypeStruct((length, DM), F32),
            jax.ShapeDtypeStruct((length, DM), LOW),
            jax.ShapeDtypeStruct((LONG, DM), LOW),
            jax.ShapeDtypeStruct((DI, DM), LOW),
            jax.ShapeDtypeStruct((DI, DM), LOW),
        ],
        scratch_shapes=[
            pltpu.VMEM((length + EDGE, WIDE), F32),
            pltpu.VMEM((length + EDGE, WIDE), F32),
            pltpu.VMEM((NSTATE, WIDE), F32),
            pltpu.VMEM((STEPS, length, WIDE), F32),
            pltpu.VMEM((length, LONG), LOW),
            pltpu.VMEM((length // BLOCK, BLOCK, BLOCK), F32),
            pltpu.VMEM((length, 2 * NSTATE), F32),
            pltpu.VMEM((length, LANES), F32),
            pltpu.VMEM((length, LANES), F32),
            pltpu.VMEM((length, LANES), F32),
            pltpu.VMEM((length // BLOCK, 8, LANES), F32),
            pltpu.VMEM((LANES, length), F32),
            pltpu.VMEM((WIDE, DM), LOW),
            pltpu.VMEM((WIDE, DM), LOW),
            pltpu.VMEM((16, LONG), LOW),
            pltpu.VMEM((16, LONG), LOW),
            dma((3 + PARTS,)),
            dma((PARTS + 1,)),
            dma((2, STEPS + 1)),
            pltpu.VMEM((NSTATE, DI), F32),
            pltpu.VMEM((8, DI), F32),
            pltpu.VMEM((8, DI), F32),
            pltpu.VMEM((NSTATE, DI), F32),
            pltpu.VMEM((NSTATE, DI), LOW),
            pltpu.VMEM((bits, NSTATE, DI), LOW),
            dma((bits, STEPS)),
            dma((bits, STEPS)),
            pltpu.VMEM((meets, 8, LONG), F32),
            pltpu.VMEM((meets, 8, LONG), F32),
            dma((meets,)),
            dma((meets,)),
            pltpu.VMEM((FEW, ROWS, DM), LOW),
            pltpu.VMEM((FEW, ROWS, 2 * PART), LOW),
            pltpu.VMEM((FEW, ROWS, PART), LOW),
            pltpu.VMEM((FEW, ROWS, PART), LOW),
            pltpu.VMEM((FEW, ROWS, PART), F32),
            pltpu.VMEM((SLOTS, ROWS, PART), LOW),
            pltpu.VMEM((moved, PART), LOW),
            dma((FEW,)),
            dma((SLOTS,)),
            dma((stages, FEW)),
            dma((stages, FEW)),
            dma((2, FEW)),
        ]
        + shares,
        compiler_params=pltpu.CompilerParams(vmem_limit_bytes=62 << 20, collective_id=2, has_side_effects=True),
        cost_estimate=pl.CostEstimate(flops=200 << 30, bytes_accessed=60 << 20, transcendentals=0),
        name="rear",
    )(proj, x, dy, bc, rb, rt, er, ew, d2, ed, dt, e2, et, states, incoming, taps, skip, heads, met, normed, tokens, upstream, gain, sums, low, low, low, low, low, dgate, wide_all, conv_all, din)


def shards(tokens, norm_gain, in_weight, conv_kernel, conv_bias, step_bias, decay_log, skip_gain, out_gain, out_weight, cotangent):
    length = tokens.shape[1]
    own, upstream = tokens[0], cotangent[0]
    turned = in_weight.T
    gain = norm_gain[None]
    skip = jnp.repeat(skip_gain, HDIM)[None]
    gains = jnp.concatenate([out_gain[None], skip, jnp.zeros((6, DI), F32)], axis=0)
    skip = jnp.broadcast_to(skip, (8, DI))
    lanes = np.arange(DI) // HDIM
    e2 = jnp.asarray((np.arange(2 * LANES)[:, None] % LANES == lanes[None]).astype(LOW))
    et = jnp.asarray((lanes[:, None] == np.arange(LANES)[None]).astype(LOW))

    taps, heads, proj, normed, x, bc, dt, rb, rt, er, ew, d2, ed, state, conv_all = enter(own, gain, conv_kernel, conv_bias[None], step_bias[None], decay_log[None], e2, turned)
    incoming, met, y, states, gate, dno, wide_all = gates(normed, upstream, state, x, bc, rb, rt, er, ew, d2, e2, turned, out_weight)
    low, dy, dgate, sums, din = middle(y, bc, incoming, ed, e2, x, gate, dno, gains, length)

    sum_in, sum_out, small, d_tokens, mixed, *_ = rear(proj, x, dy, bc, rb, rt, er, ew, d2, ed, dt, e2, et, states, incoming, taps, skip, heads, met, normed, own, upstream, gain, sums, low, dgate, wide_all, conv_all, din)
    return (
        mixed[None],
        d_tokens[None],
        small[5, :DM],
        sum_in.astype(F32).T,
        small[:CONV, :CDIM],
        small[CONV, :CDIM],
        small[6, DI : DI + HEADS],
        small[7, DI : DI + HEADS],
        jnp.sum(small[7, :DI].reshape(HEADS, HDIM), axis=1),
        small[6, :DI],
        sum_out.astype(F32),
    )


def solution(mesh):
    spread = P("wt", "seq", None)
    return jax.shard_map(
        shards,
        mesh=mesh,
        in_specs=(spread, P(), P("wt", None), P(), P(), P(), P(), P(), P(), P("wt", None), spread),
        out_specs=(spread, spread, P(), P("wt", None), P(), P(), P(), P(), P(), P(), P("wt", None)),
        check_vma=False,
    )
```

```python
import jax
import jax.numpy as jnp
import numpy as np
from jax import lax
from jax.experimental import pallas as pl
from jax.experimental.pallas import tpu as pltpu
from jax.sharding import PartitionSpec as P

DI = 3072
HEADS = 48
HDIM = 64
NSTATE = 128
CONV = 4
CDIM = 3328
EDGE = 16
BLOCK = 128
GROUP = 8
WIDE = GROUP * HDIM
STEPS = HEADS // GROUP
LONG = (STEPS + 1) * WIDE
LANES = 128
TILE = 512
FINE = 256
SHORT = 128
AHEAD = 4
LAG = 2
LAST = 320
PARTS = 4
DM = 1536
PART = DM // PARTS
OUT_PART = DI // PARTS
SLOTS = 16
FEW = 4
SLACK = 2
MESH = pl.DeviceIdType.MESH

EPS = 1e-05
F32 = jnp.float32
LOW = jnp.bfloat16


def dot(a, b, ca, cb):
    return lax.dot_general(a, b, (((ca,), (cb,)), ((), ())), preferred_element_type=F32)


def nn(a, b):
    return dot(a, b, 1, 0)


def nt(a, b):
    return dot(a, b, 1, 1)


def tn(a, b):
    return dot(a, b, 0, 0)


def exact(a, b):
    return jnp.dot(a, b, precision=lax.Precision.HIGHEST, preferred_element_type=F32)


def halves(v):
    high = v.astype(LOW)
    return jnp.concatenate([high, (v - high.astype(F32)).astype(LOW)], axis=1)


def softplus(v):
    z = jnp.exp(-jnp.abs(v))
    small = z * (1.0 - z * (0.5 - z * (1.0 / 3.0 - z * 0.25)))
    return jnp.maximum(v, 0.0) + jnp.where(z < 0.01, small, jnp.log(1.0 + z))


def rows_cols(shape):
    return (lax.broadcasted_iota(jnp.int32, shape, 0), lax.broadcasted_iota(jnp.int32, shape, 1))


class Begin:
    def __init__(self, proj_ref, taps_ref, heads_ref, e2_ref, x_ref, bc_ref, dt_ref, rb_ref, rt_ref, er_ref, ew_ref, d2_ref, ed_ref, state_ref, pad_ref, wd_ref):
        self.proj, self.taps, self.heads, self.e2 = proj_ref, taps_ref, heads_ref, e2_ref
        self.x, self.bc, self.dt, self.rb, self.rt = x_ref, bc_ref, dt_ref, rb_ref, rt_ref
        self.er, self.ew, self.d2, self.ed, self.state = er_ref, ew_ref, d2_ref, ed_ref, state_ref
        self.pad, self.wd = pad_ref, wd_ref
        self.length = x_ref.shape[0]

    def convolved(self, first, width):
        self.pad[:, :width] = self.proj[:, first : first + width].astype(F32)
        total = self.taps[CONV : CONV + 1, first : first + WIDE]
        for k in range(CONV):
            at = EDGE - CONV + 1 + k
            total = total + self.taps[k : k + 1, first : first + WIDE] * self.pad[at : at + self.length, :]
        return total * jax.nn.sigmoid(total)

    def sizes(self):
        length = self.length
        self.pad[...] = jnp.zeros_like(self.pad)
        act = self.convolved(DI, CDIM + HEADS - DI)
        self.bc[...] = act[:, : 2 * NSTATE].astype(LOW)
        raw = self.pad[EDGE:, 2 * NSTATE : 2 * NSTATE + LANES]
        used = lax.broadcasted_iota(jnp.int32, raw.shape, 1) < HEADS
        dt = jnp.where(used, softplus(jnp.where(used, raw + self.heads[0:1, :], 0.0)), 0.0)
        self.dt[...] = dt
        self.d2[...] = halves(dt)
        decay = -dt * jnp.exp(self.heads[1:2, :])
        ids, jds = rows_cols((BLOCK, BLOCK))
        lower = (ids >= jds).astype(F32)
        before = jnp.zeros((1, LANES), F32)
        whole = []
        for c in range(length // BLOCK):
            at = slice(c * BLOCK, (c + 1) * BLOCK)
            run = exact(lower, decay[at])
            last = run[BLOCK - 1 : BLOCK]
            for j in range(STEPS):
                turned = jnp.concatenate([run[:, GROUP * j :], run[:, : GROUP * j]], axis=1) if j else run
                self.rb[at, j * LANES : (j + 1) * LANES] = turned
            self.rt[:, at] = run.T
            self.er[at, :] = halves(jnp.exp(run))
            self.ew[at, :] = halves(jnp.exp(last - run))
            whole.append(run + before)
            self.ed[at, :] = halves(jnp.exp(run + before))
            before = before + last
        for c in range(length // BLOCK):
            at = slice(c * BLOCK, (c + 1) * BLOCK)
            self.wd[at, :] = halves(jnp.exp(before - whole[c]) * dt[at])

    def block(self, j):
        at = slice(j * WIDE, (j + 1) * WIDE)
        x = self.convolved(j * WIDE, WIDE).astype(LOW)
        self.x[:, at] = x
        e2 = self.e2[:, at]
        weighed = (x.astype(F32) * nn(self.wd[...], e2)).astype(LOW)
        self.state[0:NSTATE, at] = tn(self.bc[:, :NSTATE], weighed).astype(LOW)
        decay = nn(self.ed[self.length - 16 : self.length, :], e2)[15:16, :]
        high = decay.astype(LOW).astype(F32)
        ids = lax.broadcasted_iota(jnp.int32, (16, WIDE), 0)
        self.state[NSTATE : NSTATE + 16, at] = jnp.where(ids == 0, high, jnp.where(ids == 1, decay - high, 0.0)).astype(LOW)


class Stages:
    def __init__(self, ref, sem):
        self.ref, self.sem, self.count = ref, sem, ref.shape[0]
        self.flying = [None] * self.count
        self.turn = 0

    def put(self, value, target):
        at = self.turn % self.count
        if self.flying[at] is not None:
            self.flying[at].wait()
        self.ref[at] = value
        self.flying[at] = pltpu.make_async_copy(self.ref.at[at], target, self.sem.at[at])
        self.flying[at].start()
        self.turn += 1

    def rest(self):
        for one in self.flying:
            if one is not None:
                one.wait()


class Inside:
    def __init__(self, x_ref, bc_ref, rb_ref, rt_ref, er_ref, ew_ref, d2_ref, e2_ref, held_ref, y_out, states_out, ys, states):
        self.x, self.bc, self.rb, self.rt = x_ref, bc_ref, rb_ref, rt_ref
        self.er, self.ew, self.d2, self.e2, self.held = er_ref, ew_ref, d2_ref, e2_ref, held_ref
        self.y_out, self.states_out, self.ys, self.states = y_out, states_out, ys, states
        self.blocks = x_ref.shape[0] // BLOCK

    def turn(self, at):
        if at < STEPS * self.blocks:
            self.block(at // self.blocks, at % self.blocks)

    def block(self, j, c):
        at, own = slice(c * BLOCK, (c + 1) * BLOCK), slice(j * WIDE, (j + 1) * WIDE)
        ids, jds = rows_cols((BLOCK, BLOCK))
        left = lax.broadcasted_iota(jnp.int32, (BLOCK, LANES), 1) < HDIM
        input_mat, output_mat = self.bc[at, :NSTATE], self.bc[at, NSTATE:]
        e2 = self.e2[:, own]
        grow, leave = nn(self.er[at, :], e2), nn(self.ew[at, :], e2)
        x = self.x[at, own].astype(F32) * nn(self.d2[at, :], e2)
        scores = jnp.where(ids >= jds, nt(output_mat, input_mat), 0.0)
        held = self.held[...] if c else jnp.zeros_like(self.held)
        self.states.put(held.astype(LOW), self.states_out.at[c, :, own])
        carried = grow * nn(output_mat, held.astype(LOW))
        parts = []
        for pair in range(GROUP // 2):
            lanes = slice(pair * LANES, (pair + 1) * LANES)
            piece = x[:, lanes]
            mixed = []
            for head in (2 * pair, 2 * pair + 1):
                column = self.rb[at, j * LANES + head : j * LANES + head + 1]
                spread = column - self.rt[j * GROUP + head : j * GROUP + head + 1, at]
                mixed.append((scores * jnp.exp(jnp.minimum(spread, 0.0))).astype(LOW))
            both = jnp.concatenate([jnp.where(left, piece, 0.0), jnp.where(left, 0.0, piece)], axis=0)
            parts.append(nn(jnp.concatenate(mixed, axis=1), both.astype(LOW)) + carried[:, lanes])
        self.ys.put(jnp.concatenate(parts, axis=1), self.y_out.at[at, own])
        self.held[...] = held * grow[BLOCK - 1 : BLOCK, :] + tn(input_mat, (x * leave).astype(LOW))


def middle_kernel(y_ref, bc_ref, in_ref, ed_ref, e2_ref, x_ref, gate_ref, dno_ref, gains_ref, low_ref, dy_ref, dgate_ref, sums_ref, din_ref, out_ref, gated_ref):
    @pl.when(pl.program_id(0) == 0)
    def _():
        sums_ref[...] = jnp.zeros_like(sums_ref)
        din_ref[...] = jnp.zeros_like(din_ref)

    output_mat = bc_ref[:, NSTATE:]
    part = DI // PARTS
    tiles = []
    for j in range(PARTS):
        there = relative(j)
        tiles.append((slice(j * part, (j + 1) * part), pl.ds(pl.multiple_of(there * part, LANES), part)))
    square = jnp.zeros((BLOCK, 1), F32)
    cross = jnp.zeros((BLOCK, 1), F32)
    for at, there in tiles:
        far = nn(ed_ref[...], e2_ref[:, at]) * nn(output_mat, in_ref[:, at])
        out = y_ref[:, at] + far + gains_ref[1:2, at] * x_ref[:, at].astype(F32)
        gate = gate_ref[:, at].astype(F32)
        gated = out * gate * jax.nn.sigmoid(gate)
        out_ref[:, at] = out
        gated_ref[:, at] = gated
        square = square + jnp.sum(gated * gated, axis=1, keepdims=True)
        cross = cross + jnp.sum(gated * (dno_ref[:, there] * gains_ref[0:1, at]), axis=1, keepdims=True)
    scale = lax.rsqrt(square * (1.0 / DI) + EPS)
    pull = scale * scale * scale * (cross * (1.0 / DI))
    for at, there in tiles:
        gate = gate_ref[:, at].astype(F32)
        gated, out, gain = gated_ref[:, at], out_ref[:, at], gains_ref[0:1, at]
        shape = jax.nn.sigmoid(gate)
        unit = gated * scale
        low_ref[:, there] = (unit * gain).astype(LOW)
        dno = dno_ref[:, there]
        dgated = scale * (dno * gain) - gated * pull
        dy = dgated * (gate * shape)
        dy_ref[:, at] = dy.astype(LOW)
        dgate_ref[:, at] = (dgated * out * (shape * (1.0 + gate * (1.0 - shape)))).astype(LOW)
        sums_ref[0:1, at] += jnp.sum(dno * unit, axis=0, keepdims=True)
        sums_ref[1:2, at] += jnp.sum(dy * x_ref[:, at].astype(F32), axis=0, keepdims=True)
        din_ref[:, at] += tn(output_mat, (dy * nn(ed_ref[...], e2_ref[:, at])).astype(LOW))


def middle(y, bc, incoming, ed, e2, x, gate, dno, gains, length):
    rows = lambda c: (c, 0)
    fixed = lambda c: (0, 0)
    return pl.pallas_call(
        middle_kernel,
        grid=(length // BLOCK,),
        in_specs=[
            pl.BlockSpec((BLOCK, DI), rows),
            pl.BlockSpec((BLOCK, 2 * NSTATE), rows),
            pl.BlockSpec((NSTATE, DI), fixed),
            pl.BlockSpec((BLOCK, 2 * LANES), rows),
            pl.BlockSpec((2 * LANES, DI), fixed),
            pl.BlockSpec((BLOCK, DI), rows),
            pl.BlockSpec((BLOCK, DI), rows),
            pl.BlockSpec((BLOCK, DI), rows),
            pl.BlockSpec((8, DI), fixed),
        ],
        out_specs=[
            pl.BlockSpec((BLOCK, DI), rows),
            pl.BlockSpec((BLOCK, DI), rows),
            pl.BlockSpec((BLOCK, DI), rows),
            pl.BlockSpec((8, DI), fixed),
            pl.BlockSpec((NSTATE, DI), fixed),
        ],
        out_shape=[
            jax.ShapeDtypeStruct((length, DI), LOW),
            jax.ShapeDtypeStruct((length, DI), LOW),
            jax.ShapeDtypeStruct((length, DI), LOW),
            jax.ShapeDtypeStruct((8, DI), F32),
            jax.ShapeDtypeStruct((NSTATE, DI), F32),
        ],
        scratch_shapes=[pltpu.VMEM((BLOCK, DI), F32), pltpu.VMEM((BLOCK, DI), F32)],
        compiler_params=pltpu.CompilerParams(vmem_limit_bytes=48 << 20),
        cost_estimate=pl.CostEstimate(flops=12 << 30, bytes_accessed=32 << 20, transcendentals=4 << 20),
        name="middle",
    )(y, bc, incoming, ed, e2, x, gate, dno, gains)


def spot():
    wt, seq = lax.axis_index("wt"), lax.axis_index("seq")
    return wt // 2, wt % 2, seq % 2


def relative(block):
    x, core, _ = spot()
    high, low = block // 2, block % 2
    return 2 * (core + low - 2 * core * low) + (x + high - 2 * x * high)


def across_bit(axis, bit):
    index = lax.axis_index(axis)
    return {axis: index + bit - 2 * bit * ((index // bit) % 2)}


def greet(devices):
    barrier = pltpu.get_barrier_semaphore()
    for device in devices:
        pl.semaphore_signal(barrier, inc=1, device_id=device, device_id_type=MESH)
    pl.semaphore_wait(barrier, len(devices))


class Piece:
    def __init__(self, source, near, mine, pair, twin, half, sems, at, bit):
        part = pl.multiple_of((lax.axis_index("seq") // bit) % 2 * half, 16)
        own, xs, xr, ys, yr, ts, tr, keep = sems
        rows = lambda ref: ref.at[pl.ds(part, half), :]
        self.own = pltpu.make_async_copy(source, mine, own.at[at])
        self.x = self.remote(rows(source), rows(near), xs.at[at], xr.at[at], across_bit("wt", 2))
        self.y = self.remote(rows(near), rows(near), ys.at[at], yr.at[at], across_bit("seq", bit))
        self.twin = self.remote(pair, twin, ts.at[at], tr.at[at], across_bit("wt", 1))

    def remote(self, source, target, send, recv, device):
        return pltpu.make_async_remote_copy(src_ref=source, dst_ref=target, send_sem=send, recv_sem=recv, device_id=device, device_id_type=MESH)


def gather_sems(count):
    return [pltpu.SemaphoreType.DMA((count,)) for _ in range(8)]


def enter_kernel(tok_ref, gain_ref, kernel_ref, bias_ref, step_ref, log_ref, e2_ref, w_ref, taps_ref, heads_ref, proj_ref, normed_ref, x_ref, bc_ref, dt_ref, rb_ref, rt_ref, er_ref, ew_ref, d2_ref, ed_ref, state_ref, all_ref, wide_ref, last_ref, edge_ref, pad_ref, wd_ref, edge_sem, *sems):
    length = tok_ref.shape[0]
    begin = Begin(proj_ref, taps_ref, heads_ref, e2_ref, x_ref, bc_ref, dt_ref, rb_ref, rt_ref, er_ref, ew_ref, d2_ref, ed_ref, state_ref, pad_ref, wd_ref)
    seq, peers = lax.axis_index("seq"), lax.axis_size("seq")
    following, previous = {"seq": lax.rem(seq + 1, peers)}, {"seq": lax.rem(seq + peers - 1, peers)}
    greet([across_bit("wt", 1), across_bit("wt", 2), across_bit("seq", 1), across_bit("seq", 2), following, previous])
    edge = pltpu.make_async_remote_copy(src_ref=tok_ref.at[length - EDGE : length, :], dst_ref=edge_ref, send_sem=edge_sem.at[0], recv_sem=edge_sem.at[1], device_id=following, device_id_type=MESH)
    edge.start()
    count = CDIM // TILE
    pieces, products, keeps = [], [], []

    def add(target, first, rows):
        pieces.append(Piece(w_ref.at[pl.ds(first, rows), :], target.at[:, PART : 2 * PART], target.at[:, :PART], target.at[:, : 2 * PART], target.at[:, 2 * PART :], rows // 2, sems, len(pieces), 1 + len(pieces) % 2))
        products.append(None)

    def multiply(target, columns, skip, then):
        keep = pltpu.make_async_copy(target.at[skip:, :], all_ref.at[columns, :], sems[-1].at[len(keeps)])
        keeps.append(keep)

        def product():
            keep.start()
            proj_ref[:, columns] = nt(normed_ref[...], target[skip:, :]).astype(LOW)
            then()

        products[-1] = product

    add(last_ref, DI + CDIM + HEADS - LAST, LAST)
    multiply(last_ref, slice(count * TILE, CDIM + HEADS), LAST - (CDIM + HEADS - count * TILE), begin.sizes)
    for c in range(count):
        for first in range(c * TILE, (c + 1) * TILE, FINE):
            add(wide_ref.at[first : first + FINE, :], DI + first, FINE)
        multiply(wide_ref.at[c * TILE : (c + 1) * TILE, :], slice(c * TILE, (c + 1) * TILE), 0, lambda c=c: begin.block(c))
    for piece in pieces:
        piece.own.start()
    for piece in pieces[:AHEAD]:
        piece.x.start()

    def norm(v):
        v = v.astype(F32)
        return (v * lax.rsqrt(jnp.mean(v * v, axis=-1, keepdims=True) + EPS) * gain_ref[0:1, :]).astype(LOW)

    def place(at, v):
        for b in range(PARTS):
            normed_ref[at, pl.ds(pl.multiple_of(relative(b) * PART, LANES), PART)] = v[:, b * PART : (b + 1) * PART]

    taps_ref[...] = jnp.zeros_like(taps_ref)
    taps_ref[0:CONV, :CDIM] = kernel_ref[...]
    taps_ref[CONV : CONV + 1, :CDIM] = bias_ref[...]
    heads_ref[...] = jnp.zeros_like(heads_ref)
    heads_ref[0:1, :HEADS] = step_ref[...]
    heads_ref[1:2, :HEADS] = log_ref[...]
    place(slice(EDGE, EDGE + length), norm(tok_ref[...]))
    edge.wait()
    place(slice(0, EDGE), norm(jnp.where(seq == 0, 0.0, edge_ref[...].astype(F32))))
    travel_on(pieces, products)
    for keep in keeps:
        keep.wait()


def arrived(pieces, t, ahead=AHEAD):
    pieces[t].x.wait_recv()
    if t + ahead < len(pieces):
        pieces[t + ahead].x.start()


def travel_on(pieces, products, ahead=AHEAD, lag=LAG, between=None, there=0):
    count = len(pieces)
    for t in range(count + 2 * lag):
        if t < count:
            if t >= there:
                arrived(pieces, t, ahead)
            pieces[t].y.start()
        if 0 <= t - lag < count:
            pieces[t - lag].y.wait_recv()
            pieces[t - lag].own.wait()
            pieces[t - lag].twin.start()
        if 0 <= t - 2 * lag < count:
            pieces[t - 2 * lag].twin.wait_recv()
            if products[t - 2 * lag] is not None:
                products[t - 2 * lag]()
        if between is not None:
            between(t)
    for piece in pieces:
        piece.x.wait_send()
        piece.y.wait_send()
        piece.twin.wait_send()


def enter(tokens, gain, conv_kernel, conv_bias, step_bias, decay_log, e2, weight):
    length, columns = tokens.shape[0], CDIM + HEADS
    vmem, hbm = pl.BlockSpec(memory_space=pltpu.VMEM), pl.BlockSpec(memory_space=pl.ANY)
    shapes = [
        ((8, LONG), F32),
        ((8, LANES), F32),
        ((length + EDGE, columns), LOW),
        ((length + EDGE, DM), LOW),
        ((length, DI), LOW),
        ((length, 2 * NSTATE), LOW),
        ((length, LANES), F32),
        ((length, LANES * STEPS), F32),
        ((LANES, length), F32),
        ((length, 2 * LANES), LOW),
        ((length, 2 * LANES), LOW),
        ((length, 2 * LANES), LOW),
        ((length, 2 * LANES), LOW),
        ((NSTATE + 16, DI), LOW),
        ((columns, DM), LOW),
    ]
    return pl.pallas_call(
        enter_kernel,
        in_specs=[vmem] * 7 + [hbm],
        out_specs=[vmem] * (len(shapes) - 1) + [hbm],
        out_shape=[jax.ShapeDtypeStruct(shape, kind) for shape, kind in shapes],
        scratch_shapes=[
            pltpu.VMEM((CDIM // TILE * TILE, DM), LOW),
            pltpu.VMEM((LAST, DM), LOW),
            pltpu.VMEM((EDGE, DM), LOW),
            pltpu.VMEM((length + EDGE, WIDE), F32),
            pltpu.VMEM((length, 2 * LANES), LOW),
            pltpu.SemaphoreType.DMA((2,)),
        ]
        + gather_sems(CDIM // TILE * (TILE // FINE) + 1),
        compiler_params=pltpu.CompilerParams(vmem_limit_bytes=56 << 20, collective_id=0, has_side_effects=True),
        cost_estimate=pl.CostEstimate(flops=40 << 30, bytes_accessed=30 << 20, transcendentals=0),
        name="enter",
    )(tokens, gain, conv_kernel, conv_bias, step_bias, decay_log, e2, weight)


class Passing:
    def __init__(self, later, total, factor, reach, held, send, recv, met, send_sem, recv_sem):
        self.later, self.total, self.factor, self.reach, self.held = later, total, factor, reach, held
        self.send, self.recv, self.met, self.send_sem, self.recv_sem = send, recv, met, send_sem, recv_sem
        self.bits = seq_bits()

    def columns(self, j):
        return pl.ds(pl.multiple_of(j * WIDE, WIDE), WIDE)

    def copy(self, k, j):
        at = self.columns(j)
        return pltpu.make_async_remote_copy(src_ref=self.send.at[:, at], dst_ref=self.recv.at[k, :, at], send_sem=self.send_sem.at[k, j], recv_sem=self.recv_sem.at[k, j], device_id=across_bit("seq", self.bits[k]), device_id_type=MESH)

    def start(self, k, j):
        at = self.columns(j)
        self.send[0:NSTATE, at] = self.total[:, at].astype(LOW)
        if not self.later:
            factor = self.factor[0:1, at]
            high = factor.astype(LOW).astype(F32)
            ids = lax.broadcasted_iota(jnp.int32, (16, WIDE), 0)
            self.send[NSTATE : NSTATE + 16, at] = jnp.where(ids == 0, high, jnp.where(ids == 1, factor - high, 0.0)).astype(LOW)
        self.copy(k, j).start()

    def finish(self, k, j):
        self.copy(k, j).wait()
        at = self.columns(j)
        bit = self.bits[k]
        second = (lax.axis_index("seq") // bit) % 2
        takes = second == (0 if self.later else 1)
        other = self.recv[k, 0:NSTATE, at].astype(F32)
        if self.later:
            met = self.met[k : k + 1, at]
        else:
            rows = self.recv[k, NSTATE : NSTATE + 16, at].astype(F32)
            met = rows[0:1] + rows[1:2]
            self.met[k : k + 1, at] = met
        total, factor, reach = self.total[:, at], self.factor[0:1, at], self.reach[0:1, at]
        self.held[:, at] = self.held[:, at] + jnp.where(takes, reach, 0.0) * other
        self.reach[0:1, at] = jnp.where(takes, reach * met, reach)
        if k + 1 < len(self.bits):
            self.total[:, at] = jnp.where(takes, factor, 1.0) * other + jnp.where(takes, 1.0, met) * total
            self.factor[0:1, at] = factor * met
            self.start(k + 1, j)


def gates_kernel(normed_ref, up_ref, state_ref, x_ref, bc_ref, rb_ref, rt_ref, er_ref, ew_ref, d2_ref, e2_ref, w_ref, o_ref, incoming_ref, met_ref, y_out, states_out, gate_out, dno_out, wall_ref, wide_ref, deep_ref, total_ref, factor_ref, reach_ref, held_ref, send_ref, recv_ref, own_ref, y_ref, states_ref, gate_ref, dno_ref, ss_sem, sr_sem, deep_sem, stage_sem, *sems):
    stages = [Stages(ref, stage_sem.at[i]) for i, ref in enumerate((y_ref, states_ref, gate_ref, dno_ref))]
    local = Inside(x_ref, bc_ref, rb_ref, rt_ref, er_ref, ew_ref, d2_ref, e2_ref, own_ref, y_out, states_out, stages[0], stages[1])
    greet([across_bit("wt", 1), across_bit("wt", 2)] + [across_bit("seq", bit) for bit in seq_bits()])
    passing = Passing(False, total_ref, factor_ref, reach_ref, held_ref, send_ref, recv_ref, met_ref, ss_sem, sr_sem)
    total_ref[...] = state_ref[0:NSTATE, :].astype(F32)
    rows = state_ref[NSTATE : NSTATE + 16, :].astype(F32)
    factor_ref[0:1, :] = rows[0:1] + rows[1:2]
    reach_ref[...] = jnp.ones_like(reach_ref)
    held_ref[...] = jnp.zeros_like(held_ref)
    met_ref[...] = jnp.zeros_like(met_ref)
    met_ref[7:8, :] = factor_ref[0:1, :]
    for j in range(STEPS):
        passing.start(0, j)
    pieces, products, keeps = [], [], []

    for c in range(DI // TILE):
        rows = slice(c * TILE, (c + 1) * TILE)
        target = wide_ref.at[rows, :]
        pieces.append(Piece(w_ref.at[rows, :], target.at[:, PART : 2 * PART], target.at[:, :PART], target.at[:, : 2 * PART], target.at[:, 2 * PART :], TILE // 2, sems, len(pieces), 1 + len(pieces) % 3 // 2))
        keeps.append(pltpu.make_async_copy(target, wall_ref.at[rows, :], sems[-1].at[c]))

        def product(rows=rows, keep=keeps[-1]):
            keep.start()
            for first in (rows.start, rows.start + FINE):
                at = slice(first, first + FINE)
                stages[2].put(nt(normed_ref[EDGE:, :], wide_ref[at, :]).astype(LOW), gate_out.at[:, at])

        products.append(product)

    for c in range(OUT_PART // SHORT):
        rows = slice(c * SHORT, (c + 1) * SHORT)
        pieces.append(Piece(o_ref.at[rows, :], deep_ref.at[1, rows, :], deep_ref.at[0, rows, :], deep_ref.at[0:2, rows, :], deep_ref.at[2:4, rows, :], SHORT // 2, sems, len(pieces), 1 + len(pieces) % 3 // 2))
        products.append(None)
        if (c + 1) * SHORT % FINE == 0:
            first = (c + 1) * SHORT - FINE
            mine = [pltpu.make_async_copy(deep_ref.at[b, first : first + FINE, :], wall_ref.at[pl.ds(DI + b * OUT_PART + first, FINE), :], deep_sem.at[first // FINE, b]) for b in range(PARTS)]
            keeps.extend(mine)

            def product(first=first, mine=mine):
                for b in range(PARTS):
                    mine[b].start()
                    at = b * OUT_PART + first
                    stages[3].put(nt(up_ref[...], deep_ref[b, first : first + FINE, :]), dno_out.at[:, at : at + FINE])

            products[-1] = product

    for piece in pieces:
        piece.own.start()
    for piece in pieces[:AHEAD]:
        piece.x.start()

    last = len(passing.bits) - 1
    first_pieces = {2: 0, 4: 1, 5: 2, 7: 3}
    turns = iter(range(STEPS * local.blocks))
    for m in range(STEPS + 2 * (last - 1)):
        for k in range(last):
            if 0 <= m - 2 * k < STEPS:
                passing.finish(k, m - 2 * k)
        if m in first_pieces:
            arrived(pieces, first_pieces[m])
        for _ in range(2):
            local.turn(next(turns, STEPS * local.blocks))

    def between(t):
        for j, due in enumerate((0, 0, 1, 3, 5, 7)):
            if t == due:
                passing.finish(last, j)
        local.turn(next(turns, STEPS * local.blocks))

    travel_on(pieces, products, between=between, there=len(first_pieces))
    for turn in turns:
        local.turn(turn)
    incoming_ref[...] = held_ref[...].astype(LOW)
    for stage in stages:
        stage.rest()
    for keep in keeps:
        keep.wait()


def gates(normed, upstream, state, x, bc, rb, rt, er, ew, d2, e2, weight, out_weight):
    length = upstream.shape[0]
    bits = len(seq_bits())
    vmem, hbm = pl.BlockSpec(memory_space=pltpu.VMEM), pl.BlockSpec(memory_space=pl.ANY)
    dma = pltpu.SemaphoreType.DMA
    return pl.pallas_call(
        gates_kernel,
        in_specs=[vmem] * 11 + [hbm, hbm],
        out_specs=[vmem, vmem] + [hbm] * 5,
        out_shape=[
            jax.ShapeDtypeStruct((NSTATE, DI), LOW),
            jax.ShapeDtypeStruct((8, DI), F32),
            jax.ShapeDtypeStruct((length, DI), F32),
            jax.ShapeDtypeStruct((length // BLOCK, NSTATE, DI), LOW),
            jax.ShapeDtypeStruct((length, DI), LOW),
            jax.ShapeDtypeStruct((length, DI), F32),
            jax.ShapeDtypeStruct((2 * DI, DM), LOW),
        ],
        scratch_shapes=[
            pltpu.VMEM((DI, DM), LOW),
            pltpu.VMEM((PARTS, OUT_PART, DM), LOW),
            pltpu.VMEM((NSTATE, DI), F32),
            pltpu.VMEM((8, DI), F32),
            pltpu.VMEM((8, DI), F32),
            pltpu.VMEM((NSTATE, DI), F32),
            pltpu.VMEM((NSTATE + 16, DI), LOW),
            pltpu.VMEM((bits, NSTATE + 16, DI), LOW),
            pltpu.VMEM((NSTATE, WIDE), F32),
            pltpu.VMEM((2, BLOCK, WIDE), F32),
            pltpu.VMEM((2, NSTATE, WIDE), LOW),
            pltpu.VMEM((2, length, FINE), LOW),
            pltpu.VMEM((2, length, FINE), F32),
            dma((bits, STEPS)),
            dma((bits, STEPS)),
            dma((OUT_PART // FINE, PARTS)),
            dma((4, 2)),
        ]
        + gather_sems(DI // TILE + OUT_PART // SHORT),
        compiler_params=pltpu.CompilerParams(vmem_limit_bytes=58 << 20, collective_id=1, has_side_effects=True),
        cost_estimate=pl.CostEstimate(flops=50 << 30, bytes_accessed=50 << 20, transcendentals=0),
        name="gates",
    )(normed, upstream, state, x, bc, rb, rt, er, ew, d2, e2, weight, out_weight)


def seq_bits():
    bits, bit = [], 1
    while bit < lax.axis_size("seq"):
        bits.append(bit)
        bit *= 2
    return bits


ROWS = 128
LEAST = 16


class Reducer:
    def __init__(self, out, gate, conv, din, dout, held, core, sx, rx, near, res, blank, load_sem, keep_sem, send_sem, recv_sem, all_sem, parts):
        self.out, self.gate, self.conv, self.din, self.dout = out, gate, conv, din, dout
        self.held, self.core, self.sx, self.rx, self.near, self.res = held, core, sx, rx, near, res
        self.load_sem, self.keep_sem, self.send_sem, self.recv_sem, self.parts = load_sem, keep_sem, send_sem, recv_sem, parts
        self.blank, self.all_sem = blank, all_sem
        bits = seq_bits()
        seq = lax.axis_index("seq")
        self.steps = len(bits)
        self.halved = halved_bits()
        self.partners = [across_bit("wt", 1), across_bit("wt", 2)] + [across_bit("seq", bit) for bit in bits]
        self.second = [(seq // bit) % 2 for bit in bits]
        self.bases, self.sizes = [0], [ROWS]
        for bit in bits[: self.halved]:
            size = self.sizes[-1] // 2
            self.bases.append(self.bases[-1] + ((seq // bit) % 2) * size)
            self.sizes.append(size)
        self.stages = 2 + self.steps + self.halved
        self.out_count = PARTS * (OUT_PART // ROWS)
        self.gate_count = DI // ROWS
        self.columns = CDIM + HEADS
        self.count = self.out_count + self.gate_count + -(-self.columns // ROWS)
        self.total = self.count + SLACK * self.stages + 1

    def rows_at(self, j):
        return pl.ds(pl.multiple_of(self.bases[j], LEAST), self.sizes[j])

    def kinds(self, c, act):
        first_gate, first_conv = self.out_count, self.out_count + self.gate_count

        @pl.when(c < first_gate)
        def _():
            first = pl.multiple_of((c // PARTS) * ROWS, 16)
            columns = pl.ds(pl.multiple_of((c % PARTS) * PART, LANES), PART)
            act([self.out.at[pl.ds(b * OUT_PART + first, ROWS), columns] for b in range(PARTS)], lambda: self.dout.at[pl.ds(first, ROWS), columns])

        @pl.when(jnp.logical_and(c >= first_gate, c < first_conv))
        def _():
            first = pl.multiple_of((c - first_gate) * ROWS, 16)
            act([self.gate.at[pl.ds(first, ROWS), :]], lambda: self.din.at[pl.ds(first, ROWS), :])

        @pl.when(c >= first_conv)
        def _():
            first = pl.multiple_of(jnp.minimum((c - first_conv) * ROWS, self.columns - ROWS), 16)
            act([self.conv.at[pl.ds(first, ROWS), :]], lambda: self.din.at[pl.ds(DI + first, ROWS), :])

    def load(self, c):
        few = lax.rem(c, FEW)

        def act(sources, target):
            width = DM // len(sources)
            for b, source in enumerate(sources):
                pltpu.make_async_copy(source, self.held.at[few, :, b * width : (b + 1) * width], self.load_sem.at[few]).start()

        self.kinds(c, act)

    def exchange(self, s, slot, few, group=None):
        if s == 0:
            source, target = self.held.at[few, :, 2 * PART :], self.core.at[few]
        elif s == 1:
            source, target = self.sx.at[few], self.rx.at[few]
        elif s < 2 + self.steps:
            source, target = self.parts[3 * (s - 2)].at[few], self.parts[3 * (s - 2) + 1].at[few]
        else:
            j = self.stages - 1 - s
            source = target = self.res.at[slot, self.rows_at(j + 1), :]
        partner = self.partners[s] if s < 2 + self.steps else self.partners[2 + self.stages - 1 - s]
        send, recv = self.send_sem.at[s, few], self.recv_sem.at[s, few]
        if group is not None:
            send, recv = self.all_sem.at[0, group], self.all_sem.at[1, group]
        return pltpu.make_async_remote_copy(src_ref=source, dst_ref=target, send_sem=send, recv_sem=recv, device_id=partner, device_id_type=MESH)

    def grouped(self, t):
        return jnp.logical_and(t >= SLACK * (self.stages - 1), t < self.count)

    def all_done(self, t):
        group = lax.rem(t, FEW)
        for i in range(2):
            pltpu.make_async_copy(self.blank, self.blank, self.all_sem.at[i, group]).wait()

    def loaded(self, few):
        pltpu.make_async_copy(self.gate.at[0:ROWS, :], self.held.at[few], self.load_sem.at[few]).wait()

    def kept(self, slot):
        return pltpu.make_async_copy(self.res.at[slot], self.din.at[0:ROWS, :], self.keep_sem.at[slot])

    def combine(self, s, slot, few):
        if s == 0:
            self.near[few] = self.held[few, :, :PART].astype(F32) + self.core[few, :, :PART].astype(F32)
            self.sx[few] = (self.held[few, :, PART : 2 * PART].astype(F32) + self.core[few, :, PART:].astype(F32)).astype(LOW)
        elif s == 1:
            self.lay(self.near[few] + self.rx[few].astype(F32), 0, slot, few)
        elif s < 2 + self.steps:
            j = s - 2
            mine = self.parts[3 * j + 2][few] if j < self.halved else self.parts[3 * j][few].astype(F32)
            self.lay(mine + self.parts[3 * j + 1][few].astype(F32), j + 1, slot, few)

    def lay(self, value, j, slot, few):
        if j == self.steps:
            self.res[slot, self.rows_at(self.halved), :] = value.astype(LOW)
        elif j < self.halved:
            size = self.sizes[j + 1]
            low, high = value[:size], value[size:]
            second = self.second[j] == 1
            self.parts[3 * j][few] = jnp.where(second, low, high).astype(LOW)
            self.parts[3 * j + 2][few] = jnp.where(second, high, low)
        else:
            self.parts[3 * j][few] = value.astype(LOW)

    def write(self, c, slot):
        self.kinds(c, lambda sources, target: pltpu.make_async_copy(self.res.at[slot], target(), self.keep_sem.at[slot]).start())

    def step(self, t):
        steady = jnp.logical_and(t > SLACK * self.stages, t < self.count)

        @pl.when(steady)
        def _():
            slots = [(lax.rem(t - SLACK * s, SLOTS), lax.rem(t - SLACK * s, FEW)) for s in range(self.stages + 1)]
            self.kept(lax.rem(t - SLACK * self.stages - 1, SLOTS)).wait()
            self.all_done(t - SLACK)
            self.loaded(slots[0][1])
            for s in range(self.stages, 0, -1):
                self.combine(s - 1, *slots[s])
            group = lax.rem(t, FEW)
            for s in range(1, self.stages):
                self.exchange(s, *slots[s], group).start()
            self.exchange(0, *slots[0], group).start()
            self.write(t - SLACK * self.stages, slots[self.stages][0])

        @pl.when(jnp.logical_not(steady))
        def _():
            c = t - SLACK * self.stages - 1

            @pl.when(jnp.logical_and(c >= 0, c < self.count))
            def _():
                self.kept(lax.rem(c, SLOTS)).wait()

            were, are = self.grouped(t - SLACK), self.grouped(t)

            @pl.when(were)
            def _():
                self.all_done(t - SLACK)

            for s in range(self.stages, -1, -1):
                c = t - SLACK * s

                @pl.when(jnp.logical_and(c >= 0, c < self.count))
                def _(c=c, s=s):
                    slot, few = lax.rem(c, SLOTS), lax.rem(c, FEW)
                    if s > 0:

                        @pl.when(jnp.logical_not(were))
                        def _():
                            self.exchange(s - 1, slot, few).wait()

                        self.combine(s - 1, slot, few)
                    else:
                        self.loaded(few)
                    if s < self.stages:

                        @pl.when(are)
                        def _():
                            self.exchange(s, slot, few, lax.rem(t, FEW)).start()

                        @pl.when(jnp.logical_not(are))
                        def _():
                            self.exchange(s, slot, few).start()

                    else:
                        self.write(c, slot)

        @pl.when(t + 1 < self.count)
        def _():
            self.load(t + 1)


def halved_bits():
    count, rows = 0, ROWS
    while count < len(seq_bits()) and rows > LEAST:
        count, rows = count + 1, rows // 2
    return count


BLOCKS = 4
PER = 2
HALF = BLOCKS // PER
TURNS = HALF + 1
FILL_STEPS, NEAR_STEPS, BACK_STEPS, EDGE_STEPS, GATE_STEPS = STEPS, STEPS * HALF, STEPS * TURNS + 1, 1, STEPS
NEAR_AT = FILL_STEPS
BACK_AT = NEAR_AT + NEAR_STEPS
EDGE_AT = BACK_AT + BACK_STEPS
PULL_AT = EDGE_AT + EDGE_STEPS
DOT_STEPS = STEPS + 1
PULL_STEPS = 2 * GATE_STEPS + DOT_STEPS
LAST_AT = PULL_AT + PULL_STEPS
ALL_STEPS = LAST_AT + 1
PACE = ((1, FILL_STEPS - 1, 9), (NEAR_AT, NEAR_STEPS, 22), (BACK_AT, BACK_STEPS, 32), (EDGE_AT, EDGE_STEPS, 1), (PULL_AT, PULL_STEPS, 17))
DONE = sum(turns for _, _, turns in PACE)


def clip(v, low, high):
    return jnp.minimum(jnp.maximum(v, low), high)


def paced(g):
    done = 0
    for first, steps, turns in PACE:
        done = done + (turns * clip(g - first, 0, steps)) // steps
    return done


def head_block(g):
    near = clip(g - NEAR_AT, 0, NEAR_STEPS) // HALF
    over = near // STEPS
    return near * (1 - over) + over * clip((g - BACK_AT) // TURNS, 0, STEPS - 1)


def gate_block(g):
    over = clip(g - FILL_STEPS + 1, 0, 1)
    return jnp.minimum(g, FILL_STEPS - 1) * (1 - over) + over * clip(g - PULL_AT - GATE_STEPS, 0, GATE_STEPS - 1)


def near_block_at(g):
    return jnp.minimum(clip(g - NEAR_AT, 0, NEAR_STEPS) // HALF, STEPS - 1)


def rear_kernel(pc_ref, x_ref, dy_ref, bc_ref, rb_ref, rt_ref, er_ref, ew_ref, d2_ref, ed_ref, dt_ref, e2_ref, et_ref, states_ref, in_ref, taps_ref, skip_ref, heads_ref, met_ref, normed_ref, tok_ref, up_ref, gain_ref, sums_ref, low0_ref, low1_ref, low2_ref, low3_ref, low_ref, dgate_ref, wgate_ref, wconv_ref, din_ref, sum_in_ref, sum_out_ref, small_ref, dtok_ref, mixed_ref, gconv_ref, gout_ref, ggate_ref, pad_ref, dact_ref, dheld_ref, direct_ref, dconv_ref, dscores_ref, dbc_ref, ddt_ref, q_ref, v_ref, ends_ref, crossed_ref, stage_ref, second_ref, rim_ref, rim_got_ref, one_sem, fill_sem, rim_sem, total_ref, factor_ref, reach_ref, held_ref, psend_ref, precv_ref, ps_sem, pr_sem, vsend_ref, vrecv_ref, vs_sem, vr_sem, r_held, r_core, r_sx, r_rx, r_near, r_res, r_blank, load_sem, keep_sem, send_sem, recv_sem, all_sem, *parts):
    g = pl.program_id(0)
    length = x_ref.shape[0]
    seq, peers = lax.axis_index("seq"), lax.axis_size("seq")
    following, previous = {"seq": lax.rem(seq + 1, peers)}, {"seq": lax.rem(seq + peers - 1, peers)}
    reducer = Reducer(gout_ref, ggate_ref, gconv_ref, sum_in_ref, sum_out_ref, r_held, r_core, r_sx, r_rx, r_near, r_res, r_blank, load_sem, keep_sem, send_sem, recv_sem, all_sem, parts)
    passing = Passing(True, total_ref, factor_ref, reach_ref, held_ref, psend_ref, precv_ref, met_ref, ps_sem, pr_sem)
    rounds = len(passing.bits)
    block = head_block(g)

    def columns_of(j):
        return pl.ds(pl.multiple_of(j * WIDE, WIDE), WIDE)

    def edge(j):
        return pltpu.make_async_remote_copy(src_ref=rim_ref.at[:, columns_of(j)], dst_ref=rim_got_ref.at[:, columns_of(j)], send_sem=rim_sem.at[0, j], recv_sem=rim_sem.at[1, j], device_id=previous, device_id_type=MESH)

    @pl.when(g == 0)
    def _():
        greet(reducer.partners + [following, previous])
        first = pltpu.make_async_copy(din_ref, total_ref, one_sem.at[2])
        first.start()
        for ref in (dscores_ref, dbc_ref, ddt_ref, q_ref, v_ref, ends_ref, crossed_ref, held_ref):
            ref[...] = jnp.zeros_like(ref)
        reach_ref[...] = jnp.ones_like(reach_ref)
        factor_ref[0:1, :] = met_ref[7:8, :]
        first.wait()
        for j in range(STEPS):
            passing.start(0, j)

    lows = (low0_ref, low1_ref, low2_ref, low3_ref)

    def filled(i):
        copies = []
        for b in range(PARTS):
            rows = pl.ds(pl.multiple_of(b * OUT_PART + i * ROWS, ROWS), ROWS)
            copies.append(pltpu.make_async_copy(stage_ref.at[b * ROWS : (b + 1) * ROWS, :], gout_ref.at[rows, :], fill_sem.at[b]))
        copies.append(pltpu.make_async_copy(second_ref, ggate_ref.at[columns_of(i), :], fill_sem.at[PARTS]))
        return copies

    @pl.when(jnp.logical_and(g >= 1, g <= FILL_STEPS))
    def _():
        for copy in filled(g - 1):
            copy.wait()

    @pl.when(g < FILL_STEPS)
    def _():
        for b in range(PARTS):
            stage_ref[b * ROWS : (b + 1) * ROWS, :] = tn(lows[b][...], up_ref[...]).astype(LOW)
        second_ref[...] = tn(dgate_ref[...], normed_ref[EDGE:, :]).astype(LOW)
        for copy in filled(g):
            copy.start()

    @pl.when(g == 1)
    def _():
        reducer.load(jnp.int32(0))

    for k in range(rounds - 1):
        since = g - (1 + 2 * k)

        @pl.when(jnp.logical_and(since >= 0, since < STEPS))
        def _(k=k, since=since):
            passing.finish(k, since)

    def near_block(c):
        at = pl.ds(pl.multiple_of(c * BLOCK, BLOCK), BLOCK)
        ids, jds = rows_cols((BLOCK, BLOCK))
        suffix = (ids >= jds).astype(LOW)
        left = lax.broadcasted_iota(jnp.int32, (BLOCK, LANES), 1) < HDIM
        scores = jnp.where(ids <= jds, nt(bc_ref[at, :NSTATE], bc_ref[at, NSTATE:]), 0.0)
        dy = dy_ref[at, :]
        sized = x_ref[at, :].astype(F32) * nn(d2_ref[at, :], e2_ref[...])
        total = jnp.zeros((BLOCK, BLOCK), F32)
        rows = []
        for pair in range(GROUP // 2):
            lanes = slice(pair * LANES, (pair + 1) * LANES)
            piece, dpiece = sized[:, lanes], dy[:, lanes]
            both = jnp.concatenate([jnp.where(left, piece, 0.0), jnp.where(left, 0.0, piece)], axis=0).astype(LOW)
            meets = nn(both, dpiece.T)
            mixed, kept = [], []
            for half in range(2):
                head = 2 * pair + half
                spread = rt_ref[head : head + 1, at] - rb_ref[at, head : head + 1]
                decay = jnp.exp(jnp.minimum(spread, 0.0))
                meet = meets[half * BLOCK : (half + 1) * BLOCK] * decay
                total = total + meet
                mixed.append((scores * decay).astype(LOW))
                kept.append((meet * scores).astype(LOW))
            later = nn(jnp.concatenate(kept, axis=0), suffix)
            for half in range(2):
                one = later[half * BLOCK : (half + 1) * BLOCK]
                rows.append(jnp.sum(jnp.where(ids < jds, one, 0.0), axis=0, keepdims=True))
            none = jnp.zeros_like(dpiece)
            both = jnp.concatenate([jnp.where(left, dpiece, none), jnp.where(left, none, dpiece)], axis=0)
            direct_ref[block, at, lanes] = nn(jnp.concatenate(mixed, axis=1), both)
        dscores_ref[c] += total
        crossed_ref[pl.ds(pl.multiple_of(block * GROUP, GROUP), GROUP), at] = jnp.concatenate(rows, axis=0)

    @pl.when(jnp.logical_and(g >= NEAR_AT, g < BACK_AT))
    def _():
        @pl.loop(0, PER)
        def _(i):
            near_block(((g - NEAR_AT) % HALF) * PER + i)

    turn = g - BACK_AT
    part = turn % TURNS
    going = jnp.logical_and(turn >= 0, turn < STEPS * TURNS)

    @pl.when(jnp.logical_and(going, part == 0))
    def _():
        passing.finish(rounds - 1, block)
        dheld_ref[...] = held_ref[:, passing.columns(block)]

    def back_block(c):
        at = pl.ds(pl.multiple_of(c * BLOCK, BLOCK), BLOCK)
        input_mat, output_mat = bc_ref[at, :NSTATE], bc_ref[at, NSTATE:]
        e2, et = e2_ref[...], et_ref[...]
        grow, leave, size = nn(er_ref[at, :], e2), nn(ew_ref[at, :], e2), nn(d2_ref[at, :], e2)
        prior = pl.ds(pl.multiple_of(jnp.maximum(c * BLOCK - 16, 0), 16), 16)
        reach = nn(ed_ref[prior, :], e2)[15:16, :]
        reach = jnp.where(c == 0, 1.0, reach)
        state = states_ref[c].astype(F32) + reach * in_ref[...].astype(F32)
        state_low = state.astype(LOW)
        x = x_ref[at, :].astype(F32)
        dy = dy_ref[at, :].astype(F32)
        dheld = dheld_ref[...]
        dheld_low = dheld.astype(LOW)
        grown = (dy * grow).astype(LOW)
        pulled = nn(input_mat, dheld_low) * leave
        dbc_ref[at, :NSTATE] += nt((x * size * leave).astype(LOW), dheld_low)
        dbc_ref[at, NSTATE:] += nt(grown, state_low)
        carried = nn(output_mat, state_low) * grow
        q_ref[at, :] += nn((dy * carried).astype(LOW), et)
        v_ref[at, :] += nn((x * pulled).astype(LOW), et)
        last = grow[BLOCK - 1 : BLOCK, :]
        ends = jnp.sum(state * dheld, axis=0, keepdims=True) * last
        ends_ref[c] += nn(jnp.broadcast_to(ends, (16, WIDE)).astype(LOW), et)[:8]
        dheld_ref[...] = dheld * last + tn(output_mat, grown)
        direct = direct_ref[block, at, :] + pulled
        ddt_ref[at, :] += nn((x * direct).astype(LOW), et)
        dact_ref[at, :] = size * direct + skip_ref[0:1, :] * dy

    @pl.when(jnp.logical_and(going, part < HALF))
    def _():
        @pl.loop(0, PER)
        def _(i):
            back_block(BLOCKS - 1 - (part * PER + i))

    @pl.when(turn == STEPS * TURNS)
    def _():
        ids, jds = rows_cols((BLOCK, BLOCK))
        upper = (ids <= jds).astype(F32)
        under = (ids > jds).astype(F32)
        rate = jnp.exp(heads_ref[1:2, :])
        dstep_bias = jnp.zeros((1, LANES), F32)
        ddecay_log = jnp.zeros((1, LANES), F32)
        for c in range(BLOCKS):
            at = slice(c * BLOCK, (c + 1) * BLOCK)
            dscores = jnp.where(ids <= jds, dscores_ref[c], 0.0).astype(LOW)
            dact_ref[at, :NSTATE] = dbc_ref[at, :NSTATE] + nn(dscores, bc_ref[at, NSTATE:])
            dact_ref[at, NSTATE : 2 * NSTATE] = dbc_ref[at, NSTATE:] + tn(dscores, bc_ref[at, :NSTATE])
            dt = dt_ref[at, :]
            ddecay = crossed_ref[:, at].T + exact(upper, q_ref[at, :]) + exact(under, v_ref[at, :] * dt) + ends_ref[c][0:1, :]
            draw = ddt_ref[at, :] - ddecay * rate
            ddecay_log = ddecay_log - jnp.sum(ddecay * dt, axis=0, keepdims=True) * rate
            raw = pc_ref[EDGE + c * BLOCK : EDGE + (c + 1) * BLOCK, 2 * NSTATE : 2 * NSTATE + LANES].astype(F32)
            used = lax.broadcasted_iota(jnp.int32, raw.shape, 1) < HEADS
            draw = draw * jax.nn.sigmoid(jnp.where(used, raw + heads_ref[0:1, :], 0.0))
            dstep_bias = dstep_bias + jnp.sum(draw, axis=0, keepdims=True)
            dact_ref[at, 2 * NSTATE : 2 * NSTATE + LANES] = draw
            dact_ref[at, 2 * NSTATE + LANES :] = jnp.zeros((BLOCK, LANES), F32)
        ends_ref[0] = jnp.broadcast_to(dstep_bias, (8, LANES))
        ends_ref[1] = jnp.broadcast_to(ddecay_log, (8, LANES))

    @pl.when(jnp.logical_or(jnp.logical_and(going, part == HALF), turn == STEPS * TURNS))
    def _():
        here = turn // TURNS
        at = pl.ds(pl.multiple_of(here * WIDE, WIDE), WIDE)
        taps = taps_ref[:, at]
        pad_ref[...] = pc_ref[...].astype(F32)
        summed = taps[CONV : CONV + 1]
        for k in range(CONV):
            first = EDGE - CONV + 1 + k
            summed = summed + taps[k : k + 1] * pad_ref[first : first + length, :]
        shape = jax.nn.sigmoid(summed)
        dsum = dact_ref[0:length, :] * (shape * (1.0 + summed * (1.0 - shape)))
        dtap = [jnp.sum(dsum * pad_ref[EDGE - CONV + 1 + k : EDGE - CONV + 1 + k + length, :], axis=0, keepdims=True) for k in range(CONV)]
        dtap.append(jnp.sum(dsum, axis=0, keepdims=True))
        vsend_ref[0, :, at] = jnp.concatenate(dtap + [jnp.zeros((8 - len(dtap), WIDE), F32)], axis=0)
        rim_ref[:, at] = dsum[:16].astype(LOW)
        keep = dact_ref[0:length, :]
        dact_ref[0:length, :] = dsum
        dact_ref[length:, :] = jnp.zeros_like(dact_ref[length:, :])
        result = taps[CONV - 1 : CONV] * dsum
        for k in range(CONV - 1):
            by = CONV - 1 - k
            result = result + taps[k : k + 1] * dact_ref[by : by + length, :]
        lane = lax.broadcasted_iota(jnp.int32, (1, WIDE), 1)
        raw_part = jnp.logical_and(turn == STEPS * TURNS, lane >= 2 * NSTATE)
        dconv_ref[:, at] = jnp.where(raw_part, keep, result).astype(LOW)

    def stored(k):
        return pltpu.make_async_copy(stage_ref, gconv_ref.at[columns_of(k), :], one_sem.at[2])

    def settle(j):
        edge(j).wait()

        @pl.when(j >= 1)
        def _():
            stored(j - 1).wait()

        at = columns_of(j)
        bottom = slice(length - 16, length)
        got, taps = rim_got_ref[:, at].astype(F32), taps_ref[:, at]
        ids, jds = rows_cols(got.shape)
        extra = jnp.zeros_like(got)
        for i in range(CONV - 1):
            row = sum(taps[k : k + 1] * got[i - k : i - k + 1] for k in range(i + 1))
            extra = jnp.where(ids == 16 - CONV + 1 + i, row, extra)
        takes = jnp.logical_and(jds < CDIM - j * WIDE, seq < peers - 1)
        dconv_ref[bottom, at] = (dconv_ref[bottom, at].astype(F32) + jnp.where(takes, extra, 0.0)).astype(LOW)
        stage_ref[...] = tn(dconv_ref[:, at], normed_ref[EDGE:, :]).astype(LOW)
        stored(j).start()

    convolves = jnp.logical_or(jnp.logical_and(going, part == HALF), turn == STEPS * TURNS)

    @pl.when(convolves)
    def _():
        edge(turn // TURNS).start()

    @pl.when(jnp.logical_or(jnp.logical_and(convolves, turn >= TURNS), g == EDGE_AT))
    def _():
        settle(jnp.where(g == EDGE_AT, STEPS, turn // TURNS - 1))

    @pl.when(g == PULL_AT)
    def _():
        stored(STEPS).wait()

    pull = g - PULL_AT

    thirds = [slice(i * WIDE, (i + 1) * WIDE) for i in range(DM // WIDE)]
    mixed_out = pltpu.make_async_copy(stage_ref, mixed_ref, one_sem.at[2])

    @pl.when(pull == 0)
    def _():
        for i, at in enumerate(thirds):
            direct_ref[i] = tok_ref[:, at].astype(F32)

    @pl.when(jnp.logical_and(pull >= 0, pull < GATE_STEPS))
    def _():
        for i, at in enumerate(thirds):
            direct_ref[i] += nn(low_ref[...], wgate_ref[:, at])

    @pl.when(pull == GATE_STEPS)
    def _():
        for i, at in enumerate(thirds):
            stage_ref[:, at] = direct_ref[i].astype(LOW)
        mixed_out.start()
        direct_ref[0:PARTS] = jnp.zeros_like(direct_ref[0:PARTS])

    def add_pull(left, weight):
        for b in range(PARTS):
            direct_ref[b, :, :PART] += nn(left, weight[:, b * PART : (b + 1) * PART])

    @pl.when(jnp.logical_and(pull >= GATE_STEPS, pull < 2 * GATE_STEPS))
    def _():
        add_pull(dgate_ref[...], wgate_ref[...])

    @pl.when(jnp.logical_and(pull >= 2 * GATE_STEPS, pull < PULL_STEPS))
    def _():
        k = pull - 2 * GATE_STEPS
        columns = pl.ds(pl.multiple_of(k * WIDE, WIDE), WIDE)
        ids = lax.broadcasted_iota(jnp.int32, (WIDE, DM), 0)
        weight = wconv_ref[...]
        weight = jnp.where(ids < CDIM + HEADS - k * WIDE, weight, jnp.zeros_like(weight))
        add_pull(dconv_ref[:, columns], weight)

    def normed_out(b):
        return pltpu.make_async_copy(direct_ref.at[relative(b), :, 0:PART], dtok_ref.at[:, b * PART : (b + 1) * PART], one_sem.at[3 + b])

    meets = len(reducer.partners)

    def swap(k):
        return pltpu.make_async_remote_copy(src_ref=vsend_ref.at[k], dst_ref=vrecv_ref.at[k], send_sem=vs_sem.at[k], recv_sem=vr_sem.at[k], device_id=reducer.partners[k], device_id_type=MESH)

    @pl.when(g == LAST_AT)
    def _():
        blocks = [slice(b * PART, (b + 1) * PART) for b in range(PARTS)]
        square = jnp.zeros((length, 1), F32)
        cross = jnp.zeros((length, 1), F32)
        for b, at in enumerate(blocks):
            u = tok_ref[:, at].astype(F32)
            square = square + jnp.sum(u * u, axis=1, keepdims=True)
            cross = cross + jnp.sum(direct_ref[relative(b), :, :PART] * gain_ref[0:1, at] * u, axis=1, keepdims=True)
        rate = lax.rsqrt(square * (1.0 / DM) + EPS)
        pulled = rate * rate * rate * (cross * (1.0 / DM))
        for b, at in enumerate(blocks):
            u = tok_ref[:, at].astype(F32)
            there = relative(b)
            d_normed = direct_ref[there, :, :PART]
            vsend_ref[0, 5:6, at] = jnp.sum(d_normed * (u * rate), axis=0, keepdims=True)
            direct_ref[there, :, :PART] = up_ref[:, at].astype(F32) + rate * (d_normed * gain_ref[0:1, at]) - u * pulled
            normed_out(b).start()
        vsend_ref[0, 6:7, :DI] = sums_ref[0:1, :]
        vsend_ref[0, 7:8, :DI] = sums_ref[1:2, :]
        vsend_ref[0, 6:7, DI : DI + LANES] = ends_ref[0][0:1]
        vsend_ref[0, 7:8, DI : DI + LANES] = ends_ref[1][0:1]

        swap(0).start()

    @pl.loop(paced(g), paced(g + 1) + (g // LAST_AT) * (reducer.total - DONE))
    def _(t):
        reducer.step(t)
        for k in range(meets):

            @pl.when(t == DONE + 2 * (k + 1))
            def _(k=k):
                swap(k).wait()
                value = vsend_ref[k] + vrecv_ref[k]
                if k + 1 < meets:
                    vsend_ref[k + 1] = value
                    swap(k + 1).start()
                else:
                    small_ref[...] = value

    @pl.when(g == LAST_AT)
    def _():
        for b in range(PARTS):
            normed_out(b).wait()
        mixed_out.wait()


def rear(proj, x, dy, bc, rb, rt, er, ew, d2, ed, dt, e2, et, states, incoming, taps, skip, heads, met, normed, tokens, upstream, gain, sums, low, dgate, wide_all, conv_all, din):
    length = x.shape[0]
    bits, halved = len(seq_bits()), halved_bits()
    hbm = pl.BlockSpec(memory_space=pl.ANY)
    back_block = lambda g: clip((g - BACK_AT) // TURNS, 0, STEPS)
    part_block = lambda g: clip((g - BACK_AT) // TURNS, 0, STEPS - 1)

    def whole(array):
        return pl.BlockSpec(array.shape, lambda g: (0,) * array.ndim, pipeline_mode=pl.Buffered(1))

    shares = []
    for j in range(bits):
        shape = (FEW, max(ROWS >> (j + 1), LEAST), PART)
        shares += [pltpu.VMEM(shape, LOW), pltpu.VMEM(shape, LOW), pltpu.VMEM(shape, F32)]
    dma = pltpu.SemaphoreType.DMA
    stages, meets = 2 + bits + halved, 2 + bits
    moved = 3 * ROWS + 2 * sum(ROWS >> (j + 1) for j in range(halved)) + LEAST * (bits - halved)
    return pl.pallas_call(
        rear_kernel,
        grid=(ALL_STEPS,),
        in_specs=[
            pl.BlockSpec((length + EDGE, WIDE), lambda g: (0, back_block(g))),
            pl.BlockSpec((length, WIDE), lambda g: (0, head_block(g))),
            pl.BlockSpec((length, WIDE), lambda g: (0, head_block(g))),
            whole(bc),
            pl.BlockSpec((length, LANES), lambda g: (0, near_block_at(g))),
            pl.BlockSpec((GROUP, length), lambda g: (near_block_at(g), 0)),
            whole(er),
            whole(ew),
            whole(d2),
            whole(ed),
            whole(dt),
            pl.BlockSpec((2 * LANES, WIDE), lambda g: (0, head_block(g))),
            pl.BlockSpec((WIDE, LANES), lambda g: (part_block(g), 0)),
            pl.BlockSpec((length // BLOCK, NSTATE, WIDE), lambda g: (0, 0, part_block(g))),
            pl.BlockSpec((NSTATE, WIDE), lambda g: (0, part_block(g))),
            whole(taps),
            pl.BlockSpec((8, WIDE), lambda g: (0, part_block(g))),
            whole(heads),
            whole(met),
            whole(normed),
            whole(tokens),
            whole(upstream),
            whole(gain),
            whole(sums),
        ]
        + [pl.BlockSpec((length, ROWS), lambda g, b=b: (0, b * (OUT_PART // ROWS) + jnp.minimum(g, FILL_STEPS - 1))) for b in range(PARTS)]
        + [
            pl.BlockSpec((length, WIDE), lambda g: (0, clip(g - PULL_AT, 0, GATE_STEPS - 1))),
            pl.BlockSpec((length, WIDE), lambda g: (0, gate_block(g))),
            pl.BlockSpec((WIDE, DM), lambda g: ((clip(g - PULL_AT, 0, 2 * GATE_STEPS - 1) + GATE_STEPS) % (2 * GATE_STEPS), 0)),
            pl.BlockSpec((WIDE, DM), lambda g: (clip(g - PULL_AT - 2 * GATE_STEPS, 0, DOT_STEPS - 1), 0)),
            hbm,
        ],
        out_specs=[hbm, hbm, pl.BlockSpec((8, LONG), lambda g: (0, 0)), hbm, hbm, hbm, hbm, hbm],
        out_shape=[
            jax.ShapeDtypeStruct((DI + CDIM + HEADS, PART), LOW),
            jax.ShapeDtypeStruct((OUT_PART, DM), LOW),
            jax.ShapeDtypeStruct((8, LONG), F32),
            jax.ShapeDtypeStruct((length, DM), F32),
            jax.ShapeDtypeStruct((length, DM), LOW),
            jax.ShapeDtypeStruct((LONG, DM), LOW),
            jax.ShapeDtypeStruct((DI, DM), LOW),
            jax.ShapeDtypeStruct((DI, DM), LOW),
        ],
        scratch_shapes=[
            pltpu.VMEM((length + EDGE, WIDE), F32),
            pltpu.VMEM((length + EDGE, WIDE), F32),
            pltpu.VMEM((NSTATE, WIDE), F32),
            pltpu.VMEM((STEPS, length, WIDE), F32),
            pltpu.VMEM((length, LONG), LOW),
            pltpu.VMEM((length // BLOCK, BLOCK, BLOCK), F32),
            pltpu.VMEM((length, 2 * NSTATE), F32),
            pltpu.VMEM((length, LANES), F32),
            pltpu.VMEM((length, LANES), F32),
            pltpu.VMEM((length, LANES), F32),
            pltpu.VMEM((length // BLOCK, 8, LANES), F32),
            pltpu.VMEM((LANES, length), F32),
            pltpu.VMEM((WIDE, DM), LOW),
            pltpu.VMEM((WIDE, DM), LOW),
            pltpu.VMEM((16, LONG), LOW),
            pltpu.VMEM((16, LONG), LOW),
            dma((3 + PARTS,)),
            dma((PARTS + 1,)),
            dma((2, STEPS + 1)),
            pltpu.VMEM((NSTATE, DI), F32),
            pltpu.VMEM((8, DI), F32),
            pltpu.VMEM((8, DI), F32),
            pltpu.VMEM((NSTATE, DI), F32),
            pltpu.VMEM((NSTATE, DI), LOW),
            pltpu.VMEM((bits, NSTATE, DI), LOW),
            dma((bits, STEPS)),
            dma((bits, STEPS)),
            pltpu.VMEM((meets, 8, LONG), F32),
            pltpu.VMEM((meets, 8, LONG), F32),
            dma((meets,)),
            dma((meets,)),
            pltpu.VMEM((FEW, ROWS, DM), LOW),
            pltpu.VMEM((FEW, ROWS, 2 * PART), LOW),
            pltpu.VMEM((FEW, ROWS, PART), LOW),
            pltpu.VMEM((FEW, ROWS, PART), LOW),
            pltpu.VMEM((FEW, ROWS, PART), F32),
            pltpu.VMEM((SLOTS, ROWS, PART), LOW),
            pltpu.VMEM((moved, PART), LOW),
            dma((FEW,)),
            dma((SLOTS,)),
            dma((stages, FEW)),
            dma((stages, FEW)),
            dma((2, FEW)),
        ]
        + shares,
        compiler_params=pltpu.CompilerParams(vmem_limit_bytes=62 << 20, collective_id=2, has_side_effects=True),
        cost_estimate=pl.CostEstimate(flops=200 << 30, bytes_accessed=60 << 20, transcendentals=0),
        name="rear",
    )(proj, x, dy, bc, rb, rt, er, ew, d2, ed, dt, e2, et, states, incoming, taps, skip, heads, met, normed, tokens, upstream, gain, sums, low, low, low, low, low, dgate, wide_all, conv_all, din)


def shards(tokens, norm_gain, in_weight, conv_kernel, conv_bias, step_bias, decay_log, skip_gain, out_gain, out_weight, cotangent):
    length = tokens.shape[1]
    own, upstream = tokens[0], cotangent[0]
    turned = in_weight.T
    gain = norm_gain[None]
    skip = jnp.repeat(skip_gain, HDIM)[None]
    gains = jnp.concatenate([out_gain[None], skip, jnp.zeros((6, DI), F32)], axis=0)
    skip = jnp.broadcast_to(skip, (8, DI))
    lanes = np.arange(DI) // HDIM
    e2 = jnp.asarray((np.arange(2 * LANES)[:, None] % LANES == lanes[None]).astype(LOW))
    et = jnp.asarray((lanes[:, None] == np.arange(LANES)[None]).astype(LOW))

    taps, heads, proj, normed, x, bc, dt, rb, rt, er, ew, d2, ed, state, conv_all = enter(own, gain, conv_kernel, conv_bias[None], step_bias[None], decay_log[None], e2, turned)
    incoming, met, y, states, gate, dno, wide_all = gates(normed, upstream, state, x, bc, rb, rt, er, ew, d2, e2, turned, out_weight)
    low, dy, dgate, sums, din = middle(y, bc, incoming, ed, e2, x, gate, dno, gains, length)

    sum_in, sum_out, small, d_tokens, mixed, *_ = rear(proj, x, dy, bc, rb, rt, er, ew, d2, ed, dt, e2, et, states, incoming, taps, skip, heads, met, normed, own, upstream, gain, sums, low, dgate, wide_all, conv_all, din)
    return (
        mixed[None],
        d_tokens[None],
        small[5, :DM],
        sum_in.astype(F32).T,
        small[:CONV, :CDIM],
        small[CONV, :CDIM],
        small[6, DI : DI + HEADS],
        small[7, DI : DI + HEADS],
        jnp.sum(small[7, :DI].reshape(HEADS, HDIM), axis=1),
        small[6, :DI],
        sum_out.astype(F32),
    )


def solution(mesh):
    spread = P("wt", "seq", None)
    return jax.shard_map(
        shards,
        mesh=mesh,
        in_specs=(spread, P(), P("wt", None), P(), P(), P(), P(), P(), P(), P("wt", None), spread),
        out_specs=(spread, spread, P(), P("wt", None), P(), P(), P(), P(), P(), P(), P("wt", None)),
        check_vma=False,
    )
```
